32 devices in a mesh: groups: 2 (over x), tm: 8 (over z, y), band: 2 (over core).
Axes of the slice: x: 2, y: 2, z: 4, core: 2. Of those that a mesh axis runs over, the one named last changes fastest.
Arguments:
- series: float32 [262144], P(('groups', 'tm')), parts along dimension 0, may hold values from -40 to 40
- tail: float32 [512], P('groups'), parts along dimension 0, may hold values from -6 to 6
- band_starts: int32 [4], P('groups'), parts along dimension 0, may hold values from 0 to 3968, as said below
Outputs:
- row_profile: float32 [262144], P(('groups', 'tm')), parts along dimension 0
- col_profile: float32 [262144], P(('groups', 'tm')), parts along dimension 0
The draws below stay inside these ranges and needn't reach their ends.
There are 2 independent parts, one for each index of `groups`. The reference program is written for one: setup_inputs(seed, part) draws one part's arguments, and reference() takes and returns one part's arrays. A program takes and returns all parts, laid end to end along the dimension named above; each array names one. Nothing has to cross between parts.
Inputs may be any that keep to these rules, and one draw needn't show every extreme that they name: `band_starts`: one entry equals 3968.
All inputs are finite; a program needn't handle non-finite values.
Results may differ from the reference program's by a relative error of at most 0.00061.
Values sent between devices are 32-bit elements; how exact they have to be, the bound alone decides.
A program may use at most 64 MiB of HBM per device.

```python
import jax
import jax.numpy as jnp
from jax import lax

M = 256
TILE = 128
OFF_DEV = 128
BAND_SPAN = 4096
SAMPLES = 131072
BAND_BASE = 65536
N_BAND = 2


def draw_series(key, part):
    key_offset, key_scale, key_noise = jax.random.split(jax.random.fold_in(key, 11), 3)
    blocks = SAMPLES // 128
    offset = jax.random.uniform(key_offset, (blocks,), jnp.float32, -2.0, 2.0)
    scales = jnp.exp(jax.random.uniform(key_scale, (blocks,), jnp.float32, -0.69, 0.69))
    noise = jnp.clip(jax.random.normal(key_noise, (blocks, 128), jnp.float32), -6.0, 6.0)
    return (offset[:, None] + scales[:, None] * noise).reshape(SAMPLES)


def draw_band_starts(key, part):
    key_values, key_pick = jax.random.split(jax.random.fold_in(key, 23))
    highest = BAND_SPAN - OFF_DEV
    values = jax.random.randint(key_values, (N_BAND,), 0, highest + 1)
    chosen = jax.random.randint(key_pick, (), 0, N_BAND)
    return jnp.where(jnp.arange(N_BAND) == chosen, highest, values).astype(jnp.int32)


def centred(stream_key, dims, scale, reach, kind=jnp.bfloat16):
    return jnp.clip(scale * jax.random.normal(stream_key, dims, jnp.float32), -reach, reach).astype(kind)


def setup_inputs(seed: int = 0, part: int = 0) -> dict:
    key_list = jax.random.split(jax.random.key(seed), 4)
    own_keys = jax.random.split(jax.random.fold_in(key_list[3], part), 4)
    return {
        "series": draw_series(jax.random.fold_in(jax.random.fold_in(key_list[3], part), 71), part),
        "tail": centred(own_keys[1], (M,), 1.0, 6.0, jnp.float32),
        "band_starts": draw_band_starts(jax.random.fold_in(jax.random.fold_in(key_list[3], part), 71), part),
    }


EPS = 1e-06
tile_batch = 16

def hankel(samples, tile_count):
    length = tile_count * TILE + M
    shifted = jnp.stack([lax.slice_in_dim(samples, offset, offset + length) for offset in range(TILE)])
    blocks = shifted.reshape(TILE, length // TILE, TILE)
    joined = jnp.concatenate([blocks[:, stride:stride + tile_count] for stride in range(M // TILE)], axis=2)
    return jnp.swapaxes(joined, 0, 1)

def moments(matrix):
    center = lax.optimization_barrier(jnp.mean(matrix, axis=-1))
    spread = matrix - center[..., None]
    factor = lax.rsqrt(lax.optimization_barrier(jnp.sum(spread * spread, axis=-1)) + M * EPS)
    return (center, factor)

def normed(matrix, center, factor):
    return ((matrix - center[..., None]) * factor[..., None]).astype(jnp.bfloat16)

def score_group(row_z, col_z, room_left):
    tile_count = row_z.shape[0]
    row_wide = row_z.astype(jnp.float32)
    near_scores = jnp.einsum('tim,tjm->tij', row_wide, col_z[:-1].astype(jnp.float32), precision=lax.Precision.HIGHEST)
    far_scores = jnp.einsum('tim,tjm->tij', row_wide, col_z[1:, :OFF_DEV].astype(jnp.float32), precision=lax.Precision.HIGHEST)
    row_near = lax.broadcasted_iota(jnp.int32, (TILE, TILE), 0)
    col_near = lax.broadcasted_iota(jnp.int32, (TILE, TILE), 1)
    row_far = lax.broadcasted_iota(jnp.int32, (TILE, OFF_DEV), 0)
    col_far = lax.broadcasted_iota(jnp.int32, (TILE, OFF_DEV), 1)
    tile_index = jnp.arange(tile_count, dtype=jnp.int32)[:, None, None]
    keep_near = (col_near >= row_near)[None] & (col_near - row_near < OFF_DEV)[None] & (tile_index * TILE + col_near[None] < room_left)
    keep_far = (TILE + col_far - row_far < OFF_DEV)[None] & ((tile_index + 1) * TILE + col_far[None] < room_left)
    near_scores = jnp.where(keep_near, near_scores, -1.0)
    far_scores = jnp.where(keep_far, far_scores, -1.0)
    best_rows = jnp.maximum(near_scores.max(axis=2), far_scores.max(axis=2)).reshape(-1)
    floor_row = jnp.full((1, TILE), -1.0, near_scores.dtype)
    upper_part = jnp.concatenate([near_scores.max(axis=1), floor_row], axis=0)
    far_cols = jnp.pad(far_scores.max(axis=1), ((0, 0), (0, TILE - OFF_DEV)), constant_values=-1.0)
    lower_part = jnp.concatenate([floor_row, far_cols], axis=0)
    return (best_rows, jnp.maximum(upper_part, lower_part).reshape(-1))

def reference(series, tail, band_starts):
    length = series.shape[0]
    group_rows = tile_batch * TILE
    group_count = length // group_rows
    spare_cells = BAND_BASE + BAND_SPAN + 2 * group_rows + M + 2 * TILE
    extended = jnp.concatenate([series, tail, jnp.zeros((spare_cells,), series.dtype)])
    initial = jnp.full((length + spare_cells,), -1.0, series.dtype)

    def advance(columns, group_index):
        first_row = group_index * group_rows
        row_piece = lax.dynamic_slice_in_dim(extended, first_row, group_rows + M + TILE)
        matrix = hankel(row_piece, tile_batch)
        center, factor = moments(matrix)
        row_z = normed(matrix, center, factor)
        row_best = None
        for band_index in range(N_BAND):
            col_begin = (first_row + BAND_BASE + band_starts[band_index]).astype(jnp.int32)
            col_piece = lax.dynamic_slice_in_dim(extended, col_begin, (tile_batch + 2) * TILE + M)
            col_matrix = hankel(col_piece, tile_batch + 1)
            col_center, col_factor = moments(col_matrix)
            col_z = normed(col_matrix, col_center, col_factor)
            row_found, col_reach = score_group(row_z, col_z, length - col_begin)
            current = lax.dynamic_slice_in_dim(columns, col_begin, (tile_batch + 1) * TILE)
            columns = lax.dynamic_update_slice(columns, jnp.maximum(current, col_reach), (col_begin,))
            row_best = row_found if row_best is None else jnp.maximum(row_best, row_found)
        return (columns, row_best)
    columns, row_found = lax.scan(advance, initial, jnp.arange(group_count, dtype=jnp.int32))
    return (row_found.reshape(length), columns[:length])
```

```python
import functools

import jax
import jax.numpy as jnp
from jax import lax
from jax.experimental import pallas as pl
from jax.experimental.pallas import tpu as pltpu
from jax.sharding import PartitionSpec as P

M = 256
TILE = 128
OFF_DEV = 128
BAND_SPAN = 4096
BAND_BLOCKS = 4


EPS = 1e-06
tile_batch = 16


def from_behind(block, axis, distance):
    devices = range(lax.axis_size(axis))
    route = [(i - distance, i) for i in devices if i - distance in devices]
    return lax.ppermute(block, axis, route)


def hankel(samples, tile_count):
    length = tile_count * TILE + M
    shifted = jnp.stack(
        [lax.slice_in_dim(samples, offset, offset + length) for offset in range(TILE)]
    )
    blocks = shifted.reshape(TILE, length // TILE, TILE)
    joined = jnp.concatenate(
        [blocks[:, stride : stride + tile_count] for stride in range(M // TILE)], axis=2
    )
    return jnp.swapaxes(joined, 0, 1)


def moments(matrix):
    center = jnp.mean(matrix, axis=-1)
    spread = matrix - center[..., None]
    factor = lax.rsqrt(jnp.sum(spread * spread, axis=-1) + M * EPS)
    return (center, factor)


def normed(matrix, center, factor):
    return ((matrix - center[..., None]) * factor[..., None]).astype(jnp.bfloat16)


def score_group(row_z, col_z, room_left):
    tile_count = row_z.shape[0]
    near_scores = jnp.einsum("tim,tjm->tij", row_z, col_z[:-1], preferred_element_type=jnp.float32)
    far_scores = jnp.einsum(
        "tim,tjm->tij", row_z, col_z[1:, :OFF_DEV], preferred_element_type=jnp.float32
    )
    row_near = lax.broadcasted_iota(jnp.int32, (TILE, TILE), 0)
    col_near = lax.broadcasted_iota(jnp.int32, (TILE, TILE), 1)
    row_far = lax.broadcasted_iota(jnp.int32, (TILE, OFF_DEV), 0)
    col_far = lax.broadcasted_iota(jnp.int32, (TILE, OFF_DEV), 1)
    tile_index = jnp.arange(tile_count, dtype=jnp.int32)[:, None, None]
    keep_near = (
        (col_near >= row_near)[None]
        & (col_near - row_near < OFF_DEV)[None]
        & (tile_index * TILE + col_near[None] < room_left)
    )
    keep_far = (TILE + col_far - row_far < OFF_DEV)[None] & (
        (tile_index + 1) * TILE + col_far[None] < room_left
    )
    near_scores = jnp.where(keep_near, near_scores, -1.0)
    far_scores = jnp.where(keep_far, far_scores, -1.0)
    best_rows = jnp.maximum(near_scores.max(axis=2), far_scores.max(axis=2)).reshape(-1)
    floor_row = jnp.full((1, TILE), -1.0, jnp.float32)
    upper_part = jnp.concatenate([near_scores.max(axis=1), floor_row], axis=0)
    far_cols = far_scores.max(axis=1)
    lower_part = jnp.concatenate([floor_row, far_cols], axis=0)
    return (best_rows, jnp.maximum(upper_part, lower_part).reshape(-1))


def place_columns(col_groups, start, buffer_len):
    group_rows = tile_batch * TILE
    count = col_groups.shape[0]
    main_part = col_groups[:, :group_rows].reshape(-1)
    carry_part = jnp.concatenate(
        [col_groups[:, group_rows:], jnp.full((count, group_rows - TILE), -1.0, jnp.float32)],
        axis=1,
    ).reshape(-1)
    shifted = jnp.concatenate([jnp.full((group_rows,), -1.0, jnp.float32), carry_part])[
        : count * group_rows + TILE
    ]
    reached = jnp.maximum(
        jnp.concatenate([main_part, jnp.full((TILE,), -1.0, jnp.float32)]), shifted
    )
    buffer_all = jnp.full((buffer_len,), -1.0, jnp.float32)
    return lax.dynamic_update_slice(buffer_all, reached, (start,))


def body(series, tail, band_starts):
    block_len = series.shape[0]
    group_rows = tile_batch * TILE
    group_count = block_len // group_rows
    position = lax.axis_index("tm")
    devices = lax.axis_size("tm")
    distance = BAND_BLOCKS
    following = from_behind(series[:M], "tm", -1)
    following = jnp.where(position == devices - 1, tail, following)
    extended = jnp.concatenate([series, following])
    row_source = jnp.concatenate([extended, jnp.zeros((TILE,), jnp.float32)])

    def own_group(group_index):
        row_piece = lax.dynamic_slice_in_dim(
            row_source, group_index * group_rows, group_rows + M + TILE
        )
        matrix = hankel(row_piece, tile_batch)
        center, factor = moments(matrix)
        return (center.reshape(-1), factor.reshape(-1), normed(matrix, center, factor))

    centers, factors, row_z = lax.map(own_group, jnp.arange(group_count, dtype=jnp.int32))
    centers = centers.reshape(block_len)
    factors = factors.reshape(block_len)
    padding = jnp.zeros((2 * TILE,), jnp.float32)
    far_samples = from_behind(extended, "tm", -distance)
    next_samples = from_behind(series[M : M + BAND_SPAN], "tm", -distance - 1)
    pair_samples = jnp.concatenate([far_samples, next_samples, padding])
    buffer_len = block_len + BAND_SPAN + TILE
    band_count = band_starts.shape[0]
    band_here = lax.axis_index("band")
    offset_start = jnp.sum(
        jnp.where(jnp.arange(band_count, dtype=jnp.int32) == band_here, band_starts, 0)
    )
    room_all = (devices - position - distance) * block_len - offset_start

    def pair_group(inputs):
        group_index, group_z = inputs
        col_begin = offset_start + group_index * group_rows
        col_piece = lax.dynamic_slice_in_dim(pair_samples, col_begin, (tile_batch + 2) * TILE + M)
        matrix = hankel(col_piece, tile_batch + 1)
        center, factor = moments(matrix)
        col_z = normed(matrix, center, factor)
        return score_group(group_z, col_z, room_all - group_index * group_rows)

    row_best, col_groups = lax.map(pair_group, (jnp.arange(group_count, dtype=jnp.int32), row_z))
    lifted = place_columns(col_groups, offset_start, buffer_len) + 1.0
    returned = from_behind(lifted[:block_len], "tm", distance)
    returned_head = from_behind(lifted[block_len : block_len + BAND_SPAN], "tm", distance + 1)
    col_best = (
        jnp.maximum(
            returned,
            jnp.concatenate([returned_head, jnp.zeros((block_len - BAND_SPAN,), jnp.float32)]),
        )
        - 1.0
    )
    return lax.pmax((row_best.reshape(block_len), col_best), "band")


SLOTS = 4
LANES = 128


def pair_kernel(
    blocks,
    starts_ref,
    x_ref,
    tail_ref,
    row_out,
    col_out,
    ext,
    rows_x,
    shifted,
    stats,
    row_z,
    col_z,
    col_buf,
    row_res,
    col_res,
    slots,
    carry_in,
    in_send,
    in_recv,
    out_send,
    row_recv,
    slot_recv,
    carry_recv,
):
    half = BAND_BLOCKS
    block_rows = x_ref.shape[0]
    quarter = block_rows // SLOTS
    piece = 2 * quarter + 8
    band_count = starts_ref.shape[0]
    p = lax.axis_index("tm")
    b = lax.axis_index("band")
    low = p < half
    high = p >= half
    partner = lax.rem(p + half, blocks)
    part = b + 2 * (p // half)
    first = 2 * quarter + quarter * b

    def remote(src, dst, send, recv, tm, band):
        return pltpu.make_async_remote_copy(
            src_ref=src,
            dst_ref=dst,
            send_sem=send,
            recv_sem=recv,
            device_id={"tm": tm, "band": band},
            device_id_type=pl.DeviceIdType.MESH,
        )

    head_sender = jnp.logical_and(p >= b, p < half + b)
    next_sender = p > half
    next_taker = jnp.logical_and(high, p < blocks - 1)
    carry_sender = jnp.logical_and(next_taker, b == 1)
    carry_taker = next_sender

    barrier = pltpu.get_barrier_semaphore()

    def greet(tm, band):
        pl.semaphore_signal(
            barrier, 1, device_id={"tm": tm, "band": band}, device_id_type=pl.DeviceIdType.MESH
        )

    greet(p, 1 - b)
    greet(partner, 0)
    greet(partner, 1)

    @pl.when(jnp.logical_and(high, b == 1))
    def _():
        greet(p - half + 1, 1)

    @pl.when(next_taker)
    def _():
        greet(p + 1, b)

    @pl.when(carry_taker)
    def _():
        greet(p - 1, 1)

    col_buf[...] = jnp.full(col_buf.shape, -1.0, jnp.float32)

    @pl.when(low)
    def _():
        rows_x[...] = x_ref[pl.ds(pl.multiple_of(quarter * b, 8), quarter + 8), :]
        col_out[...] = jnp.full(col_out.shape, -1.0, jnp.float32)

    @pl.when(high)
    def _():
        ext[pl.ds(2 * quarter, 2 * quarter), :] = x_ref[pl.ds(2 * quarter, 2 * quarter), :]
        row_out[...] = jnp.full(row_out.shape, -1.0, jnp.float32)

    @pl.when(p == blocks - 1)
    def _():
        ext[pl.ds(block_rows, quarter + 8), :] = jnp.zeros((quarter + 8, LANES), jnp.float32)
        ext[pl.ds(block_rows, M // LANES), :] = tail_ref[...]

    head_here = jnp.where(jnp.logical_and(b == 1, jnp.logical_and(p >= 1, p <= half)), 1, 0)
    next_here = jnp.where(next_sender, 1, 0)
    carry_here = jnp.where(carry_sender, 2, 0)
    pl.semaphore_wait(barrier, 3 + head_here + next_here + carry_here)

    cols_copy = remote(
        x_ref.at[pl.ds(pl.multiple_of(quarter * b, 8), piece), :],
        ext.at[pl.ds(pl.multiple_of(first, 8), piece), :],
        in_send.at[0],
        in_recv.at[0],
        partner,
        b,
    )
    rows_copy = remote(
        x_ref.at[pl.ds(pl.multiple_of(first, 8), quarter), :],
        rows_x.at[pl.ds(0, quarter), :],
        in_send.at[1],
        in_recv.at[1],
        partner,
        b,
    )
    head_copy = remote(
        x_ref.at[pl.ds(pl.multiple_of(3 * quarter * (1 - b), 8), 8), :],
        rows_x.at[pl.ds(quarter, 8), :],
        in_send.at[2],
        in_recv.at[2],
        lax.rem(p + half - b, blocks),
        b,
    )
    next_copy = remote(
        x_ref.at[pl.ds(0, quarter + 8), :],
        ext.at[pl.ds(block_rows, quarter + 8), :],
        in_send.at[3],
        in_recv.at[3],
        lax.rem(p + blocks - 1, blocks),
        b,
    )
    pl.when(high)(cols_copy.start)
    pl.when(low)(rows_copy.start)
    pl.when(head_sender)(head_copy.start)
    pl.when(next_sender)(next_copy.start)

    pl.when(low)(cols_copy.wait_recv)

    @pl.when(high)
    def _():
        rows_copy.wait_recv()
        head_copy.wait_recv()

    pl.when(next_taker)(next_copy.wait_recv)

    span = quarter + 8
    lane = lax.broadcasted_iota(jnp.int32, (span, LANES), 1)

    def moments_of(samples):
        mean, spread = samples, None
        width = 1

        def ahead(values):
            below = pltpu.roll(values, span - 1, 0)
            if width == LANES:
                return below
            turned = pltpu.roll(values, LANES - width, 1)
            return jnp.where(lane < LANES - width, turned, pltpu.roll(turned, span - 1, 0))

        while width < M:
            other = ahead(mean)
            gap = mean - other
            term = gap * gap * (0.5 * width)
            spread = term if spread is None else spread + ahead(spread) + term
            mean = 0.5 * (mean + other)
            width *= 2
        return mean, lax.rsqrt(spread + M * EPS)

    square = (LANES, LANES)
    upper = lax.broadcasted_iota(jnp.int32, square, 1) <= lax.broadcasted_iota(jnp.int32, square, 0)
    keep = lax.broadcasted_iota(jnp.int32, square, 1) >= lax.broadcasted_iota(jnp.int32, square, 0)

    def turned_row(source, index):
        line = source[pl.ds(index, 1), :]
        return pltpu.roll(jnp.broadcast_to(line, square), 1, 1, stride=1, stride_axis=0)

    def build(source, center, factor, count, unroll, store):
        turn0 = turned_row(source, 0)
        turn1 = turned_row(source, 1)

        def step(index, state):
            turn, near = state
            following = turned_row(source, index + 2)
            far = jnp.where(upper, turn, following)
            c = center[pl.ds(index, 1), :]
            f = factor[pl.ds(index, 1), :]
            z = jnp.concatenate([(near - c) * f, (far - c) * f], axis=0)
            store(index, z)
            return following, far

        lax.fori_loop(0, count, step, (turn1, jnp.where(upper, turn0, turn1)), unroll=unroll)

    mean, factor = moments_of(rows_x[...])
    stats[0] = mean
    stats[1] = factor

    def store_row(index, z):
        row_z[index] = z.astype(jnp.bfloat16).T

    build(rows_x, stats.at[0], stats.at[1], quarter, 2, store_row)

    starts = [starts_ref[c] for c in range(band_count)]
    whole = [lax.shift_right_logical(s, 7) for s in starts]
    rest = [lax.bitwise_and(s, LANES - 1) for s in starts]
    for c in range(band_count):
        back = lax.rem(LANES - rest[c], LANES)
        here = pltpu.roll(ext[pl.ds(first + whole[c], span), :], back, 1)
        below = pltpu.roll(ext[pl.ds(first + whole[c] + 1, span), :], back, 1)
        samples = jnp.where(lane < LANES - rest[c], here, below)
        shifted[c] = samples
        mean, factor = moments_of(samples)
        stats[2 + 2 * c] = mean
        stats[3 + 2 * c] = factor

        def store_col(index, z, c=c):
            col_z[c, index] = z.astype(jnp.bfloat16)

        build(shifted.at[c], stats.at[2 + 2 * c], stats.at[3 + 2 * c], quarter + 1, 3, store_col)

    last_block = lax.rem(p, half) + half
    room_all = (blocks - last_block) * block_rows * LANES - part * quarter * LANES
    lane_row = lax.broadcasted_iota(jnp.int32, (1, LANES), 1)

    def score(index, pending):
        best = None
        left = []
        for c in range(band_count):
            both = jnp.concatenate([col_z[c, index], col_z[c, index + 1]], axis=1)
            found = jnp.dot(row_z[index], both, preferred_element_type=jnp.float32)
            room = room_all - starts[c] - index * LANES
            near = found[:, :LANES] + jnp.where(lane_row < room, 0.0, -4.0)
            far = found[:, LANES:] + jnp.where(lane_row + LANES < room, 0.0, -4.0)
            near_cols = jnp.max(jnp.where(keep, near, -4.0), axis=0, keepdims=True)
            far_cols = jnp.max(jnp.where(keep, -4.0, far), axis=0, keepdims=True)
            col_buf[c, pl.ds(quarter + index, 1), :] = jnp.maximum(
                jnp.maximum(pending[c], near_cols), -1.0
            )
            left.append(jnp.maximum(far_cols, -1.0))
            joined = jnp.where(keep, near, far)
            best = joined if best is None else jnp.maximum(best, joined)
        row_res[pl.ds(index, 1), :] = jnp.maximum(jnp.max(best.T, axis=0, keepdims=True), -1.0)
        return tuple(left)

    floor = jnp.full((1, LANES), -1.0, jnp.float32)
    pending = lax.fori_loop(0, quarter, score, (floor,) * band_count, unroll=2)
    lane_wide = lax.broadcasted_iota(jnp.int32, (2 * quarter, LANES), 1)
    reached = None
    for c in range(band_count):
        col_buf[c, pl.ds(2 * quarter, 1), :] = pending[c]
        here = pltpu.roll(col_buf[c, pl.ds(quarter - whole[c], 2 * quarter), :], rest[c], 1)
        above = pltpu.roll(col_buf[c, pl.ds(quarter - whole[c] - 1, 2 * quarter), :], rest[c], 1)
        placed = jnp.where(lane_wide >= rest[c], here, above)
        reached = placed if reached is None else jnp.maximum(reached, placed)
    col_res[...] = reached

    place = pl.ds(pl.multiple_of(part * quarter, 8), quarter)
    row_to = [
        remote(row_res, row_out.at[place, :], out_send.at[k], row_recv.at[part], tm, band)
        for k, (tm, band) in enumerate([(p, 1 - b), (partner, 0), (partner, 1)])
    ]
    slot_to = [
        remote(col_res, slots.at[part], out_send.at[3 + k], slot_recv.at[part], tm, band)
        for k, (tm, band) in enumerate([(p, 1 - b), (partner, 0), (partner, 1)])
    ]
    lower = pl.ds(0, quarter)
    lower_to = remote(
        col_res.at[lower, :],
        slots.at[part, lower, :],
        out_send.at[3],
        slot_recv.at[part],
        p,
        1 - b,
    )
    carry_to = [
        remote(
            col_res.at[pl.ds(quarter, quarter), :],
            carry_in,
            out_send.at[6 + k],
            carry_recv.at[0],
            lax.rem(p + 1, blocks),
            k,
        )
        for k in range(2)
    ]

    @pl.when(low)
    def _():
        slot_to[1].start()
        slot_to[2].start()
        row_to[0].start()
        row_out[place, :] = row_res[...]

    @pl.when(high)
    def _():
        row_to[1].start()
        row_to[2].start()

    @pl.when(jnp.logical_and(high, b == 0))
    def _():
        slot_to[0].start()
        slots[2] = col_res[...]

    @pl.when(carry_sender)
    def _():
        carry_to[0].start()
        carry_to[1].start()

    @pl.when(jnp.logical_and(high, b == 1))
    def _():
        lower_to.start()
        slots[3, lower, :] = col_res[lower, :]

    def row_from(index):
        return remote(
            row_res,
            row_out.at[pl.ds(index * quarter, quarter), :],
            out_send.at[0],
            row_recv.at[index],
            p,
            1 - b,
        )

    def slot_from(index):
        return remote(
            col_res, slots.at[index], out_send.at[0], slot_recv.at[index], p, 1 - b
        )

    @pl.when(low)
    def _():
        pl.when(b == 1)(row_from(0).wait_recv)
        pl.when(b == 0)(row_from(1).wait_recv)
        row_from(2).wait_recv()
        row_from(3).wait_recv()

    @pl.when(high)
    def _():
        slot_from(0).wait_recv()
        slot_from(1).wait_recv()

    @pl.when(jnp.logical_and(high, b == 1))
    def _():
        slot_from(2).wait_recv()

    @pl.when(jnp.logical_and(high, b == 0))
    def _():
        remote(
            col_res.at[lower, :],
            slots.at[3, lower, :],
            out_send.at[0],
            slot_recv.at[3],
            p,
            1 - b,
        ).wait_recv()

    pl.when(carry_taker)(carry_to[0].wait_recv)

    @pl.when(p == half)
    def _():
        carry_in[...] = jnp.full(carry_in.shape, -1.0, jnp.float32)

    @pl.when(high)
    def _():
        col_out[pl.ds(0, quarter), :] = jnp.maximum(slots[0, lower, :], carry_in[...])
        for k in range(1, SLOTS):
            col_out[pl.ds(k * quarter, quarter), :] = jnp.maximum(
                slots[k, lower, :], slots[k - 1, pl.ds(quarter, quarter), :]
            )

    @pl.when(high)
    def _():
        cols_copy.wait_send()
        row_to[1].wait_send()
        row_to[2].wait_send()

    @pl.when(low)
    def _():
        rows_copy.wait_send()
        slot_to[1].wait_send()
        slot_to[2].wait_send()
        row_to[0].wait_send()

    pl.when(head_sender)(head_copy.wait_send)
    pl.when(next_sender)(next_copy.wait_send)
    pl.when(jnp.logical_and(high, b == 0))(slot_to[0].wait_send)
    pl.when(jnp.logical_and(high, b == 1))(lower_to.wait_send)

    @pl.when(carry_sender)
    def _():
        carry_to[0].wait_send()
        carry_to[1].wait_send()


def spread_body(series, tail, band_starts):
    block_rows = series.shape[0] // LANES
    quarter = block_rows // SLOTS
    band_count = band_starts.shape[0]
    blocks = lax.axis_size("tm")
    span = quarter + 8
    vmem = pl.BlockSpec(memory_space=pltpu.VMEM)
    whole = jax.ShapeDtypeStruct((block_rows, LANES), jnp.float32)

    def buffer(*shape, kind=jnp.float32):
        return pltpu.VMEM(shape, kind)

    best_rows, best_cols = pl.pallas_call(
        functools.partial(pair_kernel, blocks),
        out_shape=(whole, whole),
        in_specs=[pl.BlockSpec(memory_space=pltpu.SMEM), vmem, vmem],
        out_specs=(vmem, vmem),
        scratch_shapes=[
            buffer(block_rows + span, LANES),
            buffer(span, LANES),
            buffer(band_count, span, LANES),
            buffer(2 + 2 * band_count, span, LANES),
            buffer(quarter, LANES, M, kind=jnp.bfloat16),
            buffer(band_count, quarter + 1, M, LANES, kind=jnp.bfloat16),
            buffer(band_count, 3 * quarter + 8, LANES),
            buffer(quarter, LANES),
            buffer(2 * quarter, LANES),
            buffer(SLOTS, 2 * quarter, LANES),
            buffer(quarter, LANES),
            pltpu.SemaphoreType.DMA((4,)),
            pltpu.SemaphoreType.DMA((4,)),
            pltpu.SemaphoreType.DMA((8,)),
            pltpu.SemaphoreType.DMA((SLOTS,)),
            pltpu.SemaphoreType.DMA((SLOTS,)),
            pltpu.SemaphoreType.DMA((1,)),
        ],
        compiler_params=pltpu.CompilerParams(
            collective_id=0, has_side_effects=True, vmem_limit_bytes=40 * 1024 * 1024
        ),
        name="banded_pairs",
    )(band_starts, series.reshape(block_rows, LANES), tail.reshape(-1, LANES))
    return best_rows.reshape(-1), best_cols.reshape(-1)


def solution(mesh):
    placed = (P(("groups", "tm")), P("groups"), P("groups"))

    def chosen(series, tail, band_starts):
        halves = lax.axis_size("tm") == 2 * BAND_BLOCKS
        if halves and series.shape[0] == SLOTS * BAND_SPAN and lax.axis_size("band") == 2:
            return spread_body(series, tail, band_starts)
        return body(series, tail, band_starts)

    return jax.shard_map(
        chosen,
        mesh=mesh,
        in_specs=placed,
        out_specs=(P(("groups", "tm")), P(("groups", "tm"))),
        check_vma=False,
    )
```

```python
import functools

import jax
import jax.numpy as jnp
from jax import lax
from jax.experimental import pallas as pl
from jax.experimental.pallas import tpu as pltpu
from jax.sharding import PartitionSpec as P

M = 256
TILE = 128
OFF_DEV = 128
BAND_SPAN = 4096
BAND_BLOCKS = 4


EPS = 1e-06
tile_batch = 16


def from_behind(block, axis, distance):
    devices = range(lax.axis_size(axis))
    route = [(i - distance, i) for i in devices if i - distance in devices]
    return lax.ppermute(block, axis, route)


def hankel(samples, tile_count):
    length = tile_count * TILE + M
    shifted = jnp.stack(
        [lax.slice_in_dim(samples, offset, offset + length) for offset in range(TILE)]
    )
    blocks = shifted.reshape(TILE, length // TILE, TILE)
    joined = jnp.concatenate(
        [blocks[:, stride : stride + tile_count] for stride in range(M // TILE)], axis=2
    )
    return jnp.swapaxes(joined, 0, 1)


def moments(matrix):
    center = jnp.mean(matrix, axis=-1)
    spread = matrix - center[..., None]
    factor = lax.rsqrt(jnp.sum(spread * spread, axis=-1) + M * EPS)
    return (center, factor)


def normed(matrix, center, factor):
    return ((matrix - center[..., None]) * factor[..., None]).astype(jnp.bfloat16)


def score_group(row_z, col_z, room_left):
    tile_count = row_z.shape[0]
    near_scores = jnp.einsum("tim,tjm->tij", row_z, col_z[:-1], preferred_element_type=jnp.float32)
    far_scores = jnp.einsum(
        "tim,tjm->tij", row_z, col_z[1:, :OFF_DEV], preferred_element_type=jnp.float32
    )
    row_near = lax.broadcasted_iota(jnp.int32, (TILE, TILE), 0)
    col_near = lax.broadcasted_iota(jnp.int32, (TILE, TILE), 1)
    row_far = lax.broadcasted_iota(jnp.int32, (TILE, OFF_DEV), 0)
    col_far = lax.broadcasted_iota(jnp.int32, (TILE, OFF_DEV), 1)
    tile_index = jnp.arange(tile_count, dtype=jnp.int32)[:, None, None]
    keep_near = (
        (col_near >= row_near)[None]
        & (col_near - row_near < OFF_DEV)[None]
        & (tile_index * TILE + col_near[None] < room_left)
    )
    keep_far = (TILE + col_far - row_far < OFF_DEV)[None] & (
        (tile_index + 1) * TILE + col_far[None] < room_left
    )
    near_scores = jnp.where(keep_near, near_scores, -1.0)
    far_scores = jnp.where(keep_far, far_scores, -1.0)
    best_rows = jnp.maximum(near_scores.max(axis=2), far_scores.max(axis=2)).reshape(-1)
    floor_row = jnp.full((1, TILE), -1.0, jnp.float32)
    upper_part = jnp.concatenate([near_scores.max(axis=1), floor_row], axis=0)
    far_cols = far_scores.max(axis=1)
    lower_part = jnp.concatenate([floor_row, far_cols], axis=0)
    return (best_rows, jnp.maximum(upper_part, lower_part).reshape(-1))


def place_columns(col_groups, start, buffer_len):
    group_rows = tile_batch * TILE
    count = col_groups.shape[0]
    main_part = col_groups[:, :group_rows].reshape(-1)
    carry_part = jnp.concatenate(
        [col_groups[:, group_rows:], jnp.full((count, group_rows - TILE), -1.0, jnp.float32)],
        axis=1,
    ).reshape(-1)
    shifted = jnp.concatenate([jnp.full((group_rows,), -1.0, jnp.float32), carry_part])[
        : count * group_rows + TILE
    ]
    reached = jnp.maximum(
        jnp.concatenate([main_part, jnp.full((TILE,), -1.0, jnp.float32)]), shifted
    )
    buffer_all = jnp.full((buffer_len,), -1.0, jnp.float32)
    return lax.dynamic_update_slice(buffer_all, reached, (start,))


def body(series, tail, band_starts):
    block_len = series.shape[0]
    group_rows = tile_batch * TILE
    group_count = block_len // group_rows
    position = lax.axis_index("tm")
    devices = lax.axis_size("tm")
    distance = BAND_BLOCKS
    following = from_behind(series[:M], "tm", -1)
    following = jnp.where(position == devices - 1, tail, following)
    extended = jnp.concatenate([series, following])
    row_source = jnp.concatenate([extended, jnp.zeros((TILE,), jnp.float32)])

    def own_group(group_index):
        row_piece = lax.dynamic_slice_in_dim(
            row_source, group_index * group_rows, group_rows + M + TILE
        )
        matrix = hankel(row_piece, tile_batch)
        center, factor = moments(matrix)
        return (center.reshape(-1), factor.reshape(-1), normed(matrix, center, factor))

    centers, factors, row_z = lax.map(own_group, jnp.arange(group_count, dtype=jnp.int32))
    centers = centers.reshape(block_len)
    factors = factors.reshape(block_len)
    padding = jnp.zeros((2 * TILE,), jnp.float32)
    far_samples = from_behind(extended, "tm", -distance)
    next_samples = from_behind(series[M : M + BAND_SPAN], "tm", -distance - 1)
    pair_samples = jnp.concatenate([far_samples, next_samples, padding])
    buffer_len = block_len + BAND_SPAN + TILE
    band_count = band_starts.shape[0]
    band_here = lax.axis_index("band")
    offset_start = jnp.sum(
        jnp.where(jnp.arange(band_count, dtype=jnp.int32) == band_here, band_starts, 0)
    )
    room_all = (devices - position - distance) * block_len - offset_start

    def pair_group(inputs):
        group_index, group_z = inputs
        col_begin = offset_start + group_index * group_rows
        col_piece = lax.dynamic_slice_in_dim(pair_samples, col_begin, (tile_batch + 2) * TILE + M)
        matrix = hankel(col_piece, tile_batch + 1)
        center, factor = moments(matrix)
        col_z = normed(matrix, center, factor)
        return score_group(group_z, col_z, room_all - group_index * group_rows)

    row_best, col_groups = lax.map(pair_group, (jnp.arange(group_count, dtype=jnp.int32), row_z))
    lifted = place_columns(col_groups, offset_start, buffer_len) + 1.0
    returned = from_behind(lifted[:block_len], "tm", distance)
    returned_head = from_behind(lifted[block_len : block_len + BAND_SPAN], "tm", distance + 1)
    col_best = (
        jnp.maximum(
            returned,
            jnp.concatenate([returned_head, jnp.zeros((block_len - BAND_SPAN,), jnp.float32)]),
        )
        - 1.0
    )
    return lax.pmax((row_best.reshape(block_len), col_best), "band")


SLOTS = 4
LANES = 128


def pair_kernel(
    blocks,
    starts_in,
    x_ref,
    tail_ref,
    row_out,
    col_out,
    starts_ref,
    ext,
    rows_x,
    rows_back,
    shifted,
    stats,
    across,
    row_z,
    col_z,
    col_buf,
    row_res,
    col_res,
    slots,
    carry_in,
    local,
    in_send,
    in_recv,
    out_send,
    row_recv,
    slot_recv,
    carry_recv,
):
    half = BAND_BLOCKS
    block_rows = x_ref.shape[0]
    quarter = block_rows // SLOTS
    piece = 2 * quarter + 8
    band_count = starts_ref.shape[0]
    p = lax.axis_index("tm")
    b = lax.axis_index("band")
    low = p < half
    high = p >= half
    partner = lax.rem(p + half, blocks)
    part = b + 2 * (p // half)
    first = 2 * quarter + quarter * b

    def remote(src, dst, send, recv, tm, band):
        return pltpu.make_async_remote_copy(
            src_ref=src,
            dst_ref=dst,
            send_sem=send,
            recv_sem=recv,
            device_id={"tm": tm, "band": band},
            device_id_type=pl.DeviceIdType.MESH,
        )

    head_sender = jnp.logical_and(p >= b, p < half + b)
    next_sender = p > half
    next_taker = jnp.logical_and(high, p < blocks - 1)
    carry_sender = jnp.logical_and(next_taker, b == 1)
    carry_taker = next_sender

    barrier = pltpu.get_barrier_semaphore()

    def greet(tm, band):
        pl.semaphore_signal(
            barrier, 1, device_id={"tm": tm, "band": band}, device_id_type=pl.DeviceIdType.MESH
        )

    greet(p, 1 - b)
    greet(partner, 0)
    greet(partner, 1)

    @pl.when(jnp.logical_and(high, b == 1))
    def _():
        greet(p - half + 1, 1)

    @pl.when(next_taker)
    def _():
        greet(p + 1, b)

    @pl.when(carry_taker)
    def _():
        greet(p - 1, 1)

    starts_copy = pltpu.make_async_copy(starts_in, starts_ref, local.at[0])
    own_rows = pltpu.make_async_copy(
        x_ref.at[pl.ds(pl.multiple_of(quarter * b, 8), quarter + 8), :], rows_x, local.at[1]
    )
    own_cols = pltpu.make_async_copy(
        x_ref.at[pl.ds(2 * quarter, 2 * quarter), :],
        ext.at[pl.ds(2 * quarter, 2 * quarter), :],
        local.at[1],
    )
    own_tail = pltpu.make_async_copy(
        tail_ref, ext.at[pl.ds(block_rows, M // LANES), :], local.at[2]
    )
    starts_copy.start()
    pl.when(low)(own_rows.start)
    pl.when(high)(own_cols.start)

    @pl.when(p == blocks - 1)
    def _():
        ext[pl.ds(block_rows, quarter + 8), :] = jnp.zeros((quarter + 8, LANES), jnp.float32)
        own_tail.start()

    col_buf[...] = jnp.full(col_buf.shape, -1.0, jnp.float32)

    @pl.when(low)
    def _():
        col_out[...] = jnp.full(col_out.shape, -1.0, jnp.float32)

    @pl.when(high)
    def _():
        row_out[...] = jnp.full(row_out.shape, -1.0, jnp.float32)

    head_here = jnp.where(jnp.logical_and(b == 1, jnp.logical_and(p >= 1, p <= half)), 1, 0)
    next_here = jnp.where(next_sender, 1, 0)
    carry_here = jnp.where(carry_sender, 2, 0)
    pl.semaphore_wait(barrier, 3 + head_here + next_here + carry_here)

    cols_copy = remote(
        x_ref.at[pl.ds(pl.multiple_of(quarter * b, 8), piece), :],
        ext.at[pl.ds(pl.multiple_of(first, 8), piece), :],
        in_send.at[0],
        in_recv.at[0],
        partner,
        b,
    )
    rows_copy = remote(
        x_ref.at[pl.ds(pl.multiple_of(first, 8), quarter), :],
        rows_x.at[pl.ds(0, quarter), :],
        in_send.at[1],
        in_recv.at[1],
        partner,
        b,
    )
    head_copy = remote(
        x_ref.at[pl.ds(pl.multiple_of(3 * quarter * (1 - b), 8), 8), :],
        rows_x.at[pl.ds(quarter, 8), :],
        in_send.at[2],
        in_recv.at[2],
        lax.rem(p + half - b, blocks),
        b,
    )
    next_copy = remote(
        x_ref.at[pl.ds(0, quarter + 8), :],
        ext.at[pl.ds(block_rows, quarter + 8), :],
        in_send.at[3],
        in_recv.at[3],
        lax.rem(p + blocks - 1, blocks),
        b,
    )
    pl.when(high)(cols_copy.start)
    pl.when(low)(rows_copy.start)
    pl.when(head_sender)(head_copy.start)
    pl.when(next_sender)(next_copy.start)

    starts_copy.wait()
    span = quarter + 8
    lane = lax.broadcasted_iota(jnp.int32, (span, LANES), 1)

    def moments_of(samples):
        mean, spread = samples, None
        width = 1

        def ahead(values):
            below = pltpu.roll(values, span - 1, 0)
            if width == LANES:
                return below
            turned = pltpu.roll(values, LANES - width, 1)
            return jnp.where(lane < LANES - width, turned, pltpu.roll(turned, span - 1, 0))

        while width < M:
            other = ahead(mean)
            gap = mean - other
            term = gap * gap * (0.5 * width)
            spread = term if spread is None else spread + ahead(spread) + term
            mean = 0.5 * (mean + other)
            width *= 2
        return mean, lax.rsqrt(spread + M * EPS)

    square = (LANES, LANES)
    upper = lax.broadcasted_iota(jnp.int32, square, 1) <= lax.broadcasted_iota(jnp.int32, square, 0)
    keep = lax.broadcasted_iota(jnp.int32, square, 1) >= lax.broadcasted_iota(jnp.int32, square, 0)

    def turned_row(source, index):
        line = source[pl.ds(index, 1), :]
        return pltpu.roll(jnp.broadcast_to(line, square), 1, 1, stride=1, stride_axis=0)

    lane_quarter = lax.broadcasted_iota(jnp.int32, (LANES, quarter), 1)

    def build_rows():
        samples = rows_x[...]
        mean, factor = moments_of(samples)
        across[0] = mean[:quarter].T
        across[1] = factor[:quarter].T
        flip = jnp.where(
            lax.broadcasted_iota(jnp.int32, square, 0) + lax.broadcasted_iota(jnp.int32, square, 1)
            == LANES - 1,
            1.0,
            0.0,
        ).astype(jnp.bfloat16)
        left = samples
        back = None
        for _ in range(3):
            some = left.astype(jnp.bfloat16)
            left = left - some.astype(jnp.float32)
            moved = jnp.dot(some, flip, preferred_element_type=jnp.float32)
            back = moved if back is None else back + moved
        rows_back[...] = back

        def turned(index):
            line = rows_back[pl.ds(index, 1), :]
            return pltpu.roll(jnp.broadcast_to(line, square), 0, 1, stride=1, stride_axis=0)

        def column(which, index):
            return jnp.sum(
                jnp.where(lane_quarter == index, across[which], 0.0), axis=1, keepdims=True
            )

        turn0 = turned(0)
        turn1 = turned(1)

        def step(index, state):
            turn, near = state
            following = turned(index + 2)
            far = jnp.where(keep, turn, following)
            c = column(0, index)
            f = column(1, index)
            row_z[index, :, :LANES] = ((near - c) * f).astype(jnp.bfloat16)
            row_z[index, :, LANES:] = ((far - c) * f).astype(jnp.bfloat16)
            return following, far

        lax.fori_loop(0, quarter, step, (turn1, jnp.where(keep, turn0, turn1)), unroll=4)

    starts = [starts_ref[c] for c in range(band_count)]
    whole = [lax.shift_right_logical(s, 7) for s in starts]
    rest = [lax.bitwise_and(s, LANES - 1) for s in starts]

    def build_cols():
        for c in range(band_count):
            back = lax.rem(LANES - rest[c], LANES)
            here = pltpu.roll(ext[pl.ds(first + whole[c], span), :], back, 1)
            below = pltpu.roll(ext[pl.ds(first + whole[c] + 1, span), :], back, 1)
            samples = jnp.where(lane < LANES - rest[c], here, below)
            shifted[c] = samples
            mean, factor = moments_of(samples)
            stats[2 * c] = mean
            stats[2 * c + 1] = factor

        def turned(c, index):
            line = shifted[c, pl.ds(index, 1), :]
            return pltpu.roll(jnp.broadcast_to(line, square), 1, 1, stride=1, stride_axis=0)

        for c in range(band_count):
            turn0 = turned(c, 0)
            turn1 = turned(c, 1)

            def step(index, state, c=c):
                turn, near = state
                following = turned(c, index + 2)
                far = jnp.where(upper, turn, following)
                center = stats[2 * c, pl.ds(index, 1), :]
                factor = stats[2 * c + 1, pl.ds(index, 1), :]
                col_z[c, index, :LANES, :] = ((near - center) * factor).astype(jnp.bfloat16)
                col_z[c, index, LANES:, :] = ((far - center) * factor).astype(jnp.bfloat16)
                return following, far

            lax.fori_loop(
                0, quarter + 1, step, (turn1, jnp.where(upper, turn0, turn1)), unroll=3
            )

    def phase(turn, _):
        rows_now = lax.rem(turn + p // half, 2) == 0

        @pl.when(rows_now)
        def _():
            pl.when(low)(own_rows.wait)

            @pl.when(high)
            def _():
                rows_copy.wait_recv()
                head_copy.wait_recv()

            build_rows()

        @pl.when(jnp.logical_not(rows_now))
        def _():
            pl.when(low)(cols_copy.wait_recv)
            pl.when(high)(own_cols.wait)
            pl.when(next_taker)(next_copy.wait_recv)
            pl.when(p == blocks - 1)(own_tail.wait)
            build_cols()

        return 0

    lax.fori_loop(0, 2, phase, 0)

    last_block = lax.rem(p, half) + half
    room_all = (blocks - last_block) * block_rows * LANES - part * quarter * LANES
    lane_row = lax.broadcasted_iota(jnp.int32, (1, LANES), 1)

    lane_square = lax.broadcasted_iota(jnp.int32, square, 1)

    def score(index, state):
        pending, rows_found = state
        best = None
        left = []
        for c in range(band_count):
            both = jnp.concatenate([col_z[c, index], col_z[c, index + 1]], axis=1)
            found = jnp.dot(row_z[index], both, preferred_element_type=jnp.float32)
            room = room_all - starts[c] - index * LANES
            near = found[:, :LANES] + jnp.where(lane_row < room, 0.0, -4.0)
            far = found[:, LANES:] + jnp.where(lane_row + LANES < room, 0.0, -4.0)
            near_cols = jnp.max(jnp.where(keep, near, -4.0), axis=0, keepdims=True)
            far_cols = jnp.max(jnp.where(keep, -4.0, far), axis=0, keepdims=True)
            col_buf[c, pl.ds(quarter + index, 1), :] = jnp.maximum(
                jnp.maximum(pending[c], near_cols), -1.0
            )
            left.append(jnp.maximum(far_cols, -1.0))
            joined = jnp.where(keep, near, far)
            best = joined if best is None else jnp.maximum(best, joined)
        rows_found = jnp.where(
            lane_square == index, jnp.max(best, axis=1, keepdims=True), rows_found
        )
        return tuple(left), rows_found

    floor = jnp.full((1, LANES), -1.0, jnp.float32)
    pending, rows_found = lax.fori_loop(
        0, quarter, score, ((floor,) * band_count, jnp.full(square, -1.0, jnp.float32)), unroll=4
    )
    row_res[...] = jnp.maximum(rows_found.T[:quarter], -1.0)
    lane_wide = lax.broadcasted_iota(jnp.int32, (2 * quarter, LANES), 1)
    reached = None
    for c in range(band_count):
        col_buf[c, pl.ds(2 * quarter, 1), :] = pending[c]
        here = pltpu.roll(col_buf[c, pl.ds(quarter - whole[c], 2 * quarter), :], rest[c], 1)
        above = pltpu.roll(col_buf[c, pl.ds(quarter - whole[c] - 1, 2 * quarter), :], rest[c], 1)
        placed = jnp.where(lane_wide >= rest[c], here, above)
        reached = placed if reached is None else jnp.maximum(reached, placed)
    col_res[...] = reached

    place = pl.ds(pl.multiple_of(part * quarter, 8), quarter)
    row_to = [
        remote(row_res, row_out.at[place, :], out_send.at[k], row_recv.at[part], tm, band)
        for k, (tm, band) in enumerate([(p, 1 - b), (partner, 0), (partner, 1)])
    ]
    slot_to = [
        remote(col_res, slots.at[part], out_send.at[3 + k], slot_recv.at[part], tm, band)
        for k, (tm, band) in enumerate([(p, 1 - b), (partner, 0), (partner, 1)])
    ]
    lower = pl.ds(0, quarter)
    lower_to = remote(
        col_res.at[lower, :],
        slots.at[part, lower, :],
        out_send.at[3],
        slot_recv.at[part],
        p,
        1 - b,
    )
    carry_to = [
        remote(
            col_res.at[pl.ds(quarter, quarter), :],
            carry_in,
            out_send.at[6 + k],
            carry_recv.at[0],
            lax.rem(p + 1, blocks),
            k,
        )
        for k in range(2)
    ]

    @pl.when(low)
    def _():
        slot_to[1].start()
        slot_to[2].start()
        row_to[0].start()
        row_out[place, :] = row_res[...]

    @pl.when(high)
    def _():
        row_to[1].start()
        row_to[2].start()

    @pl.when(jnp.logical_and(high, b == 0))
    def _():
        slot_to[0].start()
        slots[2] = col_res[...]

    @pl.when(carry_sender)
    def _():
        carry_to[0].start()
        carry_to[1].start()

    @pl.when(jnp.logical_and(high, b == 1))
    def _():
        lower_to.start()
        slots[3, lower, :] = col_res[lower, :]

    def row_from(index):
        return remote(
            row_res,
            row_out.at[pl.ds(index * quarter, quarter), :],
            out_send.at[0],
            row_recv.at[index],
            p,
            1 - b,
        )

    def slot_from(index):
        return remote(
            col_res, slots.at[index], out_send.at[0], slot_recv.at[index], p, 1 - b
        )

    @pl.when(low)
    def _():
        pl.when(b == 1)(row_from(0).wait_recv)
        pl.when(b == 0)(row_from(1).wait_recv)
        row_from(2).wait_recv()
        row_from(3).wait_recv()

    @pl.when(high)
    def _():
        slot_from(0).wait_recv()
        slot_from(1).wait_recv()

    @pl.when(jnp.logical_and(high, b == 1))
    def _():
        slot_from(2).wait_recv()

    @pl.when(jnp.logical_and(high, b == 0))
    def _():
        remote(
            col_res.at[lower, :],
            slots.at[3, lower, :],
            out_send.at[0],
            slot_recv.at[3],
            p,
            1 - b,
        ).wait_recv()

    pl.when(carry_taker)(carry_to[0].wait_recv)

    @pl.when(p == half)
    def _():
        carry_in[...] = jnp.full(carry_in.shape, -1.0, jnp.float32)

    @pl.when(high)
    def _():
        col_out[pl.ds(0, quarter), :] = jnp.maximum(slots[0, lower, :], carry_in[...])
        for k in range(1, SLOTS):
            col_out[pl.ds(k * quarter, quarter), :] = jnp.maximum(
                slots[k, lower, :], slots[k - 1, pl.ds(quarter, quarter), :]
            )

    @pl.when(high)
    def _():
        cols_copy.wait_send()
        row_to[1].wait_send()
        row_to[2].wait_send()

    @pl.when(low)
    def _():
        rows_copy.wait_send()
        slot_to[1].wait_send()
        slot_to[2].wait_send()
        row_to[0].wait_send()

    pl.when(head_sender)(head_copy.wait_send)
    pl.when(next_sender)(next_copy.wait_send)
    pl.when(jnp.logical_and(high, b == 0))(slot_to[0].wait_send)
    pl.when(jnp.logical_and(high, b == 1))(lower_to.wait_send)

    @pl.when(carry_sender)
    def _():
        carry_to[0].wait_send()
        carry_to[1].wait_send()


def spread_body(series, tail, band_starts):
    block_rows = series.shape[0] // LANES
    quarter = block_rows // SLOTS
    band_count = band_starts.shape[0]
    blocks = lax.axis_size("tm")
    span = quarter + 8
    vmem = pl.BlockSpec(memory_space=pltpu.VMEM)
    whole = jax.ShapeDtypeStruct((block_rows, LANES), jnp.float32)

    def buffer(*shape, kind=jnp.float32):
        return pltpu.VMEM(shape, kind)

    best_rows, best_cols = pl.pallas_call(
        functools.partial(pair_kernel, blocks),
        out_shape=(whole, whole),
        in_specs=[pl.BlockSpec(memory_space=pltpu.HBM)] * 3,
        out_specs=(vmem, vmem),
        scratch_shapes=[
            pltpu.SMEM((band_count,), jnp.int32),
            buffer(block_rows + span, LANES),
            buffer(span, LANES),
            buffer(span, LANES),
            buffer(band_count, span, LANES),
            buffer(2 * band_count, span, LANES),
            buffer(2, LANES, quarter),
            buffer(quarter, LANES, M, kind=jnp.bfloat16),
            buffer(band_count, quarter + 1, M, LANES, kind=jnp.bfloat16),
            buffer(band_count, 3 * quarter + 8, LANES),
            buffer(quarter, LANES),
            buffer(2 * quarter, LANES),
            buffer(SLOTS, 2 * quarter, LANES),
            buffer(quarter, LANES),
            pltpu.SemaphoreType.DMA((3,)),
            pltpu.SemaphoreType.DMA((4,)),
            pltpu.SemaphoreType.DMA((4,)),
            pltpu.SemaphoreType.DMA((8,)),
            pltpu.SemaphoreType.DMA((SLOTS,)),
            pltpu.SemaphoreType.DMA((SLOTS,)),
            pltpu.SemaphoreType.DMA((1,)),
        ],
        compiler_params=pltpu.CompilerParams(
            collective_id=0, has_side_effects=True, vmem_limit_bytes=64 * 1024 * 1024 - 32768
        ),
        name="banded_pairs",
    )(band_starts, series.reshape(block_rows, LANES), tail.reshape(-1, LANES))
    return best_rows.reshape(-1), best_cols.reshape(-1)


def solution(mesh):
    placed = (P(("groups", "tm")), P("groups"), P("groups"))

    def chosen(series, tail, band_starts):
        halves = lax.axis_size("tm") == 2 * BAND_BLOCKS
        if halves and series.shape[0] == SLOTS * BAND_SPAN and lax.axis_size("band") == 2:
            return spread_body(series, tail, band_starts)
        return body(series, tail, band_starts)

    return jax.shard_map(
        chosen,
        mesh=mesh,
        in_specs=placed,
        out_specs=(P(("groups", "tm")), P(("groups", "tm"))),
        check_vma=False,
    )
```

```python
import functools

import jax
import jax.numpy as jnp
from jax import lax
from jax.experimental import pallas as pl
from jax.experimental.pallas import tpu as pltpu
from jax.sharding import PartitionSpec as P

M = 256
TILE = 128
OFF_DEV = 128
BAND_SPAN = 4096
BAND_BLOCKS = 4


EPS = 1e-06
tile_batch = 16


def from_behind(block, axis, distance):
    devices = range(lax.axis_size(axis))
    route = [(i - distance, i) for i in devices if i - distance in devices]
    return lax.ppermute(block, axis, route)


def hankel(samples, tile_count):
    length = tile_count * TILE + M
    shifted = jnp.stack(
        [lax.slice_in_dim(samples, offset, offset + length) for offset in range(TILE)]
    )
    blocks = shifted.reshape(TILE, length // TILE, TILE)
    joined = jnp.concatenate(
        [blocks[:, stride : stride + tile_count] for stride in range(M // TILE)], axis=2
    )
    return jnp.swapaxes(joined, 0, 1)


def moments(matrix):
    center = jnp.mean(matrix, axis=-1)
    spread = matrix - center[..., None]
    factor = lax.rsqrt(jnp.sum(spread * spread, axis=-1) + M * EPS)
    return (center, factor)


def normed(matrix, center, factor):
    return ((matrix - center[..., None]) * factor[..., None]).astype(jnp.bfloat16)


def score_group(row_z, col_z, room_left):
    tile_count = row_z.shape[0]
    near_scores = jnp.einsum("tim,tjm->tij", row_z, col_z[:-1], preferred_element_type=jnp.float32)
    far_scores = jnp.einsum(
        "tim,tjm->tij", row_z, col_z[1:, :OFF_DEV], preferred_element_type=jnp.float32
    )
    row_near = lax.broadcasted_iota(jnp.int32, (TILE, TILE), 0)
    col_near = lax.broadcasted_iota(jnp.int32, (TILE, TILE), 1)
    row_far = lax.broadcasted_iota(jnp.int32, (TILE, OFF_DEV), 0)
    col_far = lax.broadcasted_iota(jnp.int32, (TILE, OFF_DEV), 1)
    tile_index = jnp.arange(tile_count, dtype=jnp.int32)[:, None, None]
    keep_near = (
        (col_near >= row_near)[None]
        & (col_near - row_near < OFF_DEV)[None]
        & (tile_index * TILE + col_near[None] < room_left)
    )
    keep_far = (TILE + col_far - row_far < OFF_DEV)[None] & (
        (tile_index + 1) * TILE + col_far[None] < room_left
    )
    near_scores = jnp.where(keep_near, near_scores, -1.0)
    far_scores = jnp.where(keep_far, far_scores, -1.0)
    best_rows = jnp.maximum(near_scores.max(axis=2), far_scores.max(axis=2)).reshape(-1)
    floor_row = jnp.full((1, TILE), -1.0, jnp.float32)
    upper_part = jnp.concatenate([near_scores.max(axis=1), floor_row], axis=0)
    far_cols = far_scores.max(axis=1)
    lower_part = jnp.concatenate([floor_row, far_cols], axis=0)
    return (best_rows, jnp.maximum(upper_part, lower_part).reshape(-1))


def place_columns(col_groups, start, buffer_len):
    group_rows = tile_batch * TILE
    count = col_groups.shape[0]
    main_part = col_groups[:, :group_rows].reshape(-1)
    carry_part = jnp.concatenate(
        [col_groups[:, group_rows:], jnp.full((count, group_rows - TILE), -1.0, jnp.float32)],
        axis=1,
    ).reshape(-1)
    shifted = jnp.concatenate([jnp.full((group_rows,), -1.0, jnp.float32), carry_part])[
        : count * group_rows + TILE
    ]
    reached = jnp.maximum(
        jnp.concatenate([main_part, jnp.full((TILE,), -1.0, jnp.float32)]), shifted
    )
    buffer_all = jnp.full((buffer_len,), -1.0, jnp.float32)
    return lax.dynamic_update_slice(buffer_all, reached, (start,))


def body(series, tail, band_starts):
    block_len = series.shape[0]
    group_rows = tile_batch * TILE
    group_count = block_len // group_rows
    position = lax.axis_index("tm")
    devices = lax.axis_size("tm")
    distance = BAND_BLOCKS
    following = from_behind(series[:M], "tm", -1)
    following = jnp.where(position == devices - 1, tail, following)
    extended = jnp.concatenate([series, following])
    row_source = jnp.concatenate([extended, jnp.zeros((TILE,), jnp.float32)])

    def own_group(group_index):
        row_piece = lax.dynamic_slice_in_dim(
            row_source, group_index * group_rows, group_rows + M + TILE
        )
        matrix = hankel(row_piece, tile_batch)
        center, factor = moments(matrix)
        return (center.reshape(-1), factor.reshape(-1), normed(matrix, center, factor))

    centers, factors, row_z = lax.map(own_group, jnp.arange(group_count, dtype=jnp.int32))
    centers = centers.reshape(block_len)
    factors = factors.reshape(block_len)
    padding = jnp.zeros((2 * TILE,), jnp.float32)
    far_samples = from_behind(extended, "tm", -distance)
    next_samples = from_behind(series[M : M + BAND_SPAN], "tm", -distance - 1)
    pair_samples = jnp.concatenate([far_samples, next_samples, padding])
    buffer_len = block_len + BAND_SPAN + TILE
    band_count = band_starts.shape[0]
    band_here = lax.axis_index("band")
    offset_start = jnp.sum(
        jnp.where(jnp.arange(band_count, dtype=jnp.int32) == band_here, band_starts, 0)
    )
    room_all = (devices - position - distance) * block_len - offset_start

    def pair_group(inputs):
        group_index, group_z = inputs
        col_begin = offset_start + group_index * group_rows
        col_piece = lax.dynamic_slice_in_dim(pair_samples, col_begin, (tile_batch + 2) * TILE + M)
        matrix = hankel(col_piece, tile_batch + 1)
        center, factor = moments(matrix)
        col_z = normed(matrix, center, factor)
        return score_group(group_z, col_z, room_all - group_index * group_rows)

    row_best, col_groups = lax.map(pair_group, (jnp.arange(group_count, dtype=jnp.int32), row_z))
    lifted = place_columns(col_groups, offset_start, buffer_len) + 1.0
    returned = from_behind(lifted[:block_len], "tm", distance)
    returned_head = from_behind(lifted[block_len : block_len + BAND_SPAN], "tm", distance + 1)
    col_best = (
        jnp.maximum(
            returned,
            jnp.concatenate([returned_head, jnp.zeros((block_len - BAND_SPAN,), jnp.float32)]),
        )
        - 1.0
    )
    return lax.pmax((row_best.reshape(block_len), col_best), "band")


SLOTS = 4
STRIP = 16
LANES = 128


def pair_kernel(
    blocks,
    starts_in,
    x_ref,
    tail_ref,
    row_out,
    col_out,
    starts_ref,
    ext,
    rows_x,
    rows_back,
    shifted,
    stats,
    across,
    row_z,
    col_z,
    col_buf,
    row_res,
    col_res,
    slots,
    carry_in,
    local,
    in_send,
    in_recv,
    out_send,
    row_recv,
    slot_recv,
    carry_recv,
):
    half = BAND_BLOCKS
    block_rows = x_ref.shape[0]
    quarter = block_rows // SLOTS
    piece = 2 * quarter + 8
    band_count = starts_ref.shape[0]
    p = lax.axis_index("tm")
    b = lax.axis_index("band")
    low = p < half
    high = p >= half
    partner = lax.rem(p + half, blocks)
    part = b + 2 * (p // half)
    first = 2 * quarter + quarter * b

    def remote(src, dst, send, recv, tm, band):
        return pltpu.make_async_remote_copy(
            src_ref=src,
            dst_ref=dst,
            send_sem=send,
            recv_sem=recv,
            device_id={"tm": tm, "band": band},
            device_id_type=pl.DeviceIdType.MESH,
        )

    head_sender = jnp.logical_and(p >= b, p < half + b)
    next_sender = p > half
    next_taker = jnp.logical_and(high, p < blocks - 1)
    carry_sender = jnp.logical_and(next_taker, b == 1)
    carry_taker = next_sender

    barrier = pltpu.get_barrier_semaphore()

    def greet(tm, band):
        pl.semaphore_signal(
            barrier, 1, device_id={"tm": tm, "band": band}, device_id_type=pl.DeviceIdType.MESH
        )

    greet(p, 1 - b)
    greet(partner, 0)
    greet(partner, 1)

    @pl.when(jnp.logical_and(high, b == 1))
    def _():
        greet(p - half + 1, 1)

    @pl.when(next_taker)
    def _():
        greet(p + 1, b)

    @pl.when(carry_taker)
    def _():
        greet(p - 1, 1)

    starts_copy = pltpu.make_async_copy(starts_in, starts_ref, local.at[0])
    own_rows = pltpu.make_async_copy(
        x_ref.at[pl.ds(pl.multiple_of(quarter * b, 8), quarter + 8), :], rows_x, local.at[1]
    )
    own_cols = pltpu.make_async_copy(
        x_ref.at[pl.ds(2 * quarter, 2 * quarter), :],
        ext.at[pl.ds(2 * quarter, 2 * quarter), :],
        local.at[1],
    )
    own_tail = pltpu.make_async_copy(
        tail_ref, ext.at[pl.ds(block_rows, M // LANES), :], local.at[2]
    )
    starts_copy.start()
    pl.when(low)(own_rows.start)
    pl.when(high)(own_cols.start)

    @pl.when(p == blocks - 1)
    def _():
        ext[pl.ds(block_rows, quarter + 8), :] = jnp.zeros((quarter + 8, LANES), jnp.float32)
        own_tail.start()

    col_buf[...] = jnp.full(col_buf.shape, -1.0, jnp.float32)

    @pl.when(low)
    def _():
        col_out[...] = jnp.full(col_out.shape, -1.0, jnp.float32)

    @pl.when(high)
    def _():
        row_out[...] = jnp.full(row_out.shape, -1.0, jnp.float32)

    head_here = jnp.where(jnp.logical_and(b == 1, jnp.logical_and(p >= 1, p <= half)), 1, 0)
    next_here = jnp.where(next_sender, 1, 0)
    carry_here = jnp.where(carry_sender, 2, 0)
    pl.semaphore_wait(barrier, 3 + head_here + next_here + carry_here)

    cols_copy = remote(
        x_ref.at[pl.ds(pl.multiple_of(quarter * b, 8), piece), :],
        ext.at[pl.ds(pl.multiple_of(first, 8), piece), :],
        in_send.at[0],
        in_recv.at[0],
        partner,
        b,
    )
    rows_copy = remote(
        x_ref.at[pl.ds(pl.multiple_of(first, 8), quarter), :],
        rows_x.at[pl.ds(0, quarter), :],
        in_send.at[1],
        in_recv.at[1],
        partner,
        b,
    )
    head_copy = remote(
        x_ref.at[pl.ds(pl.multiple_of(3 * quarter * (1 - b), 8), 8), :],
        rows_x.at[pl.ds(quarter, 8), :],
        in_send.at[2],
        in_recv.at[2],
        lax.rem(p + half - b, blocks),
        b,
    )
    next_copy = remote(
        x_ref.at[pl.ds(0, quarter + 8), :],
        ext.at[pl.ds(block_rows, quarter + 8), :],
        in_send.at[3],
        in_recv.at[3],
        lax.rem(p + blocks - 1, blocks),
        b,
    )
    pl.when(high)(cols_copy.start)
    pl.when(low)(rows_copy.start)
    pl.when(head_sender)(head_copy.start)
    pl.when(next_sender)(next_copy.start)

    starts_copy.wait()
    span = quarter + 8
    lane = lax.broadcasted_iota(jnp.int32, (span, LANES), 1)

    def moments_of(samples):
        mean, spread = samples, None
        width = 1

        def ahead(values):
            below = pltpu.roll(values, span - 1, 0)
            if width == LANES:
                return below
            turned = pltpu.roll(values, LANES - width, 1)
            return jnp.where(lane < LANES - width, turned, pltpu.roll(turned, span - 1, 0))

        while width < M:
            other = ahead(mean)
            gap = mean - other
            term = gap * gap * (0.5 * width)
            spread = term if spread is None else spread + ahead(spread) + term
            mean = 0.5 * (mean + other)
            width *= 2
        return mean, lax.rsqrt(spread + M * EPS)

    square = (LANES, LANES)
    keep = lax.broadcasted_iota(jnp.int32, square, 1) >= lax.broadcasted_iota(jnp.int32, square, 0)

    def turned_row(source, index):
        line = source[pl.ds(index, 1), :]
        return pltpu.roll(jnp.broadcast_to(line, square), 1, 1, stride=1, stride_axis=0)

    strip_lane = lax.broadcasted_iota(jnp.int32, (STRIP, LANES), 1)
    strip_row = lax.broadcasted_iota(jnp.int32, (STRIP, LANES), 0)
    strip_quarter = lax.broadcasted_iota(jnp.int32, (STRIP, quarter), 1)

    def build_rows():
        samples = rows_x[...]
        mean, factor = moments_of(samples)
        across[0] = mean[:quarter].T
        across[1] = factor[:quarter].T
        flip = jnp.where(
            lax.broadcasted_iota(jnp.int32, square, 0) + lax.broadcasted_iota(jnp.int32, square, 1)
            == LANES - 1,
            1.0,
            0.0,
        ).astype(jnp.bfloat16)
        left = samples
        back = None
        for _ in range(3):
            some = left.astype(jnp.bfloat16)
            left = left - some.astype(jnp.float32)
            moved = jnp.dot(some, flip, preferred_element_type=jnp.float32)
            back = moved if back is None else back + moved
        rows_back[...] = back

        for top in range(0, LANES, STRIP):
            strip = pl.ds(top, STRIP)
            inside = strip_lane >= strip_row + top
            centers = across[0, strip, :]
            factors = across[1, strip, :]

            def turned(index, top=top):
                line = rows_back[pl.ds(index, 1), :]
                return pltpu.roll(
                    jnp.broadcast_to(line, (STRIP, LANES)), top, 1, stride=1, stride_axis=0
                )

            def column(values, index):
                chosen = jnp.where(strip_quarter == index, values, 0.0)
                return jnp.sum(chosen, axis=1, keepdims=True)

            def step(
                index,
                state,
                strip=strip,
                inside=inside,
                centers=centers,
                factors=factors,
                turned=turned,
            ):
                turn, near = state
                following = turned(index + 2)
                far = jnp.where(inside, turn, following)
                c = column(centers, index)
                f = column(factors, index)
                row_z[index, strip, :LANES] = ((near - c) * f).astype(jnp.bfloat16)
                row_z[index, strip, LANES:] = ((far - c) * f).astype(jnp.bfloat16)
                return following, far

            turn0 = turned(0)
            turn1 = turned(1)
            lax.fori_loop(
                0, quarter, step, (turn1, jnp.where(inside, turn0, turn1)), unroll=8
            )

    starts = [starts_ref[c] for c in range(band_count)]
    whole = [lax.shift_right_logical(s, 7) for s in starts]
    rest = [lax.bitwise_and(s, LANES - 1) for s in starts]

    def build_cols():
        for c in range(band_count):
            back = lax.rem(LANES - rest[c], LANES)
            here = pltpu.roll(ext[pl.ds(first + whole[c], span), :], back, 1)
            below = pltpu.roll(ext[pl.ds(first + whole[c] + 1, span), :], back, 1)
            samples = jnp.where(lane < LANES - rest[c], here, below)
            shifted[c] = samples
            mean, factor = moments_of(samples)
            stats[2 * c] = mean
            stats[2 * c + 1] = factor

        for top in range(0, LANES, STRIP):
            strip = pl.ds(top, STRIP)
            strip_far = pl.ds(LANES + top, STRIP)
            inside = strip_lane <= strip_row + top

            def turned(c, index, top=top):
                line = shifted[c, pl.ds(index, 1), :]
                return pltpu.roll(
                    jnp.broadcast_to(line, (STRIP, LANES)), top + 1, 1, stride=1, stride_axis=0
                )

            def step(
                index, state, strip=strip, strip_far=strip_far, inside=inside, turned=turned
            ):
                after = []
                for c in range(band_count):
                    turn, near = state[c]
                    following = turned(c, index + 2)
                    far = jnp.where(inside, turn, following)
                    center = stats[2 * c, pl.ds(index, 1), :]
                    factor = stats[2 * c + 1, pl.ds(index, 1), :]
                    col_z[c, index, strip, :] = ((near - center) * factor).astype(jnp.bfloat16)
                    col_z[c, index, strip_far, :] = ((far - center) * factor).astype(jnp.bfloat16)
                    after.append((following, far))
                return tuple(after)

            begin = []
            for c in range(band_count):
                turn0 = turned(c, 0)
                turn1 = turned(c, 1)
                begin.append((turn1, jnp.where(inside, turn0, turn1)))
            lax.fori_loop(0, quarter + 1, step, tuple(begin), unroll=11)

    def phase(turn, _):
        rows_now = lax.rem(turn + p // half, 2) == 0

        @pl.when(rows_now)
        def _():
            pl.when(low)(own_rows.wait)

            @pl.when(high)
            def _():
                rows_copy.wait_recv()
                head_copy.wait_recv()

            build_rows()

        @pl.when(jnp.logical_not(rows_now))
        def _():
            pl.when(low)(cols_copy.wait_recv)
            pl.when(high)(own_cols.wait)
            pl.when(next_taker)(next_copy.wait_recv)
            pl.when(p == blocks - 1)(own_tail.wait)
            build_cols()

        return 0

    lax.fori_loop(0, 2, phase, 0)

    last_block = lax.rem(p, half) + half
    room_all = (blocks - last_block) * block_rows * LANES - part * quarter * LANES
    lane_row = lax.broadcasted_iota(jnp.int32, (1, LANES), 1)

    lane_square = lax.broadcasted_iota(jnp.int32, square, 1)

    def score(index, state):
        pending, rows_found = state
        best = None
        left = []
        for c in range(band_count):
            both = jnp.concatenate([col_z[c, index], col_z[c, index + 1]], axis=1)
            found = jnp.dot(row_z[index], both, preferred_element_type=jnp.float32)
            room = room_all - starts[c] - index * LANES
            near = found[:, :LANES] + jnp.where(lane_row < room, 0.0, -4.0)
            far = found[:, LANES:] + jnp.where(lane_row + LANES < room, 0.0, -4.0)
            near_cols = jnp.max(jnp.where(keep, near, -4.0), axis=0, keepdims=True)
            far_cols = jnp.max(jnp.where(keep, -4.0, far), axis=0, keepdims=True)
            col_buf[c, pl.ds(quarter + index, 1), :] = jnp.maximum(
                jnp.maximum(pending[c], near_cols), -1.0
            )
            left.append(jnp.maximum(far_cols, -1.0))
            joined = jnp.where(keep, near, far)
            best = joined if best is None else jnp.maximum(best, joined)
        rows_found = jnp.where(
            lane_square == index, jnp.max(best, axis=1, keepdims=True), rows_found
        )
        return tuple(left), rows_found

    floor = jnp.full((1, LANES), -1.0, jnp.float32)
    pending, rows_found = lax.fori_loop(
        0, quarter, score, ((floor,) * band_count, jnp.full(square, -1.0, jnp.float32)), unroll=4
    )
    row_res[...] = jnp.maximum(rows_found.T[:quarter], -1.0)
    lane_wide = lax.broadcasted_iota(jnp.int32, (2 * quarter, LANES), 1)
    reached = None
    for c in range(band_count):
        col_buf[c, pl.ds(2 * quarter, 1), :] = pending[c]
        here = pltpu.roll(col_buf[c, pl.ds(quarter - whole[c], 2 * quarter), :], rest[c], 1)
        above = pltpu.roll(col_buf[c, pl.ds(quarter - whole[c] - 1, 2 * quarter), :], rest[c], 1)
        placed = jnp.where(lane_wide >= rest[c], here, above)
        reached = placed if reached is None else jnp.maximum(reached, placed)
    col_res[...] = reached

    place = pl.ds(pl.multiple_of(part * quarter, 8), quarter)
    row_to = [
        remote(row_res, row_out.at[place, :], out_send.at[k], row_recv.at[part], tm, band)
        for k, (tm, band) in enumerate([(p, 1 - b), (partner, 0), (partner, 1)])
    ]
    slot_to = [
        remote(col_res, slots.at[part], out_send.at[3 + k], slot_recv.at[part], tm, band)
        for k, (tm, band) in enumerate([(p, 1 - b), (partner, 0), (partner, 1)])
    ]
    lower = pl.ds(0, quarter)
    lower_to = remote(
        col_res.at[lower, :],
        slots.at[part, lower, :],
        out_send.at[3],
        slot_recv.at[part],
        p,
        1 - b,
    )
    carry_to = [
        remote(
            col_res.at[pl.ds(quarter, quarter), :],
            carry_in,
            out_send.at[6 + k],
            carry_recv.at[0],
            lax.rem(p + 1, blocks),
            k,
        )
        for k in range(2)
    ]

    @pl.when(low)
    def _():
        slot_to[1].start()
        slot_to[2].start()
        row_to[0].start()
        row_out[place, :] = row_res[...]

    @pl.when(high)
    def _():
        row_to[1].start()
        row_to[2].start()

    @pl.when(jnp.logical_and(high, b == 0))
    def _():
        slot_to[0].start()
        slots[2] = col_res[...]

    @pl.when(carry_sender)
    def _():
        carry_to[0].start()
        carry_to[1].start()

    @pl.when(jnp.logical_and(high, b == 1))
    def _():
        lower_to.start()
        slots[3, lower, :] = col_res[lower, :]

    def row_from(index):
        return remote(
            row_res,
            row_out.at[pl.ds(index * quarter, quarter), :],
            out_send.at[0],
            row_recv.at[index],
            p,
            1 - b,
        )

    def slot_from(index):
        return remote(
            col_res, slots.at[index], out_send.at[0], slot_recv.at[index], p, 1 - b
        )

    @pl.when(low)
    def _():
        pl.when(b == 1)(row_from(0).wait_recv)
        pl.when(b == 0)(row_from(1).wait_recv)
        row_from(2).wait_recv()
        row_from(3).wait_recv()

    @pl.when(high)
    def _():
        slot_from(0).wait_recv()
        slot_from(1).wait_recv()

    @pl.when(jnp.logical_and(high, b == 1))
    def _():
        slot_from(2).wait_recv()

    @pl.when(jnp.logical_and(high, b == 0))
    def _():
        remote(
            col_res.at[lower, :],
            slots.at[3, lower, :],
            out_send.at[0],
            slot_recv.at[3],
            p,
            1 - b,
        ).wait_recv()

    pl.when(carry_taker)(carry_to[0].wait_recv)

    @pl.when(p == half)
    def _():
        carry_in[...] = jnp.full(carry_in.shape, -1.0, jnp.float32)

    @pl.when(high)
    def _():
        col_out[pl.ds(0, quarter), :] = jnp.maximum(slots[0, lower, :], carry_in[...])
        for k in range(1, SLOTS):
            col_out[pl.ds(k * quarter, quarter), :] = jnp.maximum(
                slots[k, lower, :], slots[k - 1, pl.ds(quarter, quarter), :]
            )

    @pl.when(high)
    def _():
        cols_copy.wait_send()
        row_to[1].wait_send()
        row_to[2].wait_send()

    @pl.when(low)
    def _():
        rows_copy.wait_send()
        slot_to[1].wait_send()
        slot_to[2].wait_send()
        row_to[0].wait_send()

    pl.when(head_sender)(head_copy.wait_send)
    pl.when(next_sender)(next_copy.wait_send)
    pl.when(jnp.logical_and(high, b == 0))(slot_to[0].wait_send)
    pl.when(jnp.logical_and(high, b == 1))(lower_to.wait_send)

    @pl.when(carry_sender)
    def _():
        carry_to[0].wait_send()
        carry_to[1].wait_send()


def spread_body(series, tail, band_starts):
    block_rows = series.shape[0] // LANES
    quarter = block_rows // SLOTS
    band_count = band_starts.shape[0]
    blocks = lax.axis_size("tm")
    span = quarter + 8
    vmem = pl.BlockSpec(memory_space=pltpu.VMEM)
    whole = jax.ShapeDtypeStruct((block_rows, LANES), jnp.float32)

    operands = (band_starts, series.reshape(block_rows, LANES), tail.reshape(-1, LANES))

    def buffer(*shape, kind=jnp.float32):
        return pltpu.VMEM(shape, kind)

    best_rows, best_cols = pl.pallas_call(
        functools.partial(pair_kernel, blocks),
        out_shape=(whole, whole),
        in_specs=[pl.BlockSpec(memory_space=pltpu.HBM)] * 3,
        out_specs=(vmem, vmem),
        scratch_shapes=[
            pltpu.SMEM((band_count,), jnp.int32),
            buffer(block_rows + span, LANES),
            buffer(span, LANES),
            buffer(span, LANES),
            buffer(band_count, span, LANES),
            buffer(2 * band_count, span, LANES),
            buffer(2, LANES, quarter),
            buffer(quarter, LANES, M, kind=jnp.bfloat16),
            buffer(band_count, quarter + 1, M, LANES, kind=jnp.bfloat16),
            buffer(band_count, 3 * quarter + 8, LANES),
            buffer(quarter, LANES),
            buffer(2 * quarter, LANES),
            buffer(SLOTS, 2 * quarter, LANES),
            buffer(quarter, LANES),
            pltpu.SemaphoreType.DMA((3,)),
            pltpu.SemaphoreType.DMA((4,)),
            pltpu.SemaphoreType.DMA((4,)),
            pltpu.SemaphoreType.DMA((8,)),
            pltpu.SemaphoreType.DMA((SLOTS,)),
            pltpu.SemaphoreType.DMA((SLOTS,)),
            pltpu.SemaphoreType.DMA((1,)),
        ],
        compiler_params=pltpu.CompilerParams(
            collective_id=0, has_side_effects=True, vmem_limit_bytes=40 * 1024 * 1024
        ),
        name="banded_pairs",
    )(*[pltpu.with_memory_space_constraint(a, pltpu.HBM) for a in operands])
    return best_rows.reshape(-1), best_cols.reshape(-1)


def solution(mesh):
    placed = (P(("groups", "tm")), P("groups"), P("groups"))

    def chosen(series, tail, band_starts):
        halves = lax.axis_size("tm") == 2 * BAND_BLOCKS
        if halves and series.shape[0] == SLOTS * BAND_SPAN and lax.axis_size("band") == 2:
            return spread_body(series, tail, band_starts)
        return body(series, tail, band_starts)

    return jax.shard_map(
        chosen,
        mesh=mesh,
        in_specs=placed,
        out_specs=(P(("groups", "tm")), P(("groups", "tm"))),
        check_vma=False,
    )
```

```python
import functools

import jax
import jax.numpy as jnp
from jax import lax
from jax.experimental import pallas as pl
from jax.experimental.pallas import tpu as pltpu
from jax.sharding import PartitionSpec as P

M = 256
TILE = 128
OFF_DEV = 128
BAND_SPAN = 4096
BAND_BLOCKS = 4


EPS = 1e-06
tile_batch = 16


def from_behind(block, axis, distance):
    devices = range(lax.axis_size(axis))
    route = [(i - distance, i) for i in devices if i - distance in devices]
    return lax.ppermute(block, axis, route)


def hankel(samples, tile_count):
    length = tile_count * TILE + M
    shifted = jnp.stack(
        [lax.slice_in_dim(samples, offset, offset + length) for offset in range(TILE)]
    )
    blocks = shifted.reshape(TILE, length // TILE, TILE)
    joined = jnp.concatenate(
        [blocks[:, stride : stride + tile_count] for stride in range(M // TILE)], axis=2
    )
    return jnp.swapaxes(joined, 0, 1)


def moments(matrix):
    center = jnp.mean(matrix, axis=-1)
    spread = matrix - center[..., None]
    factor = lax.rsqrt(jnp.sum(spread * spread, axis=-1) + M * EPS)
    return (center, factor)


def normed(matrix, center, factor):
    return ((matrix - center[..., None]) * factor[..., None]).astype(jnp.bfloat16)


def score_group(row_z, col_z, room_left):
    tile_count = row_z.shape[0]
    near_scores = jnp.einsum("tim,tjm->tij", row_z, col_z[:-1], preferred_element_type=jnp.float32)
    far_scores = jnp.einsum(
        "tim,tjm->tij", row_z, col_z[1:, :OFF_DEV], preferred_element_type=jnp.float32
    )
    row_near = lax.broadcasted_iota(jnp.int32, (TILE, TILE), 0)
    col_near = lax.broadcasted_iota(jnp.int32, (TILE, TILE), 1)
    row_far = lax.broadcasted_iota(jnp.int32, (TILE, OFF_DEV), 0)
    col_far = lax.broadcasted_iota(jnp.int32, (TILE, OFF_DEV), 1)
    tile_index = jnp.arange(tile_count, dtype=jnp.int32)[:, None, None]
    keep_near = (
        (col_near >= row_near)[None]
        & (col_near - row_near < OFF_DEV)[None]
        & (tile_index * TILE + col_near[None] < room_left)
    )
    keep_far = (TILE + col_far - row_far < OFF_DEV)[None] & (
        (tile_index + 1) * TILE + col_far[None] < room_left
    )
    near_scores = jnp.where(keep_near, near_scores, -1.0)
    far_scores = jnp.where(keep_far, far_scores, -1.0)
    best_rows = jnp.maximum(near_scores.max(axis=2), far_scores.max(axis=2)).reshape(-1)
    floor_row = jnp.full((1, TILE), -1.0, jnp.float32)
    upper_part = jnp.concatenate([near_scores.max(axis=1), floor_row], axis=0)
    far_cols = far_scores.max(axis=1)
    lower_part = jnp.concatenate([floor_row, far_cols], axis=0)
    return (best_rows, jnp.maximum(upper_part, lower_part).reshape(-1))


def place_columns(col_groups, start, buffer_len):
    group_rows = tile_batch * TILE
    count = col_groups.shape[0]
    main_part = col_groups[:, :group_rows].reshape(-1)
    carry_part = jnp.concatenate(
        [col_groups[:, group_rows:], jnp.full((count, group_rows - TILE), -1.0, jnp.float32)],
        axis=1,
    ).reshape(-1)
    shifted = jnp.concatenate([jnp.full((group_rows,), -1.0, jnp.float32), carry_part])[
        : count * group_rows + TILE
    ]
    reached = jnp.maximum(
        jnp.concatenate([main_part, jnp.full((TILE,), -1.0, jnp.float32)]), shifted
    )
    buffer_all = jnp.full((buffer_len,), -1.0, jnp.float32)
    return lax.dynamic_update_slice(buffer_all, reached, (start,))


def body(series, tail, band_starts):
    block_len = series.shape[0]
    group_rows = tile_batch * TILE
    group_count = block_len // group_rows
    position = lax.axis_index("tm")
    devices = lax.axis_size("tm")
    distance = BAND_BLOCKS
    following = from_behind(series[:M], "tm", -1)
    following = jnp.where(position == devices - 1, tail, following)
    extended = jnp.concatenate([series, following])
    row_source = jnp.concatenate([extended, jnp.zeros((TILE,), jnp.float32)])

    def own_group(group_index):
        row_piece = lax.dynamic_slice_in_dim(
            row_source, group_index * group_rows, group_rows + M + TILE
        )
        matrix = hankel(row_piece, tile_batch)
        center, factor = moments(matrix)
        return (center.reshape(-1), factor.reshape(-1), normed(matrix, center, factor))

    centers, factors, row_z = lax.map(own_group, jnp.arange(group_count, dtype=jnp.int32))
    centers = centers.reshape(block_len)
    factors = factors.reshape(block_len)
    padding = jnp.zeros((2 * TILE,), jnp.float32)
    far_samples = from_behind(extended, "tm", -distance)
    next_samples = from_behind(series[M : M + BAND_SPAN], "tm", -distance - 1)
    pair_samples = jnp.concatenate([far_samples, next_samples, padding])
    buffer_len = block_len + BAND_SPAN + TILE
    band_count = band_starts.shape[0]
    band_here = lax.axis_index("band")
    offset_start = jnp.sum(
        jnp.where(jnp.arange(band_count, dtype=jnp.int32) == band_here, band_starts, 0)
    )
    room_all = (devices - position - distance) * block_len - offset_start

    def pair_group(inputs):
        group_index, group_z = inputs
        col_begin = offset_start + group_index * group_rows
        col_piece = lax.dynamic_slice_in_dim(pair_samples, col_begin, (tile_batch + 2) * TILE + M)
        matrix = hankel(col_piece, tile_batch + 1)
        center, factor = moments(matrix)
        col_z = normed(matrix, center, factor)
        return score_group(group_z, col_z, room_all - group_index * group_rows)

    row_best, col_groups = lax.map(pair_group, (jnp.arange(group_count, dtype=jnp.int32), row_z))
    lifted = place_columns(col_groups, offset_start, buffer_len) + 1.0
    returned = from_behind(lifted[:block_len], "tm", distance)
    returned_head = from_behind(lifted[block_len : block_len + BAND_SPAN], "tm", distance + 1)
    col_best = (
        jnp.maximum(
            returned,
            jnp.concatenate([returned_head, jnp.zeros((block_len - BAND_SPAN,), jnp.float32)]),
        )
        - 1.0
    )
    return lax.pmax((row_best.reshape(block_len), col_best), "band")


SLOTS = 4
LANES = 128


def pair_kernel(
    blocks,
    starts_in,
    x_ref,
    tail_ref,
    row_out,
    col_out,
    starts_ref,
    ext,
    rows_x,
    rows_back,
    shifted,
    stats,
    across,
    row_z,
    col_z,
    col_buf,
    row_res,
    col_res,
    slots,
    carry_in,
    local,
    in_send,
    in_recv,
    out_send,
    row_recv,
    slot_recv,
    carry_recv,
):
    half = BAND_BLOCKS
    block_rows = x_ref.shape[0]
    quarter = block_rows // SLOTS
    piece = 2 * quarter + 8
    band_count = starts_ref.shape[0]
    p = lax.axis_index("tm")
    b = lax.axis_index("band")
    low = p < half
    high = p >= half
    partner = lax.rem(p + half, blocks)
    part = b + 2 * (p // half)
    first = 2 * quarter + quarter * b

    def remote(src, dst, send, recv, tm, band):
        return pltpu.make_async_remote_copy(
            src_ref=src,
            dst_ref=dst,
            send_sem=send,
            recv_sem=recv,
            device_id={"tm": tm, "band": band},
            device_id_type=pl.DeviceIdType.MESH,
        )

    head_sender = jnp.logical_and(p >= b, p < half + b)
    next_sender = p > half
    next_taker = jnp.logical_and(high, p < blocks - 1)
    carry_sender = jnp.logical_and(next_taker, b == 1)
    carry_taker = next_sender

    barrier = pltpu.get_barrier_semaphore()

    def greet(tm, band):
        pl.semaphore_signal(
            barrier, 1, device_id={"tm": tm, "band": band}, device_id_type=pl.DeviceIdType.MESH
        )

    greet(p, 1 - b)
    greet(partner, 0)
    greet(partner, 1)

    @pl.when(jnp.logical_and(high, b == 1))
    def _():
        greet(p - half + 1, 1)

    @pl.when(next_taker)
    def _():
        greet(p + 1, b)

    @pl.when(carry_taker)
    def _():
        greet(p - 1, 1)

    starts_copy = pltpu.make_async_copy(starts_in, starts_ref, local.at[0])
    own_rows = pltpu.make_async_copy(
        x_ref.at[pl.ds(pl.multiple_of(quarter * b, 8), quarter + 8), :], rows_x, local.at[1]
    )
    own_cols = pltpu.make_async_copy(
        x_ref.at[pl.ds(2 * quarter, 2 * quarter), :],
        ext.at[pl.ds(2 * quarter, 2 * quarter), :],
        local.at[1],
    )
    own_tail = pltpu.make_async_copy(
        tail_ref, ext.at[pl.ds(block_rows, M // LANES), :], local.at[2]
    )
    starts_copy.start()
    pl.when(low)(own_rows.start)
    pl.when(high)(own_cols.start)

    @pl.when(p == blocks - 1)
    def _():
        ext[pl.ds(block_rows, quarter + 8), :] = jnp.zeros((quarter + 8, LANES), jnp.float32)
        own_tail.start()

    col_buf[...] = jnp.full(col_buf.shape, -1.0, jnp.float32)

    @pl.when(low)
    def _():
        col_out[...] = jnp.full(col_out.shape, -1.0, jnp.float32)

    @pl.when(high)
    def _():
        row_out[...] = jnp.full(row_out.shape, -1.0, jnp.float32)

    head_here = jnp.where(jnp.logical_and(b == 1, jnp.logical_and(p >= 1, p <= half)), 1, 0)
    next_here = jnp.where(next_sender, 1, 0)
    carry_here = jnp.where(carry_sender, 2, 0)
    pl.semaphore_wait(barrier, 3 + head_here + next_here + carry_here)

    cols_copy = remote(
        x_ref.at[pl.ds(pl.multiple_of(quarter * b, 8), piece), :],
        ext.at[pl.ds(pl.multiple_of(first, 8), piece), :],
        in_send.at[0],
        in_recv.at[0],
        partner,
        b,
    )
    rows_copy = remote(
        x_ref.at[pl.ds(pl.multiple_of(first, 8), quarter), :],
        rows_x.at[pl.ds(0, quarter), :],
        in_send.at[1],
        in_recv.at[1],
        partner,
        b,
    )
    head_copy = remote(
        x_ref.at[pl.ds(pl.multiple_of(3 * quarter * (1 - b), 8), 8), :],
        rows_x.at[pl.ds(quarter, 8), :],
        in_send.at[2],
        in_recv.at[2],
        lax.rem(p + half - b, blocks),
        b,
    )
    next_copy = remote(
        x_ref.at[pl.ds(0, quarter + 8), :],
        ext.at[pl.ds(block_rows, quarter + 8), :],
        in_send.at[3],
        in_recv.at[3],
        lax.rem(p + blocks - 1, blocks),
        b,
    )
    pl.when(high)(cols_copy.start)
    pl.when(low)(rows_copy.start)
    pl.when(head_sender)(head_copy.start)
    pl.when(next_sender)(next_copy.start)

    starts_copy.wait()
    span = quarter + 8
    lane = lax.broadcasted_iota(jnp.int32, (span, LANES), 1)

    def moments_of(samples):
        mean, spread = samples, None
        width = 1

        def ahead(values):
            below = pltpu.roll(values, span - 1, 0)
            if width == LANES:
                return below
            turned = pltpu.roll(values, LANES - width, 1)
            return jnp.where(lane < LANES - width, turned, pltpu.roll(turned, span - 1, 0))

        while width < M:
            other = ahead(mean)
            gap = mean - other
            term = gap * gap * (0.5 * width)
            spread = term if spread is None else spread + ahead(spread) + term
            mean = 0.5 * (mean + other)
            width *= 2
        return mean, lax.rsqrt(spread + M * EPS)

    square = (LANES, LANES)
    upper = lax.broadcasted_iota(jnp.int32, square, 1) <= lax.broadcasted_iota(jnp.int32, square, 0)
    keep = lax.broadcasted_iota(jnp.int32, square, 1) >= lax.broadcasted_iota(jnp.int32, square, 0)

    def turned_row(source, index):
        line = source[pl.ds(index, 1), :]
        return pltpu.roll(jnp.broadcast_to(line, square), 1, 1, stride=1, stride_axis=0)

    lane_quarter = lax.broadcasted_iota(jnp.int32, (LANES, quarter), 1)

    def build_rows():
        samples = rows_x[...]
        mean, factor = moments_of(samples)
        across[0] = mean[:quarter].T
        across[1] = factor[:quarter].T
        flip = jnp.where(
            lax.broadcasted_iota(jnp.int32, square, 0) + lax.broadcasted_iota(jnp.int32, square, 1)
            == LANES - 1,
            1.0,
            0.0,
        ).astype(jnp.bfloat16)
        left = samples
        back = None
        for _ in range(3):
            some = left.astype(jnp.bfloat16)
            left = left - some.astype(jnp.float32)
            moved = jnp.dot(some, flip, preferred_element_type=jnp.float32)
            back = moved if back is None else back + moved
        rows_back[...] = back

        def turned(index):
            line = rows_back[pl.ds(index, 1), :]
            return pltpu.roll(jnp.broadcast_to(line, square), 0, 1, stride=1, stride_axis=0)

        def column(which, index):
            return jnp.sum(
                jnp.where(lane_quarter == index, across[which], 0.0), axis=1, keepdims=True
            )

        turn0 = turned(0)
        turn1 = turned(1)

        def step(index, state):
            turn, near = state
            following = turned(index + 2)
            far = jnp.where(keep, turn, following)
            c = column(0, index)
            f = column(1, index)
            row_z[index, :, :LANES] = ((near - c) * f).astype(jnp.bfloat16)
            row_z[index, :, LANES:] = ((far - c) * f).astype(jnp.bfloat16)
            return following, far

        lax.fori_loop(0, quarter, step, (turn1, jnp.where(keep, turn0, turn1)), unroll=8)

    starts = [starts_ref[c] for c in range(band_count)]
    whole = [lax.shift_right_logical(s, 7) for s in starts]
    rest = [lax.bitwise_and(s, LANES - 1) for s in starts]

    def build_cols():
        for c in range(band_count):
            back = lax.rem(LANES - rest[c], LANES)
            here = pltpu.roll(ext[pl.ds(first + whole[c], span), :], back, 1)
            below = pltpu.roll(ext[pl.ds(first + whole[c] + 1, span), :], back, 1)
            samples = jnp.where(lane < LANES - rest[c], here, below)
            shifted[c] = samples
            mean, factor = moments_of(samples)
            stats[2 * c] = mean
            stats[2 * c + 1] = factor

        def turned(c, index):
            line = shifted[c, pl.ds(index, 1), :]
            return pltpu.roll(jnp.broadcast_to(line, square), 1, 1, stride=1, stride_axis=0)

        def one_band(c, _):
            turn0 = turned(c, 0)
            turn1 = turned(c, 1)

            def step(index, state):
                turn, near = state
                following = turned(c, index + 2)
                far = jnp.where(upper, turn, following)
                center = stats[2 * c, pl.ds(index, 1), :]
                factor = stats[2 * c + 1, pl.ds(index, 1), :]
                col_z[c, index, :LANES, :] = ((near - center) * factor).astype(jnp.bfloat16)
                col_z[c, index, LANES:, :] = ((far - center) * factor).astype(jnp.bfloat16)
                return following, far

            lax.fori_loop(
                0, quarter + 1, step, (turn1, jnp.where(upper, turn0, turn1)), unroll=11
            )
            return 0

        lax.fori_loop(0, band_count, one_band, 0)

    def phase(turn, _):
        rows_now = lax.rem(turn + p // half, 2) == 0

        @pl.when(rows_now)
        def _():
            pl.when(low)(own_rows.wait)

            @pl.when(high)
            def _():
                rows_copy.wait_recv()
                head_copy.wait_recv()

            build_rows()

        @pl.when(jnp.logical_not(rows_now))
        def _():
            pl.when(low)(cols_copy.wait_recv)
            pl.when(high)(own_cols.wait)
            pl.when(next_taker)(next_copy.wait_recv)
            pl.when(p == blocks - 1)(own_tail.wait)
            build_cols()

        return 0

    lax.fori_loop(0, 2, phase, 0)

    last_block = lax.rem(p, half) + half
    room_all = (blocks - last_block) * block_rows * LANES - part * quarter * LANES
    lane_row = lax.broadcasted_iota(jnp.int32, (1, LANES), 1)

    lane_square = lax.broadcasted_iota(jnp.int32, square, 1)

    def score(index, state):
        pending, rows_found = state
        best = None
        left = []
        for c in range(band_count):
            both = jnp.concatenate([col_z[c, index], col_z[c, index + 1]], axis=1)
            found = jnp.dot(row_z[index], both, preferred_element_type=jnp.float32)
            room = room_all - starts[c] - index * LANES
            near = found[:, :LANES] + jnp.where(lane_row < room, 0.0, -4.0)
            far = found[:, LANES:] + jnp.where(lane_row + LANES < room, 0.0, -4.0)
            near_cols = jnp.max(jnp.where(keep, near, -4.0), axis=0, keepdims=True)
            far_cols = jnp.max(jnp.where(keep, -4.0, far), axis=0, keepdims=True)
            col_buf[c, pl.ds(quarter + index, 1), :] = jnp.maximum(
                jnp.maximum(pending[c], near_cols), -1.0
            )
            left.append(jnp.maximum(far_cols, -1.0))
            joined = jnp.where(keep, near, far)
            best = joined if best is None else jnp.maximum(best, joined)
        rows_found = jnp.where(
            lane_square == index, jnp.max(best, axis=1, keepdims=True), rows_found
        )
        return tuple(left), rows_found

    floor = jnp.full((1, LANES), -1.0, jnp.float32)
    pending, rows_found = lax.fori_loop(
        0, quarter, score, ((floor,) * band_count, jnp.full(square, -1.0, jnp.float32)), unroll=8
    )
    row_res[...] = jnp.maximum(rows_found.T[:quarter], -1.0)
    lane_wide = lax.broadcasted_iota(jnp.int32, (2 * quarter, LANES), 1)
    reached = None
    for c in range(band_count):
        col_buf[c, pl.ds(2 * quarter, 1), :] = pending[c]
        here = pltpu.roll(col_buf[c, pl.ds(quarter - whole[c], 2 * quarter), :], rest[c], 1)
        above = pltpu.roll(col_buf[c, pl.ds(quarter - whole[c] - 1, 2 * quarter), :], rest[c], 1)
        placed = jnp.where(lane_wide >= rest[c], here, above)
        reached = placed if reached is None else jnp.maximum(reached, placed)
    col_res[...] = reached

    place = pl.ds(pl.multiple_of(part * quarter, 8), quarter)
    row_to = [
        remote(row_res, row_out.at[place, :], out_send.at[k], row_recv.at[part], tm, band)
        for k, (tm, band) in enumerate([(p, 1 - b), (partner, 0), (partner, 1)])
    ]
    slot_to = [
        remote(col_res, slots.at[part], out_send.at[3 + k], slot_recv.at[part], tm, band)
        for k, (tm, band) in enumerate([(p, 1 - b), (partner, 0), (partner, 1)])
    ]
    lower = pl.ds(0, quarter)
    lower_to = remote(
        col_res.at[lower, :],
        slots.at[part, lower, :],
        out_send.at[3],
        slot_recv.at[part],
        p,
        1 - b,
    )
    carry_to = [
        remote(
            col_res.at[pl.ds(quarter, quarter), :],
            carry_in,
            out_send.at[6 + k],
            carry_recv.at[0],
            lax.rem(p + 1, blocks),
            k,
        )
        for k in range(2)
    ]

    @pl.when(low)
    def _():
        slot_to[1].start()
        slot_to[2].start()
        row_to[0].start()
        row_out[place, :] = row_res[...]

    @pl.when(high)
    def _():
        row_to[1].start()
        row_to[2].start()

    @pl.when(jnp.logical_and(high, b == 0))
    def _():
        slot_to[0].start()
        slots[2] = col_res[...]

    @pl.when(carry_sender)
    def _():
        carry_to[0].start()
        carry_to[1].start()

    @pl.when(jnp.logical_and(high, b == 1))
    def _():
        lower_to.start()
        slots[3, lower, :] = col_res[lower, :]

    def row_from(index):
        return remote(
            row_res,
            row_out.at[pl.ds(index * quarter, quarter), :],
            out_send.at[0],
            row_recv.at[index],
            p,
            1 - b,
        )

    def slot_from(index):
        return remote(
            col_res, slots.at[index], out_send.at[0], slot_recv.at[index], p, 1 - b
        )

    @pl.when(low)
    def _():
        pl.when(b == 1)(row_from(0).wait_recv)
        pl.when(b == 0)(row_from(1).wait_recv)
        row_from(2).wait_recv()
        row_from(3).wait_recv()

    @pl.when(high)
    def _():
        slot_from(0).wait_recv()
        slot_from(1).wait_recv()

    @pl.when(jnp.logical_and(high, b == 1))
    def _():
        slot_from(2).wait_recv()

    @pl.when(jnp.logical_and(high, b == 0))
    def _():
        remote(
            col_res.at[lower, :],
            slots.at[3, lower, :],
            out_send.at[0],
            slot_recv.at[3],
            p,
            1 - b,
        ).wait_recv()

    pl.when(carry_taker)(carry_to[0].wait_recv)

    @pl.when(p == half)
    def _():
        carry_in[...] = jnp.full(carry_in.shape, -1.0, jnp.float32)

    @pl.when(high)
    def _():
        col_out[pl.ds(0, quarter), :] = jnp.maximum(slots[0, lower, :], carry_in[...])
        for k in range(1, SLOTS):
            col_out[pl.ds(k * quarter, quarter), :] = jnp.maximum(
                slots[k, lower, :], slots[k - 1, pl.ds(quarter, quarter), :]
            )

    @pl.when(high)
    def _():
        cols_copy.wait_send()
        row_to[1].wait_send()
        row_to[2].wait_send()

    @pl.when(low)
    def _():
        rows_copy.wait_send()
        slot_to[1].wait_send()
        slot_to[2].wait_send()
        row_to[0].wait_send()

    pl.when(head_sender)(head_copy.wait_send)
    pl.when(next_sender)(next_copy.wait_send)
    pl.when(jnp.logical_and(high, b == 0))(slot_to[0].wait_send)
    pl.when(jnp.logical_and(high, b == 1))(lower_to.wait_send)

    @pl.when(carry_sender)
    def _():
        carry_to[0].wait_send()
        carry_to[1].wait_send()


def spread_body(series, tail, band_starts):
    block_rows = series.shape[0] // LANES
    quarter = block_rows // SLOTS
    band_count = band_starts.shape[0]
    blocks = lax.axis_size("tm")
    span = quarter + 8
    vmem = pl.BlockSpec(memory_space=pltpu.VMEM)
    whole = jax.ShapeDtypeStruct((block_rows, LANES), jnp.float32)

    operands = (band_starts, series.reshape(block_rows, LANES), tail.reshape(-1, LANES))

    def buffer(*shape, kind=jnp.float32):
        return pltpu.VMEM(shape, kind)

    best_rows, best_cols = pl.pallas_call(
        functools.partial(pair_kernel, blocks),
        out_shape=(whole, whole),
        in_specs=[pl.BlockSpec(memory_space=pltpu.HBM)] * 3,
        out_specs=(vmem, vmem),
        scratch_shapes=[
            pltpu.SMEM((band_count,), jnp.int32),
            buffer(block_rows + span, LANES),
            buffer(span, LANES),
            buffer(span, LANES),
            buffer(band_count, span, LANES),
            buffer(2 * band_count, span, LANES),
            buffer(2, LANES, quarter),
            buffer(quarter, LANES, M, kind=jnp.bfloat16),
            buffer(band_count, quarter + 1, M, LANES, kind=jnp.bfloat16),
            buffer(band_count, 3 * quarter + 8, LANES),
            buffer(quarter, LANES),
            buffer(2 * quarter, LANES),
            buffer(SLOTS, 2 * quarter, LANES),
            buffer(quarter, LANES),
            pltpu.SemaphoreType.DMA((3,)),
            pltpu.SemaphoreType.DMA((4,)),
            pltpu.SemaphoreType.DMA((4,)),
            pltpu.SemaphoreType.DMA((8,)),
            pltpu.SemaphoreType.DMA((SLOTS,)),
            pltpu.SemaphoreType.DMA((SLOTS,)),
            pltpu.SemaphoreType.DMA((1,)),
        ],
        compiler_params=pltpu.CompilerParams(
            collective_id=0, has_side_effects=True, vmem_limit_bytes=40 * 1024 * 1024
        ),
        name="banded_pairs",
    )(*[pltpu.with_memory_space_constraint(a, pltpu.HBM) for a in operands])
    return best_rows.reshape(-1), best_cols.reshape(-1)


def solution(mesh):
    placed = (P(("groups", "tm")), P("groups"), P("groups"))

    def chosen(series, tail, band_starts):
        halves = lax.axis_size("tm") == 2 * BAND_BLOCKS
        if halves and series.shape[0] == SLOTS * BAND_SPAN and lax.axis_size("band") == 2:
            return spread_body(series, tail, band_starts)
        return body(series, tail, band_starts)

    return jax.shard_map(
        chosen,
        mesh=mesh,
        in_specs=placed,
        out_specs=(P(("groups", "tm")), P(("groups", "tm"))),
        check_vma=False,
    )
```

```python
import functools

import jax
import jax.numpy as jnp
from jax import lax
from jax.experimental import pallas as pl
from jax.experimental.pallas import tpu as pltpu
from jax.sharding import PartitionSpec as P

M = 256
TILE = 128
OFF_DEV = 128
BAND_SPAN = 4096
BAND_BLOCKS = 4


EPS = 1e-06
tile_batch = 16


def from_behind(block, axis, distance):
    devices = range(lax.axis_size(axis))
    route = [(i - distance, i) for i in devices if i - distance in devices]
    return lax.ppermute(block, axis, route)


def hankel(samples, tile_count):
    length = tile_count * TILE + M
    shifted = jnp.stack(
        [lax.slice_in_dim(samples, offset, offset + length) for offset in range(TILE)]
    )
    blocks = shifted.reshape(TILE, length // TILE, TILE)
    joined = jnp.concatenate(
        [blocks[:, stride : stride + tile_count] for stride in range(M // TILE)], axis=2
    )
    return jnp.swapaxes(joined, 0, 1)


def moments(matrix):
    center = jnp.mean(matrix, axis=-1)
    spread = matrix - center[..., None]
    factor = lax.rsqrt(jnp.sum(spread * spread, axis=-1) + M * EPS)
    return (center, factor)


def normed(matrix, center, factor):
    return ((matrix - center[..., None]) * factor[..., None]).astype(jnp.bfloat16)


def score_group(row_z, col_z, room_left):
    tile_count = row_z.shape[0]
    near_scores = jnp.einsum("tim,tjm->tij", row_z, col_z[:-1], preferred_element_type=jnp.float32)
    far_scores = jnp.einsum(
        "tim,tjm->tij", row_z, col_z[1:, :OFF_DEV], preferred_element_type=jnp.float32
    )
    row_near = lax.broadcasted_iota(jnp.int32, (TILE, TILE), 0)
    col_near = lax.broadcasted_iota(jnp.int32, (TILE, TILE), 1)
    row_far = lax.broadcasted_iota(jnp.int32, (TILE, OFF_DEV), 0)
    col_far = lax.broadcasted_iota(jnp.int32, (TILE, OFF_DEV), 1)
    tile_index = jnp.arange(tile_count, dtype=jnp.int32)[:, None, None]
    keep_near = (
        (col_near >= row_near)[None]
        & (col_near - row_near < OFF_DEV)[None]
        & (tile_index * TILE + col_near[None] < room_left)
    )
    keep_far = (TILE + col_far - row_far < OFF_DEV)[None] & (
        (tile_index + 1) * TILE + col_far[None] < room_left
    )
    near_scores = jnp.where(keep_near, near_scores, -1.0)
    far_scores = jnp.where(keep_far, far_scores, -1.0)
    best_rows = jnp.maximum(near_scores.max(axis=2), far_scores.max(axis=2)).reshape(-1)
    floor_row = jnp.full((1, TILE), -1.0, jnp.float32)
    upper_part = jnp.concatenate([near_scores.max(axis=1), floor_row], axis=0)
    far_cols = far_scores.max(axis=1)
    lower_part = jnp.concatenate([floor_row, far_cols], axis=0)
    return (best_rows, jnp.maximum(upper_part, lower_part).reshape(-1))


def place_columns(col_groups, start, buffer_len):
    group_rows = tile_batch * TILE
    count = col_groups.shape[0]
    main_part = col_groups[:, :group_rows].reshape(-1)
    carry_part = jnp.concatenate(
        [col_groups[:, group_rows:], jnp.full((count, group_rows - TILE), -1.0, jnp.float32)],
        axis=1,
    ).reshape(-1)
    shifted = jnp.concatenate([jnp.full((group_rows,), -1.0, jnp.float32), carry_part])[
        : count * group_rows + TILE
    ]
    reached = jnp.maximum(
        jnp.concatenate([main_part, jnp.full((TILE,), -1.0, jnp.float32)]), shifted
    )
    buffer_all = jnp.full((buffer_len,), -1.0, jnp.float32)
    return lax.dynamic_update_slice(buffer_all, reached, (start,))


def body(series, tail, band_starts):
    block_len = series.shape[0]
    group_rows = tile_batch * TILE
    group_count = block_len // group_rows
    position = lax.axis_index("tm")
    devices = lax.axis_size("tm")
    distance = BAND_BLOCKS
    following = from_behind(series[:M], "tm", -1)
    following = jnp.where(position == devices - 1, tail, following)
    extended = jnp.concatenate([series, following])
    row_source = jnp.concatenate([extended, jnp.zeros((TILE,), jnp.float32)])

    def own_group(group_index):
        row_piece = lax.dynamic_slice_in_dim(
            row_source, group_index * group_rows, group_rows + M + TILE
        )
        matrix = hankel(row_piece, tile_batch)
        center, factor = moments(matrix)
        return (center.reshape(-1), factor.reshape(-1), normed(matrix, center, factor))

    centers, factors, row_z = lax.map(own_group, jnp.arange(group_count, dtype=jnp.int32))
    centers = centers.reshape(block_len)
    factors = factors.reshape(block_len)
    padding = jnp.zeros((2 * TILE,), jnp.float32)
    far_samples = from_behind(extended, "tm", -distance)
    next_samples = from_behind(series[M : M + BAND_SPAN], "tm", -distance - 1)
    pair_samples = jnp.concatenate([far_samples, next_samples, padding])
    buffer_len = block_len + BAND_SPAN + TILE
    band_count = band_starts.shape[0]
    band_here = lax.axis_index("band")
    offset_start = jnp.sum(
        jnp.where(jnp.arange(band_count, dtype=jnp.int32) == band_here, band_starts, 0)
    )
    room_all = (devices - position - distance) * block_len - offset_start

    def pair_group(inputs):
        group_index, group_z = inputs
        col_begin = offset_start + group_index * group_rows
        col_piece = lax.dynamic_slice_in_dim(pair_samples, col_begin, (tile_batch + 2) * TILE + M)
        matrix = hankel(col_piece, tile_batch + 1)
        center, factor = moments(matrix)
        col_z = normed(matrix, center, factor)
        return score_group(group_z, col_z, room_all - group_index * group_rows)

    row_best, col_groups = lax.map(pair_group, (jnp.arange(group_count, dtype=jnp.int32), row_z))
    lifted = place_columns(col_groups, offset_start, buffer_len) + 1.0
    returned = from_behind(lifted[:block_len], "tm", distance)
    returned_head = from_behind(lifted[block_len : block_len + BAND_SPAN], "tm", distance + 1)
    col_best = (
        jnp.maximum(
            returned,
            jnp.concatenate([returned_head, jnp.zeros((block_len - BAND_SPAN,), jnp.float32)]),
        )
        - 1.0
    )
    return lax.pmax((row_best.reshape(block_len), col_best), "band")


SLOTS = 4
LANES = 128


def pair_kernel(
    blocks,
    starts_in,
    x_ref,
    tail_ref,
    row_out,
    col_out,
    starts_ref,
    ext,
    rows_x,
    rows_back,
    shifted,
    stats,
    across,
    row_z,
    col_z,
    col_buf,
    row_res,
    col_res,
    slots,
    carry_in,
    local,
    in_send,
    in_recv,
    out_send,
    row_recv,
    slot_recv,
    carry_recv,
):
    half = BAND_BLOCKS
    block_rows = x_ref.shape[0]
    quarter = block_rows // SLOTS
    piece = 2 * quarter + 8
    band_count = starts_ref.shape[0]
    p = lax.axis_index("tm")
    b = lax.axis_index("band")
    low = p < half
    high = p >= half
    partner = lax.rem(p + half, blocks)
    part = b + 2 * (p // half)
    first = 2 * quarter + quarter * b

    def remote(src, dst, send, recv, tm, band):
        return pltpu.make_async_remote_copy(
            src_ref=src,
            dst_ref=dst,
            send_sem=send,
            recv_sem=recv,
            device_id={"tm": tm, "band": band},
            device_id_type=pl.DeviceIdType.MESH,
        )

    head_sender = jnp.logical_and(p >= b, p < half + b)
    next_sender = p > half
    next_taker = jnp.logical_and(high, p < blocks - 1)
    carry_sender = jnp.logical_and(next_taker, b == 1)
    carry_taker = next_sender

    barrier = pltpu.get_barrier_semaphore()

    def greet(tm, band):
        pl.semaphore_signal(
            barrier, 1, device_id={"tm": tm, "band": band}, device_id_type=pl.DeviceIdType.MESH
        )

    greet(p, 1 - b)
    greet(partner, 0)
    greet(partner, 1)

    @pl.when(jnp.logical_and(high, b == 1))
    def _():
        greet(p - half + 1, 1)

    @pl.when(next_taker)
    def _():
        greet(p + 1, b)

    @pl.when(carry_taker)
    def _():
        greet(p - 1, 1)

    starts_copy = pltpu.make_async_copy(starts_in, starts_ref, local.at[0])
    own_rows = pltpu.make_async_copy(
        x_ref.at[pl.ds(pl.multiple_of(quarter * b, 8), quarter + 8), :], rows_x, local.at[1]
    )
    own_cols = pltpu.make_async_copy(
        x_ref.at[pl.ds(2 * quarter, 2 * quarter), :],
        ext.at[pl.ds(2 * quarter, 2 * quarter), :],
        local.at[1],
    )
    own_tail = pltpu.make_async_copy(
        tail_ref, ext.at[pl.ds(block_rows, M // LANES), :], local.at[2]
    )
    starts_copy.start()
    pl.when(low)(own_rows.start)
    pl.when(high)(own_cols.start)

    @pl.when(p == blocks - 1)
    def _():
        ext[pl.ds(block_rows, quarter + 8), :] = jnp.zeros((quarter + 8, LANES), jnp.float32)
        own_tail.start()

    col_buf[...] = jnp.full(col_buf.shape, -1.0, jnp.float32)

    @pl.when(low)
    def _():
        col_out[...] = jnp.full(col_out.shape, -1.0, jnp.float32)

    @pl.when(high)
    def _():
        row_out[...] = jnp.full(row_out.shape, -1.0, jnp.float32)

    head_here = jnp.where(jnp.logical_and(b == 1, jnp.logical_and(p >= 1, p <= half)), 1, 0)
    next_here = jnp.where(next_sender, 1, 0)
    carry_here = jnp.where(carry_sender, 2, 0)
    pl.semaphore_wait(barrier, 3 + head_here + next_here + carry_here)

    cols_copy = remote(
        x_ref.at[pl.ds(pl.multiple_of(quarter * b, 8), piece), :],
        ext.at[pl.ds(pl.multiple_of(first, 8), piece), :],
        in_send.at[0],
        in_recv.at[0],
        partner,
        b,
    )
    rows_copy = remote(
        x_ref.at[pl.ds(pl.multiple_of(first, 8), quarter), :],
        rows_x.at[pl.ds(0, quarter), :],
        in_send.at[1],
        in_recv.at[1],
        partner,
        b,
    )
    head_copy = remote(
        x_ref.at[pl.ds(pl.multiple_of(3 * quarter * (1 - b), 8), 8), :],
        rows_x.at[pl.ds(quarter, 8), :],
        in_send.at[2],
        in_recv.at[2],
        lax.rem(p + half - b, blocks),
        b,
    )
    next_copy = remote(
        x_ref.at[pl.ds(0, quarter + 8), :],
        ext.at[pl.ds(block_rows, quarter + 8), :],
        in_send.at[3],
        in_recv.at[3],
        lax.rem(p + blocks - 1, blocks),
        b,
    )
    pl.when(high)(cols_copy.start)
    pl.when(low)(rows_copy.start)
    pl.when(head_sender)(head_copy.start)
    pl.when(next_sender)(next_copy.start)

    starts_copy.wait()
    span = quarter + 8
    lane = lax.broadcasted_iota(jnp.int32, (span, LANES), 1)

    def moments_of(samples):
        mean, spread = samples, None
        width = 1

        def ahead(values):
            below = pltpu.roll(values, span - 1, 0)
            if width == LANES:
                return below
            turned = pltpu.roll(values, LANES - width, 1)
            return jnp.where(lane < LANES - width, turned, pltpu.roll(turned, span - 1, 0))

        while width < M:
            other = ahead(mean)
            gap = mean - other
            term = gap * gap * (0.5 * width)
            spread = term if spread is None else spread + ahead(spread) + term
            mean = 0.5 * (mean + other)
            width *= 2
        return mean, lax.rsqrt(spread + M * EPS)

    square = (LANES, LANES)
    upper = lax.broadcasted_iota(jnp.int32, square, 1) <= lax.broadcasted_iota(jnp.int32, square, 0)
    keep = lax.broadcasted_iota(jnp.int32, square, 1) >= lax.broadcasted_iota(jnp.int32, square, 0)

    def turned_row(source, index):
        line = source[pl.ds(index, 1), :]
        return pltpu.roll(jnp.broadcast_to(line, square), 1, 1, stride=1, stride_axis=0)

    lane_quarter = lax.broadcasted_iota(jnp.int32, (LANES, quarter), 1)

    def build_rows():
        samples = rows_x[...]
        mean, factor = moments_of(samples)
        across[0] = mean[:quarter].T
        across[1] = factor[:quarter].T
        flip = jnp.where(
            lax.broadcasted_iota(jnp.int32, square, 0) + lax.broadcasted_iota(jnp.int32, square, 1)
            == LANES - 1,
            1.0,
            0.0,
        ).astype(jnp.bfloat16)
        left = samples
        back = None
        for _ in range(3):
            some = left.astype(jnp.bfloat16)
            left = left - some.astype(jnp.float32)
            moved = jnp.dot(some, flip, preferred_element_type=jnp.float32)
            back = moved if back is None else back + moved
        rows_back[...] = back

        def turned(index):
            line = rows_back[pl.ds(index, 1), :]
            return pltpu.roll(jnp.broadcast_to(line, square), 0, 1, stride=1, stride_axis=0)

        def column(which, index):
            return jnp.sum(
                jnp.where(lane_quarter == index, across[which], 0.0), axis=1, keepdims=True
            )

        turn0 = turned(0)
        turn1 = turned(1)

        def step(index, state):
            turn, near = state
            following = turned(index + 2)
            far = jnp.where(keep, turn, following)
            c = column(0, index)
            f = column(1, index)
            row_z[index, :, :LANES] = ((near - c) * f).astype(jnp.bfloat16)
            row_z[index, :, LANES:] = ((far - c) * f).astype(jnp.bfloat16)
            return following, far

        lax.fori_loop(0, quarter, step, (turn1, jnp.where(keep, turn0, turn1)), unroll=16)

    starts = [starts_ref[c] for c in range(band_count)]
    whole = [lax.shift_right_logical(s, 7) for s in starts]
    rest = [lax.bitwise_and(s, LANES - 1) for s in starts]

    def build_cols():
        for c in range(band_count):
            back = lax.rem(LANES - rest[c], LANES)
            here = pltpu.roll(ext[pl.ds(first + whole[c], span), :], back, 1)
            below = pltpu.roll(ext[pl.ds(first + whole[c] + 1, span), :], back, 1)
            samples = jnp.where(lane < LANES - rest[c], here, below)
            shifted[c] = samples
            mean, factor = moments_of(samples)
            stats[2 * c] = mean
            stats[2 * c + 1] = factor

        def turned(c, index):
            line = shifted[c, pl.ds(index, 1), :]
            return pltpu.roll(jnp.broadcast_to(line, square), 1, 1, stride=1, stride_axis=0)

        def one_band(c, _):
            turn0 = turned(c, 0)
            turn1 = turned(c, 1)

            def step(index, state):
                turn, near = state
                following = turned(c, index + 2)
                far = jnp.where(upper, turn, following)
                center = stats[2 * c, pl.ds(index, 1), :]
                factor = stats[2 * c + 1, pl.ds(index, 1), :]
                col_z[c, index, :LANES, :] = ((near - center) * factor).astype(jnp.bfloat16)
                col_z[c, index, LANES:, :] = ((far - center) * factor).astype(jnp.bfloat16)
                return following, far

            lax.fori_loop(
                0, quarter + 1, step, (turn1, jnp.where(upper, turn0, turn1)), unroll=33
            )
            return 0

        lax.fori_loop(0, band_count, one_band, 0)

    def phase(turn, _):
        rows_now = lax.rem(turn + p // half, 2) == 0

        @pl.when(rows_now)
        def _():
            pl.when(low)(own_rows.wait)

            @pl.when(high)
            def _():
                rows_copy.wait_recv()
                head_copy.wait_recv()

            build_rows()

        @pl.when(jnp.logical_not(rows_now))
        def _():
            pl.when(low)(cols_copy.wait_recv)
            pl.when(high)(own_cols.wait)
            pl.when(next_taker)(next_copy.wait_recv)
            pl.when(p == blocks - 1)(own_tail.wait)
            build_cols()

        return 0

    lax.fori_loop(0, 2, phase, 0)

    last_block = lax.rem(p, half) + half
    room_all = (blocks - last_block) * block_rows * LANES - part * quarter * LANES
    lane_row = lax.broadcasted_iota(jnp.int32, (1, LANES), 1)

    lane_square = lax.broadcasted_iota(jnp.int32, square, 1)

    def score(index, state):
        pending, rows_found = state
        best = None
        left = []
        for c in range(band_count):
            both = jnp.concatenate([col_z[c, index], col_z[c, index + 1]], axis=1)
            found = jnp.dot(row_z[index], both, preferred_element_type=jnp.float32)
            room = room_all - starts[c] - index * LANES
            near = found[:, :LANES] + jnp.where(lane_row < room, 0.0, -4.0)
            far = found[:, LANES:] + jnp.where(lane_row + LANES < room, 0.0, -4.0)
            near_cols = jnp.max(jnp.where(keep, near, -4.0), axis=0, keepdims=True)
            far_cols = jnp.max(jnp.where(keep, -4.0, far), axis=0, keepdims=True)
            col_buf[c, pl.ds(quarter + index, 1), :] = jnp.maximum(
                jnp.maximum(pending[c], near_cols), -1.0
            )
            left.append(jnp.maximum(far_cols, -1.0))
            joined = jnp.where(keep, near, far)
            best = joined if best is None else jnp.maximum(best, joined)
        rows_found = jnp.where(
            lane_square == index, jnp.max(best, axis=1, keepdims=True), rows_found
        )
        return tuple(left), rows_found

    floor = jnp.full((1, LANES), -1.0, jnp.float32)
    pending, rows_found = lax.fori_loop(
        0, quarter, score, ((floor,) * band_count, jnp.full(square, -1.0, jnp.float32)), unroll=16
    )
    row_res[...] = jnp.maximum(rows_found.T[:quarter], -1.0)
    lane_wide = lax.broadcasted_iota(jnp.int32, (2 * quarter, LANES), 1)
    reached = None
    for c in range(band_count):
        col_buf[c, pl.ds(2 * quarter, 1), :] = pending[c]
        here = pltpu.roll(col_buf[c, pl.ds(quarter - whole[c], 2 * quarter), :], rest[c], 1)
        above = pltpu.roll(col_buf[c, pl.ds(quarter - whole[c] - 1, 2 * quarter), :], rest[c], 1)
        placed = jnp.where(lane_wide >= rest[c], here, above)
        reached = placed if reached is None else jnp.maximum(reached, placed)
    col_res[...] = reached

    place = pl.ds(pl.multiple_of(part * quarter, 8), quarter)
    row_to = [
        remote(row_res, row_out.at[place, :], out_send.at[k], row_recv.at[part], tm, band)
        for k, (tm, band) in enumerate([(p, 1 - b), (partner, 0), (partner, 1)])
    ]
    slot_to = [
        remote(col_res, slots.at[part], out_send.at[3 + k], slot_recv.at[part], tm, band)
        for k, (tm, band) in enumerate([(p, 1 - b), (partner, 0), (partner, 1)])
    ]
    lower = pl.ds(0, quarter)
    lower_to = remote(
        col_res.at[lower, :],
        slots.at[part, lower, :],
        out_send.at[3],
        slot_recv.at[part],
        p,
        1 - b,
    )
    carry_to = [
        remote(
            col_res.at[pl.ds(quarter, quarter), :],
            carry_in,
            out_send.at[6 + k],
            carry_recv.at[0],
            lax.rem(p + 1, blocks),
            k,
        )
        for k in range(2)
    ]

    @pl.when(low)
    def _():
        slot_to[1].start()
        slot_to[2].start()
        row_to[0].start()
        row_out[place, :] = row_res[...]

    @pl.when(high)
    def _():
        row_to[1].start()
        row_to[2].start()

    @pl.when(jnp.logical_and(high, b == 0))
    def _():
        slot_to[0].start()
        slots[2] = col_res[...]

    @pl.when(carry_sender)
    def _():
        carry_to[0].start()
        carry_to[1].start()

    @pl.when(jnp.logical_and(high, b == 1))
    def _():
        lower_to.start()
        slots[3, lower, :] = col_res[lower, :]

    def row_from(index):
        return remote(
            row_res,
            row_out.at[pl.ds(index * quarter, quarter), :],
            out_send.at[0],
            row_recv.at[index],
            p,
            1 - b,
        )

    def slot_from(index):
        return remote(
            col_res, slots.at[index], out_send.at[0], slot_recv.at[index], p, 1 - b
        )

    @pl.when(low)
    def _():
        pl.when(b == 1)(row_from(0).wait_recv)
        pl.when(b == 0)(row_from(1).wait_recv)
        row_from(2).wait_recv()
        row_from(3).wait_recv()

    @pl.when(high)
    def _():
        slot_from(0).wait_recv()
        slot_from(1).wait_recv()

    @pl.when(jnp.logical_and(high, b == 1))
    def _():
        slot_from(2).wait_recv()

    @pl.when(jnp.logical_and(high, b == 0))
    def _():
        remote(
            col_res.at[lower, :],
            slots.at[3, lower, :],
            out_send.at[0],
            slot_recv.at[3],
            p,
            1 - b,
        ).wait_recv()

    pl.when(carry_taker)(carry_to[0].wait_recv)

    @pl.when(p == half)
    def _():
        carry_in[...] = jnp.full(carry_in.shape, -1.0, jnp.float32)

    @pl.when(high)
    def _():
        col_out[pl.ds(0, quarter), :] = jnp.maximum(slots[0, lower, :], carry_in[...])
        for k in range(1, SLOTS):
            col_out[pl.ds(k * quarter, quarter), :] = jnp.maximum(
                slots[k, lower, :], slots[k - 1, pl.ds(quarter, quarter), :]
            )

    @pl.when(high)
    def _():
        cols_copy.wait_send()
        row_to[1].wait_send()
        row_to[2].wait_send()

    @pl.when(low)
    def _():
        rows_copy.wait_send()
        slot_to[1].wait_send()
        slot_to[2].wait_send()
        row_to[0].wait_send()

    pl.when(head_sender)(head_copy.wait_send)
    pl.when(next_sender)(next_copy.wait_send)
    pl.when(jnp.logical_and(high, b == 0))(slot_to[0].wait_send)
    pl.when(jnp.logical_and(high, b == 1))(lower_to.wait_send)

    @pl.when(carry_sender)
    def _():
        carry_to[0].wait_send()
        carry_to[1].wait_send()


def spread_body(series, tail, band_starts):
    block_rows = series.shape[0] // LANES
    quarter = block_rows // SLOTS
    band_count = band_starts.shape[0]
    blocks = lax.axis_size("tm")
    span = quarter + 8
    vmem = pl.BlockSpec(memory_space=pltpu.VMEM)
    whole = jax.ShapeDtypeStruct((block_rows, LANES), jnp.float32)

    operands = (band_starts, series.reshape(block_rows, LANES), tail.reshape(-1, LANES))

    def buffer(*shape, kind=jnp.float32):
        return pltpu.VMEM(shape, kind)

    best_rows, best_cols = pl.pallas_call(
        functools.partial(pair_kernel, blocks),
        out_shape=(whole, whole),
        in_specs=[pl.BlockSpec(memory_space=pltpu.HBM)] * 3,
        out_specs=(vmem, vmem),
        scratch_shapes=[
            pltpu.SMEM((band_count,), jnp.int32),
            buffer(block_rows + span, LANES),
            buffer(span, LANES),
            buffer(span, LANES),
            buffer(band_count, span, LANES),
            buffer(2 * band_count, span, LANES),
            buffer(2, LANES, quarter),
            buffer(quarter, LANES, M, kind=jnp.bfloat16),
            buffer(band_count, quarter + 1, M, LANES, kind=jnp.bfloat16),
            buffer(band_count, 3 * quarter + 8, LANES),
            buffer(quarter, LANES),
            buffer(2 * quarter, LANES),
            buffer(SLOTS, 2 * quarter, LANES),
            buffer(quarter, LANES),
            pltpu.SemaphoreType.DMA((3,)),
            pltpu.SemaphoreType.DMA((4,)),
            pltpu.SemaphoreType.DMA((4,)),
            pltpu.SemaphoreType.DMA((8,)),
            pltpu.SemaphoreType.DMA((SLOTS,)),
            pltpu.SemaphoreType.DMA((SLOTS,)),
            pltpu.SemaphoreType.DMA((1,)),
        ],
        compiler_params=pltpu.CompilerParams(
            collective_id=0, has_side_effects=True, vmem_limit_bytes=40 * 1024 * 1024
        ),
        name="banded_pairs",
    )(*[pltpu.with_memory_space_constraint(a, pltpu.HBM) for a in operands])
    return best_rows.reshape(-1), best_cols.reshape(-1)


def solution(mesh):
    placed = (P(("groups", "tm")), P("groups"), P("groups"))

    def chosen(series, tail, band_starts):
        halves = lax.axis_size("tm") == 2 * BAND_BLOCKS
        if halves and series.shape[0] == SLOTS * BAND_SPAN and lax.axis_size("band") == 2:
            return spread_body(series, tail, band_starts)
        return body(series, tail, band_starts)

    return jax.shard_map(
        chosen,
        mesh=mesh,
        in_specs=placed,
        out_specs=(P(("groups", "tm")), P(("groups", "tm"))),
        check_vma=False,
    )
```

```python
import functools

import jax
import jax.numpy as jnp
from jax import lax
from jax.experimental import pallas as pl
from jax.experimental.pallas import tpu as pltpu
from jax.sharding import PartitionSpec as P

M = 256
TILE = 128
OFF_DEV = 128
BAND_SPAN = 4096
BAND_BLOCKS = 4


EPS = 1e-06
tile_batch = 16


def from_behind(block, axis, distance):
    devices = range(lax.axis_size(axis))
    route = [(i - distance, i) for i in devices if i - distance in devices]
    return lax.ppermute(block, axis, route)


def hankel(samples, tile_count):
    length = tile_count * TILE + M
    shifted = jnp.stack(
        [lax.slice_in_dim(samples, offset, offset + length) for offset in range(TILE)]
    )
    blocks = shifted.reshape(TILE, length // TILE, TILE)
    joined = jnp.concatenate(
        [blocks[:, stride : stride + tile_count] for stride in range(M // TILE)], axis=2
    )
    return jnp.swapaxes(joined, 0, 1)


def moments(matrix):
    center = jnp.mean(matrix, axis=-1)
    spread = matrix - center[..., None]
    factor = lax.rsqrt(jnp.sum(spread * spread, axis=-1) + M * EPS)
    return (center, factor)


def normed(matrix, center, factor):
    return ((matrix - center[..., None]) * factor[..., None]).astype(jnp.bfloat16)


def score_group(row_z, col_z, room_left):
    tile_count = row_z.shape[0]
    near_scores = jnp.einsum("tim,tjm->tij", row_z, col_z[:-1], preferred_element_type=jnp.float32)
    far_scores = jnp.einsum(
        "tim,tjm->tij", row_z, col_z[1:, :OFF_DEV], preferred_element_type=jnp.float32
    )
    row_near = lax.broadcasted_iota(jnp.int32, (TILE, TILE), 0)
    col_near = lax.broadcasted_iota(jnp.int32, (TILE, TILE), 1)
    row_far = lax.broadcasted_iota(jnp.int32, (TILE, OFF_DEV), 0)
    col_far = lax.broadcasted_iota(jnp.int32, (TILE, OFF_DEV), 1)
    tile_index = jnp.arange(tile_count, dtype=jnp.int32)[:, None, None]
    keep_near = (
        (col_near >= row_near)[None]
        & (col_near - row_near < OFF_DEV)[None]
        & (tile_index * TILE + col_near[None] < room_left)
    )
    keep_far = (TILE + col_far - row_far < OFF_DEV)[None] & (
        (tile_index + 1) * TILE + col_far[None] < room_left
    )
    near_scores = jnp.where(keep_near, near_scores, -1.0)
    far_scores = jnp.where(keep_far, far_scores, -1.0)
    best_rows = jnp.maximum(near_scores.max(axis=2), far_scores.max(axis=2)).reshape(-1)
    floor_row = jnp.full((1, TILE), -1.0, jnp.float32)
    upper_part = jnp.concatenate([near_scores.max(axis=1), floor_row], axis=0)
    far_cols = far_scores.max(axis=1)
    lower_part = jnp.concatenate([floor_row, far_cols], axis=0)
    return (best_rows, jnp.maximum(upper_part, lower_part).reshape(-1))


def place_columns(col_groups, start, buffer_len):
    group_rows = tile_batch * TILE
    count = col_groups.shape[0]
    main_part = col_groups[:, :group_rows].reshape(-1)
    carry_part = jnp.concatenate(
        [col_groups[:, group_rows:], jnp.full((count, group_rows - TILE), -1.0, jnp.float32)],
        axis=1,
    ).reshape(-1)
    shifted = jnp.concatenate([jnp.full((group_rows,), -1.0, jnp.float32), carry_part])[
        : count * group_rows + TILE
    ]
    reached = jnp.maximum(
        jnp.concatenate([main_part, jnp.full((TILE,), -1.0, jnp.float32)]), shifted
    )
    buffer_all = jnp.full((buffer_len,), -1.0, jnp.float32)
    return lax.dynamic_update_slice(buffer_all, reached, (start,))


def body(series, tail, band_starts):
    block_len = series.shape[0]
    group_rows = tile_batch * TILE
    group_count = block_len // group_rows
    position = lax.axis_index("tm")
    devices = lax.axis_size("tm")
    distance = BAND_BLOCKS
    following = from_behind(series[:M], "tm", -1)
    following = jnp.where(position == devices - 1, tail, following)
    extended = jnp.concatenate([series, following])
    row_source = jnp.concatenate([extended, jnp.zeros((TILE,), jnp.float32)])

    def own_group(group_index):
        row_piece = lax.dynamic_slice_in_dim(
            row_source, group_index * group_rows, group_rows + M + TILE
        )
        matrix = hankel(row_piece, tile_batch)
        center, factor = moments(matrix)
        return (center.reshape(-1), factor.reshape(-1), normed(matrix, center, factor))

    centers, factors, row_z = lax.map(own_group, jnp.arange(group_count, dtype=jnp.int32))
    centers = centers.reshape(block_len)
    factors = factors.reshape(block_len)
    padding = jnp.zeros((2 * TILE,), jnp.float32)
    far_samples = from_behind(extended, "tm", -distance)
    next_samples = from_behind(series[M : M + BAND_SPAN], "tm", -distance - 1)
    pair_samples = jnp.concatenate([far_samples, next_samples, padding])
    buffer_len = block_len + BAND_SPAN + TILE
    band_count = band_starts.shape[0]
    band_here = lax.axis_index("band")
    offset_start = jnp.sum(
        jnp.where(jnp.arange(band_count, dtype=jnp.int32) == band_here, band_starts, 0)
    )
    room_all = (devices - position - distance) * block_len - offset_start

    def pair_group(inputs):
        group_index, group_z = inputs
        col_begin = offset_start + group_index * group_rows
        col_piece = lax.dynamic_slice_in_dim(pair_samples, col_begin, (tile_batch + 2) * TILE + M)
        matrix = hankel(col_piece, tile_batch + 1)
        center, factor = moments(matrix)
        col_z = normed(matrix, center, factor)
        return score_group(group_z, col_z, room_all - group_index * group_rows)

    row_best, col_groups = lax.map(pair_group, (jnp.arange(group_count, dtype=jnp.int32), row_z))
    lifted = place_columns(col_groups, offset_start, buffer_len) + 1.0
    returned = from_behind(lifted[:block_len], "tm", distance)
    returned_head = from_behind(lifted[block_len : block_len + BAND_SPAN], "tm", distance + 1)
    col_best = (
        jnp.maximum(
            returned,
            jnp.concatenate([returned_head, jnp.zeros((block_len - BAND_SPAN,), jnp.float32)]),
        )
        - 1.0
    )
    return lax.pmax((row_best.reshape(block_len), col_best), "band")


SLOTS = 4
LANES = 128


def pair_kernel(
    blocks,
    starts_in,
    x_ref,
    tail_ref,
    both_out,
    starts_ref,
    ext,
    rows_x,
    rows_back,
    shifted,
    stats,
    across,
    row_z,
    col_z,
    col_buf,
    row_res,
    col_res,
    slots,
    carry_in,
    local,
    in_send,
    in_recv,
    out_send,
    row_recv,
    slot_recv,
    carry_recv,
):
    half = BAND_BLOCKS
    block_rows = x_ref.shape[0]
    quarter = block_rows // SLOTS
    piece = 2 * quarter + 8
    band_count = starts_ref.shape[0]
    row_out = both_out.at[pl.ds(0, block_rows), :]
    col_out = both_out.at[pl.ds(block_rows, block_rows), :]
    p = lax.axis_index("tm")
    b = lax.axis_index("band")
    low = p < half
    high = p >= half
    partner = lax.rem(p + half, blocks)
    part = b + 2 * (p // half)
    first = 2 * quarter + quarter * b

    def remote(src, dst, send, recv, tm, band):
        return pltpu.make_async_remote_copy(
            src_ref=src,
            dst_ref=dst,
            send_sem=send,
            recv_sem=recv,
            device_id={"tm": tm, "band": band},
            device_id_type=pl.DeviceIdType.MESH,
        )

    head_sender = jnp.logical_and(p >= b, p < half + b)
    next_sender = p > half
    next_taker = jnp.logical_and(high, p < blocks - 1)
    carry_sender = jnp.logical_and(next_taker, b == 1)
    carry_taker = next_sender

    barrier = pltpu.get_barrier_semaphore()

    def greet(tm, band):
        pl.semaphore_signal(
            barrier, 1, device_id={"tm": tm, "band": band}, device_id_type=pl.DeviceIdType.MESH
        )

    greet(p, 1 - b)
    greet(partner, 0)
    greet(partner, 1)

    @pl.when(jnp.logical_and(high, b == 1))
    def _():
        greet(p - half + 1, 1)

    @pl.when(next_taker)
    def _():
        greet(p + 1, b)

    @pl.when(carry_taker)
    def _():
        greet(p - 1, 1)

    starts_copy = pltpu.make_async_copy(starts_in, starts_ref, local.at[0])
    own_rows = pltpu.make_async_copy(
        x_ref.at[pl.ds(pl.multiple_of(quarter * b, 8), quarter + 8), :], rows_x, local.at[1]
    )
    own_cols = pltpu.make_async_copy(
        x_ref.at[pl.ds(2 * quarter, 2 * quarter), :],
        ext.at[pl.ds(2 * quarter, 2 * quarter), :],
        local.at[1],
    )
    own_tail = pltpu.make_async_copy(
        tail_ref, ext.at[pl.ds(block_rows, M // LANES), :], local.at[2]
    )
    starts_copy.start()
    pl.when(low)(own_rows.start)
    pl.when(high)(own_cols.start)

    @pl.when(p == blocks - 1)
    def _():
        ext[pl.ds(block_rows, quarter + 8), :] = jnp.zeros((quarter + 8, LANES), jnp.float32)
        own_tail.start()

    col_buf[...] = jnp.full(col_buf.shape, -1.0, jnp.float32)

    @pl.when(low)
    def _():
        col_out[...] = jnp.full(col_out.shape, -1.0, jnp.float32)

    @pl.when(high)
    def _():
        row_out[...] = jnp.full(row_out.shape, -1.0, jnp.float32)

    head_here = jnp.where(jnp.logical_and(b == 1, jnp.logical_and(p >= 1, p <= half)), 1, 0)
    next_here = jnp.where(next_sender, 1, 0)
    carry_here = jnp.where(carry_sender, 2, 0)
    pl.semaphore_wait(barrier, 3 + head_here + next_here + carry_here)

    cols_copy = remote(
        x_ref.at[pl.ds(pl.multiple_of(quarter * b, 8), piece), :],
        ext.at[pl.ds(pl.multiple_of(first, 8), piece), :],
        in_send.at[0],
        in_recv.at[0],
        partner,
        b,
    )
    rows_copy = remote(
        x_ref.at[pl.ds(pl.multiple_of(first, 8), quarter), :],
        rows_x.at[pl.ds(0, quarter), :],
        in_send.at[1],
        in_recv.at[1],
        partner,
        b,
    )
    head_copy = remote(
        x_ref.at[pl.ds(pl.multiple_of(3 * quarter * (1 - b), 8), 8), :],
        rows_x.at[pl.ds(quarter, 8), :],
        in_send.at[2],
        in_recv.at[2],
        lax.rem(p + half - b, blocks),
        b,
    )
    next_copy = remote(
        x_ref.at[pl.ds(0, quarter + 8), :],
        ext.at[pl.ds(block_rows, quarter + 8), :],
        in_send.at[3],
        in_recv.at[3],
        lax.rem(p + blocks - 1, blocks),
        b,
    )
    pl.when(high)(cols_copy.start)
    pl.when(low)(rows_copy.start)
    pl.when(head_sender)(head_copy.start)
    pl.when(next_sender)(next_copy.start)

    starts_copy.wait()
    span = quarter + 8
    lane = lax.broadcasted_iota(jnp.int32, (span, LANES), 1)

    def moments_of(samples):
        mean, spread = samples, None
        width = 1

        def ahead(values):
            below = pltpu.roll(values, span - 1, 0)
            if width == LANES:
                return below
            turned = pltpu.roll(values, LANES - width, 1)
            return jnp.where(lane < LANES - width, turned, pltpu.roll(turned, span - 1, 0))

        while width < M:
            other = ahead(mean)
            gap = mean - other
            term = gap * gap * (0.5 * width)
            spread = term if spread is None else spread + ahead(spread) + term
            mean = 0.5 * (mean + other)
            width *= 2
        return mean, lax.rsqrt(spread + M * EPS)

    square = (LANES, LANES)
    upper = lax.broadcasted_iota(jnp.int32, square, 1) <= lax.broadcasted_iota(jnp.int32, square, 0)
    keep = lax.broadcasted_iota(jnp.int32, square, 1) >= lax.broadcasted_iota(jnp.int32, square, 0)

    def turned_row(source, index):
        line = source[pl.ds(index, 1), :]
        return pltpu.roll(jnp.broadcast_to(line, square), 1, 1, stride=1, stride_axis=0)


    def build_rows():
        samples = rows_x[...]
        mean, factor = moments_of(samples)
        across[0] = mean[:quarter].T
        across[1] = factor[:quarter].T
        flip = jnp.where(
            lax.broadcasted_iota(jnp.int32, square, 0) + lax.broadcasted_iota(jnp.int32, square, 1)
            == LANES - 1,
            1.0,
            0.0,
        ).astype(jnp.bfloat16)
        left = samples
        back = None
        for _ in range(3):
            some = left.astype(jnp.bfloat16)
            left = left - some.astype(jnp.float32)
            moved = jnp.dot(some, flip, preferred_element_type=jnp.float32)
            back = moved if back is None else back + moved
        rows_back[...] = back

        def turned(index):
            line = rows_back[pl.ds(index, 1), :]
            return pltpu.roll(jnp.broadcast_to(line, square), 0, 1, stride=1, stride_axis=0)

        turn = turned(1)
        near = jnp.where(keep, turned(0), turn)
        for index in range(quarter):
            following = turned(index + 2)
            far = jnp.where(keep, turn, following)
            c = across[0, :, index : index + 1]
            f = across[1, :, index : index + 1]
            row_z[index, :, :LANES] = ((near - c) * f).astype(jnp.bfloat16)
            row_z[index, :, LANES:] = ((far - c) * f).astype(jnp.bfloat16)
            turn, near = following, far

    starts = [starts_ref[c] for c in range(band_count)]
    whole = [lax.shift_right_logical(s, 7) for s in starts]
    rest = [lax.bitwise_and(s, LANES - 1) for s in starts]

    def build_cols():
        for c in range(band_count):
            back = lax.rem(LANES - rest[c], LANES)
            here = pltpu.roll(ext[pl.ds(first + whole[c], span), :], back, 1)
            below = pltpu.roll(ext[pl.ds(first + whole[c] + 1, span), :], back, 1)
            samples = jnp.where(lane < LANES - rest[c], here, below)
            shifted[c] = samples
            mean, factor = moments_of(samples)
            stats[2 * c] = mean
            stats[2 * c + 1] = factor

        def turned(c, index):
            line = shifted[c, pl.ds(index, 1), :]
            return pltpu.roll(jnp.broadcast_to(line, square), 1, 1, stride=1, stride_axis=0)

        def one_band(c, _):
            turn0 = turned(c, 0)
            turn1 = turned(c, 1)

            def step(index, state):
                turn, near = state
                following = turned(c, index + 2)
                far = jnp.where(upper, turn, following)
                center = stats[2 * c, pl.ds(index, 1), :]
                factor = stats[2 * c + 1, pl.ds(index, 1), :]
                col_z[c, index, :LANES, :] = ((near - center) * factor).astype(jnp.bfloat16)
                col_z[c, index, LANES:, :] = ((far - center) * factor).astype(jnp.bfloat16)
                return following, far

            lax.fori_loop(
                0, quarter + 1, step, (turn1, jnp.where(upper, turn0, turn1)), unroll=33
            )
            return 0

        lax.fori_loop(0, band_count, one_band, 0)

    def phase(turn, _):
        rows_now = lax.rem(turn + p // half, 2) == 0

        @pl.when(rows_now)
        def _():
            pl.when(low)(own_rows.wait)

            @pl.when(high)
            def _():
                rows_copy.wait_recv()
                head_copy.wait_recv()

            build_rows()

        @pl.when(jnp.logical_not(rows_now))
        def _():
            pl.when(low)(cols_copy.wait_recv)
            pl.when(high)(own_cols.wait)
            pl.when(next_taker)(next_copy.wait_recv)
            pl.when(p == blocks - 1)(own_tail.wait)
            build_cols()

        return 0

    lax.fori_loop(0, 2, phase, 0)

    last_block = lax.rem(p, half) + half
    room_all = (blocks - last_block) * block_rows * LANES - part * quarter * LANES
    lane_row = lax.broadcasted_iota(jnp.int32, (1, LANES), 1)

    lane_square = lax.broadcasted_iota(jnp.int32, square, 1)

    def score(index, state):
        pending, rows_found = state
        best = None
        left = []
        for c in range(band_count):
            both = jnp.concatenate([col_z[c, index], col_z[c, index + 1]], axis=1)
            found = jnp.dot(row_z[index], both, preferred_element_type=jnp.float32)
            room = room_all - starts[c] - index * LANES
            near = found[:, :LANES] + jnp.where(lane_row < room, 0.0, -4.0)
            far = found[:, LANES:] + jnp.where(lane_row + LANES < room, 0.0, -4.0)
            near_cols = jnp.max(jnp.where(keep, near, -4.0), axis=0, keepdims=True)
            far_cols = jnp.max(jnp.where(keep, -4.0, far), axis=0, keepdims=True)
            col_buf[c, pl.ds(quarter + index, 1), :] = jnp.maximum(
                jnp.maximum(pending[c], near_cols), -1.0
            )
            left.append(jnp.maximum(far_cols, -1.0))
            joined = jnp.where(keep, near, far)
            best = joined if best is None else jnp.maximum(best, joined)
        rows_found = jnp.where(
            lane_square == index, jnp.max(best, axis=1, keepdims=True), rows_found
        )
        return tuple(left), rows_found

    floor = jnp.full((1, LANES), -1.0, jnp.float32)
    pending, rows_found = lax.fori_loop(
        0, quarter, score, ((floor,) * band_count, jnp.full(square, -1.0, jnp.float32)), unroll=16
    )
    row_res[...] = jnp.maximum(rows_found.T[:quarter], -1.0)
    lane_wide = lax.broadcasted_iota(jnp.int32, (2 * quarter, LANES), 1)
    reached = None
    for c in range(band_count):
        col_buf[c, pl.ds(2 * quarter, 1), :] = pending[c]
        here = pltpu.roll(col_buf[c, pl.ds(quarter - whole[c], 2 * quarter), :], rest[c], 1)
        above = pltpu.roll(col_buf[c, pl.ds(quarter - whole[c] - 1, 2 * quarter), :], rest[c], 1)
        placed = jnp.where(lane_wide >= rest[c], here, above)
        reached = placed if reached is None else jnp.maximum(reached, placed)
    col_res[...] = reached

    place = pl.ds(pl.multiple_of(part * quarter, 8), quarter)
    row_to = [
        remote(row_res, row_out.at[place, :], out_send.at[k], row_recv.at[part], tm, band)
        for k, (tm, band) in enumerate([(p, 1 - b), (partner, 0), (partner, 1)])
    ]
    slot_to = [
        remote(col_res, slots.at[part], out_send.at[3 + k], slot_recv.at[part], tm, band)
        for k, (tm, band) in enumerate([(p, 1 - b), (partner, 0), (partner, 1)])
    ]
    lower = pl.ds(0, quarter)
    lower_to = remote(
        col_res.at[lower, :],
        slots.at[part, lower, :],
        out_send.at[3],
        slot_recv.at[part],
        p,
        1 - b,
    )
    carry_to = [
        remote(
            col_res.at[pl.ds(quarter, quarter), :],
            carry_in,
            out_send.at[6 + k],
            carry_recv.at[0],
            lax.rem(p + 1, blocks),
            k,
        )
        for k in range(2)
    ]

    @pl.when(low)
    def _():
        slot_to[1].start()
        slot_to[2].start()
        row_to[0].start()
        row_out[place, :] = row_res[...]

    @pl.when(high)
    def _():
        row_to[1].start()
        row_to[2].start()

    @pl.when(jnp.logical_and(high, b == 0))
    def _():
        slot_to[0].start()
        slots[2] = col_res[...]

    @pl.when(carry_sender)
    def _():
        carry_to[0].start()
        carry_to[1].start()

    @pl.when(jnp.logical_and(high, b == 1))
    def _():
        lower_to.start()
        slots[3, lower, :] = col_res[lower, :]

    def row_from(index):
        return remote(
            row_res,
            row_out.at[pl.ds(index * quarter, quarter), :],
            out_send.at[0],
            row_recv.at[index],
            p,
            1 - b,
        )

    def slot_from(index):
        return remote(
            col_res, slots.at[index], out_send.at[0], slot_recv.at[index], p, 1 - b
        )

    @pl.when(low)
    def _():
        pl.when(b == 1)(row_from(0).wait_recv)
        pl.when(b == 0)(row_from(1).wait_recv)
        row_from(2).wait_recv()
        row_from(3).wait_recv()

    @pl.when(high)
    def _():
        slot_from(0).wait_recv()
        slot_from(1).wait_recv()

    @pl.when(jnp.logical_and(high, b == 1))
    def _():
        slot_from(2).wait_recv()

    @pl.when(jnp.logical_and(high, b == 0))
    def _():
        remote(
            col_res.at[lower, :],
            slots.at[3, lower, :],
            out_send.at[0],
            slot_recv.at[3],
            p,
            1 - b,
        ).wait_recv()

    pl.when(carry_taker)(carry_to[0].wait_recv)

    @pl.when(p == half)
    def _():
        carry_in[...] = jnp.full(carry_in.shape, -1.0, jnp.float32)

    @pl.when(high)
    def _():
        col_out[pl.ds(0, quarter), :] = jnp.maximum(slots[0, lower, :], carry_in[...])
        for k in range(1, SLOTS):
            col_out[pl.ds(k * quarter, quarter), :] = jnp.maximum(
                slots[k, lower, :], slots[k - 1, pl.ds(quarter, quarter), :]
            )

    @pl.when(high)
    def _():
        cols_copy.wait_send()
        row_to[1].wait_send()
        row_to[2].wait_send()

    @pl.when(low)
    def _():
        rows_copy.wait_send()
        slot_to[1].wait_send()
        slot_to[2].wait_send()
        row_to[0].wait_send()

    pl.when(head_sender)(head_copy.wait_send)
    pl.when(next_sender)(next_copy.wait_send)
    pl.when(jnp.logical_and(high, b == 0))(slot_to[0].wait_send)
    pl.when(jnp.logical_and(high, b == 1))(lower_to.wait_send)

    @pl.when(carry_sender)
    def _():
        carry_to[0].wait_send()
        carry_to[1].wait_send()


def spread_body(series, tail, band_starts):
    block_rows = series.shape[0] // LANES
    quarter = block_rows // SLOTS
    band_count = band_starts.shape[0]
    blocks = lax.axis_size("tm")
    span = quarter + 8
    vmem = pl.BlockSpec(memory_space=pltpu.VMEM)
    length = series.shape[0]
    outputs = jax.ShapeDtypeStruct((2 * block_rows, LANES), jnp.float32)

    operands = (band_starts, series.reshape(block_rows, LANES), tail.reshape(-1, LANES))

    def buffer(*shape, kind=jnp.float32):
        return pltpu.VMEM(shape, kind)

    both = pl.pallas_call(
        functools.partial(pair_kernel, blocks),
        out_shape=outputs,
        in_specs=[pl.BlockSpec(memory_space=pltpu.HBM)] * 3,
        out_specs=vmem,
        scratch_shapes=[
            pltpu.SMEM((band_count,), jnp.int32),
            buffer(block_rows + span, LANES),
            buffer(span, LANES),
            buffer(span, LANES),
            buffer(band_count, span, LANES),
            buffer(2 * band_count, span, LANES),
            buffer(2, LANES, quarter),
            buffer(quarter, LANES, M, kind=jnp.bfloat16),
            buffer(band_count, quarter + 1, M, LANES, kind=jnp.bfloat16),
            buffer(band_count, 3 * quarter + 8, LANES),
            buffer(quarter, LANES),
            buffer(2 * quarter, LANES),
            buffer(SLOTS, 2 * quarter, LANES),
            buffer(quarter, LANES),
            pltpu.SemaphoreType.DMA((3,)),
            pltpu.SemaphoreType.DMA((4,)),
            pltpu.SemaphoreType.DMA((4,)),
            pltpu.SemaphoreType.DMA((8,)),
            pltpu.SemaphoreType.DMA((SLOTS,)),
            pltpu.SemaphoreType.DMA((SLOTS,)),
            pltpu.SemaphoreType.DMA((1,)),
        ],
        compiler_params=pltpu.CompilerParams(
            collective_id=0, has_side_effects=True, vmem_limit_bytes=40 * 1024 * 1024
        ),
        name="banded_pairs",
    )(*[pltpu.with_memory_space_constraint(a, pltpu.HBM) for a in operands])
    flat = both.reshape(-1)
    return flat[:length], flat[length:]


def solution(mesh):
    placed = (P(("groups", "tm")), P("groups"), P("groups"))

    def chosen(series, tail, band_starts):
        halves = lax.axis_size("tm") == 2 * BAND_BLOCKS
        if halves and series.shape[0] == SLOTS * BAND_SPAN and lax.axis_size("band") == 2:
            return spread_body(series, tail, band_starts)
        return body(series, tail, band_starts)

    return jax.shard_map(
        chosen,
        mesh=mesh,
        in_specs=placed,
        out_specs=(P(("groups", "tm")), P(("groups", "tm"))),
        check_vma=False,
    )
```

```python
import functools

import jax
import jax.numpy as jnp
from jax import lax
from jax.experimental import pallas as pl
from jax.experimental.pallas import tpu as pltpu
from jax.sharding import PartitionSpec as P

M = 256
TILE = 128
OFF_DEV = 128
BAND_SPAN = 4096
BAND_BLOCKS = 4


EPS = 1e-06
tile_batch = 16


def from_behind(block, axis, distance):
    devices = range(lax.axis_size(axis))
    route = [(i - distance, i) for i in devices if i - distance in devices]
    return lax.ppermute(block, axis, route)


def hankel(samples, tile_count):
    length = tile_count * TILE + M
    shifted = jnp.stack(
        [lax.slice_in_dim(samples, offset, offset + length) for offset in range(TILE)]
    )
    blocks = shifted.reshape(TILE, length // TILE, TILE)
    joined = jnp.concatenate(
        [blocks[:, stride : stride + tile_count] for stride in range(M // TILE)], axis=2
    )
    return jnp.swapaxes(joined, 0, 1)


def moments(matrix):
    center = jnp.mean(matrix, axis=-1)
    spread = matrix - center[..., None]
    factor = lax.rsqrt(jnp.sum(spread * spread, axis=-1) + M * EPS)
    return (center, factor)


def normed(matrix, center, factor):
    return ((matrix - center[..., None]) * factor[..., None]).astype(jnp.bfloat16)


def score_group(row_z, col_z, room_left):
    tile_count = row_z.shape[0]
    near_scores = jnp.einsum("tim,tjm->tij", row_z, col_z[:-1], preferred_element_type=jnp.float32)
    far_scores = jnp.einsum(
        "tim,tjm->tij", row_z, col_z[1:, :OFF_DEV], preferred_element_type=jnp.float32
    )
    row_near = lax.broadcasted_iota(jnp.int32, (TILE, TILE), 0)
    col_near = lax.broadcasted_iota(jnp.int32, (TILE, TILE), 1)
    row_far = lax.broadcasted_iota(jnp.int32, (TILE, OFF_DEV), 0)
    col_far = lax.broadcasted_iota(jnp.int32, (TILE, OFF_DEV), 1)
    tile_index = jnp.arange(tile_count, dtype=jnp.int32)[:, None, None]
    keep_near = (
        (col_near >= row_near)[None]
        & (col_near - row_near < OFF_DEV)[None]
        & (tile_index * TILE + col_near[None] < room_left)
    )
    keep_far = (TILE + col_far - row_far < OFF_DEV)[None] & (
        (tile_index + 1) * TILE + col_far[None] < room_left
    )
    near_scores = jnp.where(keep_near, near_scores, -1.0)
    far_scores = jnp.where(keep_far, far_scores, -1.0)
    best_rows = jnp.maximum(near_scores.max(axis=2), far_scores.max(axis=2)).reshape(-1)
    floor_row = jnp.full((1, TILE), -1.0, jnp.float32)
    upper_part = jnp.concatenate([near_scores.max(axis=1), floor_row], axis=0)
    far_cols = far_scores.max(axis=1)
    lower_part = jnp.concatenate([floor_row, far_cols], axis=0)
    return (best_rows, jnp.maximum(upper_part, lower_part).reshape(-1))


def place_columns(col_groups, start, buffer_len):
    group_rows = tile_batch * TILE
    count = col_groups.shape[0]
    main_part = col_groups[:, :group_rows].reshape(-1)
    carry_part = jnp.concatenate(
        [col_groups[:, group_rows:], jnp.full((count, group_rows - TILE), -1.0, jnp.float32)],
        axis=1,
    ).reshape(-1)
    shifted = jnp.concatenate([jnp.full((group_rows,), -1.0, jnp.float32), carry_part])[
        : count * group_rows + TILE
    ]
    reached = jnp.maximum(
        jnp.concatenate([main_part, jnp.full((TILE,), -1.0, jnp.float32)]), shifted
    )
    buffer_all = jnp.full((buffer_len,), -1.0, jnp.float32)
    return lax.dynamic_update_slice(buffer_all, reached, (start,))


def body(series, tail, band_starts):
    block_len = series.shape[0]
    group_rows = tile_batch * TILE
    group_count = block_len // group_rows
    position = lax.axis_index("tm")
    devices = lax.axis_size("tm")
    distance = BAND_BLOCKS
    following = from_behind(series[:M], "tm", -1)
    following = jnp.where(position == devices - 1, tail, following)
    extended = jnp.concatenate([series, following])
    row_source = jnp.concatenate([extended, jnp.zeros((TILE,), jnp.float32)])

    def own_group(group_index):
        row_piece = lax.dynamic_slice_in_dim(
            row_source, group_index * group_rows, group_rows + M + TILE
        )
        matrix = hankel(row_piece, tile_batch)
        center, factor = moments(matrix)
        return (center.reshape(-1), factor.reshape(-1), normed(matrix, center, factor))

    centers, factors, row_z = lax.map(own_group, jnp.arange(group_count, dtype=jnp.int32))
    centers = centers.reshape(block_len)
    factors = factors.reshape(block_len)
    padding = jnp.zeros((2 * TILE,), jnp.float32)
    far_samples = from_behind(extended, "tm", -distance)
    next_samples = from_behind(series[M : M + BAND_SPAN], "tm", -distance - 1)
    pair_samples = jnp.concatenate([far_samples, next_samples, padding])
    buffer_len = block_len + BAND_SPAN + TILE
    band_count = band_starts.shape[0]
    band_here = lax.axis_index("band")
    offset_start = jnp.sum(
        jnp.where(jnp.arange(band_count, dtype=jnp.int32) == band_here, band_starts, 0)
    )
    room_all = (devices - position - distance) * block_len - offset_start

    def pair_group(inputs):
        group_index, group_z = inputs
        col_begin = offset_start + group_index * group_rows
        col_piece = lax.dynamic_slice_in_dim(pair_samples, col_begin, (tile_batch + 2) * TILE + M)
        matrix = hankel(col_piece, tile_batch + 1)
        center, factor = moments(matrix)
        col_z = normed(matrix, center, factor)
        return score_group(group_z, col_z, room_all - group_index * group_rows)

    row_best, col_groups = lax.map(pair_group, (jnp.arange(group_count, dtype=jnp.int32), row_z))
    lifted = place_columns(col_groups, offset_start, buffer_len) + 1.0
    returned = from_behind(lifted[:block_len], "tm", distance)
    returned_head = from_behind(lifted[block_len : block_len + BAND_SPAN], "tm", distance + 1)
    col_best = (
        jnp.maximum(
            returned,
            jnp.concatenate([returned_head, jnp.zeros((block_len - BAND_SPAN,), jnp.float32)]),
        )
        - 1.0
    )
    return lax.pmax((row_best.reshape(block_len), col_best), "band")


SLOTS = 4
LANES = 128


def pair_kernel(
    blocks,
    starts_in,
    x_ref,
    tail_ref,
    both_out,
    starts_ref,
    ext,
    rows_x,
    rows_back,
    shifted,
    stats,
    across,
    row_z,
    col_z,
    col_buf,
    row_res,
    col_res,
    slots,
    carry_in,
    local,
    in_send,
    in_recv,
    out_send,
    row_recv,
    slot_recv,
    carry_recv,
):
    half = BAND_BLOCKS
    block_rows = x_ref.shape[0]
    quarter = block_rows // SLOTS
    piece = 2 * quarter + 8
    band_count = starts_ref.shape[0]
    row_out = both_out.at[pl.ds(0, block_rows), :]
    col_out = both_out.at[pl.ds(block_rows, block_rows), :]
    p = lax.axis_index("tm")
    b = lax.axis_index("band")
    low = p < half
    high = p >= half
    partner = lax.rem(p + half, blocks)
    part = b + 2 * (p // half)
    first = 2 * quarter + quarter * b

    def remote(src, dst, send, recv, tm, band):
        return pltpu.make_async_remote_copy(
            src_ref=src,
            dst_ref=dst,
            send_sem=send,
            recv_sem=recv,
            device_id={"tm": tm, "band": band},
            device_id_type=pl.DeviceIdType.MESH,
        )

    head_sender = jnp.logical_and(p >= b, p < half + b)
    next_sender = p > half
    next_taker = jnp.logical_and(high, p < blocks - 1)
    carry_sender = jnp.logical_and(next_taker, b == 1)
    carry_taker = next_sender

    barrier = pltpu.get_barrier_semaphore()

    def greet(tm, band):
        pl.semaphore_signal(
            barrier, 1, device_id={"tm": tm, "band": band}, device_id_type=pl.DeviceIdType.MESH
        )

    greet(p, 1 - b)
    greet(partner, 0)
    greet(partner, 1)

    @pl.when(jnp.logical_and(high, b == 1))
    def _():
        greet(p - half + 1, 1)

    @pl.when(next_taker)
    def _():
        greet(p + 1, b)

    @pl.when(carry_taker)
    def _():
        greet(p - 1, 1)

    starts_copy = pltpu.make_async_copy(starts_in, starts_ref, local.at[0])
    own_rows = pltpu.make_async_copy(
        x_ref.at[pl.ds(pl.multiple_of(quarter * b, 8), quarter + 8), :], rows_x, local.at[1]
    )
    own_cols = pltpu.make_async_copy(
        x_ref.at[pl.ds(2 * quarter, 2 * quarter), :],
        ext.at[pl.ds(2 * quarter, 2 * quarter), :],
        local.at[1],
    )
    own_tail = pltpu.make_async_copy(
        tail_ref, ext.at[pl.ds(block_rows, M // LANES), :], local.at[2]
    )
    starts_copy.start()
    pl.when(low)(own_rows.start)
    pl.when(high)(own_cols.start)

    @pl.when(p == blocks - 1)
    def _():
        ext[pl.ds(block_rows, quarter + 8), :] = jnp.zeros((quarter + 8, LANES), jnp.float32)
        own_tail.start()

    col_buf[...] = jnp.full(col_buf.shape, -1.0, jnp.float32)

    @pl.when(low)
    def _():
        col_out[...] = jnp.full(col_out.shape, -1.0, jnp.float32)

    @pl.when(high)
    def _():
        row_out[...] = jnp.full(row_out.shape, -1.0, jnp.float32)

    head_here = jnp.where(jnp.logical_and(b == 1, jnp.logical_and(p >= 1, p <= half)), 1, 0)
    next_here = jnp.where(next_sender, 1, 0)
    carry_here = jnp.where(carry_sender, 2, 0)
    pl.semaphore_wait(barrier, 3 + head_here + next_here + carry_here)

    cols_copy = remote(
        x_ref.at[pl.ds(pl.multiple_of(quarter * b, 8), piece), :],
        ext.at[pl.ds(pl.multiple_of(first, 8), piece), :],
        in_send.at[0],
        in_recv.at[0],
        partner,
        b,
    )
    rows_copy = remote(
        x_ref.at[pl.ds(pl.multiple_of(first, 8), quarter), :],
        rows_x.at[pl.ds(0, quarter), :],
        in_send.at[1],
        in_recv.at[1],
        partner,
        b,
    )
    head_copy = remote(
        x_ref.at[pl.ds(pl.multiple_of(3 * quarter * (1 - b), 8), 8), :],
        rows_x.at[pl.ds(quarter, 8), :],
        in_send.at[2],
        in_recv.at[2],
        lax.rem(p + half - b, blocks),
        b,
    )
    next_copy = remote(
        x_ref.at[pl.ds(0, quarter + 8), :],
        ext.at[pl.ds(block_rows, quarter + 8), :],
        in_send.at[3],
        in_recv.at[3],
        lax.rem(p + blocks - 1, blocks),
        b,
    )
    pl.when(high)(cols_copy.start)
    pl.when(low)(rows_copy.start)
    pl.when(head_sender)(head_copy.start)
    pl.when(next_sender)(next_copy.start)

    starts_copy.wait()
    span = quarter + 8
    lane = lax.broadcasted_iota(jnp.int32, (span, LANES), 1)

    def moments_of(samples):
        mean, spread = samples, None
        width = 1

        def ahead(values):
            below = pltpu.roll(values, span - 1, 0)
            if width == LANES:
                return below
            turned = pltpu.roll(values, LANES - width, 1)
            return jnp.where(lane < LANES - width, turned, pltpu.roll(turned, span - 1, 0))

        while width < M:
            other = ahead(mean)
            gap = mean - other
            term = gap * gap * (0.5 * width)
            spread = term if spread is None else spread + ahead(spread) + term
            mean = 0.5 * (mean + other)
            width *= 2
        return mean, lax.rsqrt(spread + M * EPS)

    square = (LANES, LANES)
    upper = lax.broadcasted_iota(jnp.int32, square, 1) <= lax.broadcasted_iota(jnp.int32, square, 0)
    keep = lax.broadcasted_iota(jnp.int32, square, 1) >= lax.broadcasted_iota(jnp.int32, square, 0)

    def turned_row(source, index):
        line = source[pl.ds(index, 1), :]
        return pltpu.roll(jnp.broadcast_to(line, square), 1, 1, stride=1, stride_axis=0)


    def build_rows():
        samples = rows_x[...]
        mean, factor = moments_of(samples)
        across[0] = mean[:quarter].T
        across[1] = factor[:quarter].T
        flip = jnp.where(
            lax.broadcasted_iota(jnp.int32, square, 0) + lax.broadcasted_iota(jnp.int32, square, 1)
            == LANES - 1,
            1.0,
            0.0,
        ).astype(jnp.bfloat16)
        left = samples
        back = None
        for _ in range(3):
            some = left.astype(jnp.bfloat16)
            left = left - some.astype(jnp.float32)
            moved = jnp.dot(some, flip, preferred_element_type=jnp.float32)
            back = moved if back is None else back + moved
        rows_back[...] = back

        def turned(index):
            line = rows_back[pl.ds(index, 1), :]
            return pltpu.roll(jnp.broadcast_to(line, square), 0, 1, stride=1, stride_axis=0)

        turn = turned(1)
        near = jnp.where(keep, turned(0), turn)
        for index in range(quarter):
            following = turned(index + 2)
            far = jnp.where(keep, turn, following)
            c = across[0, :, index : index + 1]
            f = across[1, :, index : index + 1]
            row_z[index, :, :LANES] = ((near - c) * f).astype(jnp.bfloat16)
            row_z[index, :, LANES:] = ((far - c) * f).astype(jnp.bfloat16)
            turn, near = following, far

    starts = [starts_ref[c] for c in range(band_count)]
    whole = [lax.shift_right_logical(s, 7) for s in starts]
    rest = [lax.bitwise_and(s, LANES - 1) for s in starts]

    def build_cols():
        for c in range(band_count):
            back = lax.rem(LANES - rest[c], LANES)
            here = pltpu.roll(ext[pl.ds(first + whole[c], span), :], back, 1)
            below = pltpu.roll(ext[pl.ds(first + whole[c] + 1, span), :], back, 1)
            samples = jnp.where(lane < LANES - rest[c], here, below)
            shifted[c] = samples
            mean, factor = moments_of(samples)
            stats[2 * c] = mean
            stats[2 * c + 1] = factor

        for c in range(band_count - 1):
            build_band(c)

    def col_turned(c, index):
        line = shifted[c, pl.ds(index, 1), :]
        return pltpu.roll(jnp.broadcast_to(line, square), 1, 1, stride=1, stride_axis=0)

    def col_begin(c):
        turn = col_turned(c, 1)
        return turn, jnp.where(upper, col_turned(c, 0), turn)

    def col_tile(c, index, state):
        turn, near = state
        following = col_turned(c, index + 2)
        far = jnp.where(upper, turn, following)
        center = stats[2 * c, pl.ds(index, 1), :]
        factor = stats[2 * c + 1, pl.ds(index, 1), :]
        col_z[c, index, :LANES, :] = ((near - center) * factor).astype(jnp.bfloat16)
        col_z[c, index, LANES:, :] = ((far - center) * factor).astype(jnp.bfloat16)
        return following, far

    def build_band(c):
        state = col_begin(c)
        for index in range(quarter + 1):
            state = col_tile(c, index, state)

    def phase(turn, _):
        rows_now = lax.rem(turn + p // half, 2) == 0

        @pl.when(rows_now)
        def _():
            pl.when(low)(own_rows.wait)

            @pl.when(high)
            def _():
                rows_copy.wait_recv()
                head_copy.wait_recv()

            build_rows()

        @pl.when(jnp.logical_not(rows_now))
        def _():
            pl.when(low)(cols_copy.wait_recv)
            pl.when(high)(own_cols.wait)
            pl.when(next_taker)(next_copy.wait_recv)
            pl.when(p == blocks - 1)(own_tail.wait)
            build_cols()

        return 0

    lax.fori_loop(0, 2, phase, 0)

    last_block = lax.rem(p, half) + half
    room_all = (blocks - last_block) * block_rows * LANES - part * quarter * LANES
    lane_row = lax.broadcasted_iota(jnp.int32, (1, LANES), 1)

    lane_square = lax.broadcasted_iota(jnp.int32, square, 1)

    def score(index, state):
        pending, rows_found = state
        best = None
        left = []
        for c in range(band_count):
            both = jnp.concatenate([col_z[c, index], col_z[c, index + 1]], axis=1)
            found = jnp.dot(row_z[index], both, preferred_element_type=jnp.float32)
            room = room_all - starts[c] - index * LANES
            near = found[:, :LANES] + jnp.where(lane_row < room, 0.0, -4.0)
            far = found[:, LANES:] + jnp.where(lane_row + LANES < room, 0.0, -4.0)
            near_cols = jnp.max(jnp.where(keep, near, -4.0), axis=0, keepdims=True)
            far_cols = jnp.max(jnp.where(keep, -4.0, far), axis=0, keepdims=True)
            col_buf[c, pl.ds(quarter + index, 1), :] = jnp.maximum(
                jnp.maximum(pending[c], near_cols), -1.0
            )
            left.append(jnp.maximum(far_cols, -1.0))
            joined = jnp.where(keep, near, far)
            best = joined if best is None else jnp.maximum(best, joined)
        rows_found = jnp.where(
            lane_square == index, jnp.max(best, axis=1, keepdims=True), rows_found
        )
        return tuple(left), rows_found

    floor = jnp.full((1, LANES), -1.0, jnp.float32)
    ahead = band_count - 1
    col_state = col_tile(ahead, 0, col_begin(ahead))
    state = ((floor,) * band_count, jnp.full(square, -1.0, jnp.float32))
    for index in range(quarter):
        col_state = col_tile(ahead, index + 1, col_state)
        state = score(index, state)
    pending, rows_found = state
    row_res[...] = jnp.maximum(rows_found.T[:quarter], -1.0)
    lane_wide = lax.broadcasted_iota(jnp.int32, (2 * quarter, LANES), 1)
    reached = None
    for c in range(band_count):
        col_buf[c, pl.ds(2 * quarter, 1), :] = pending[c]
        here = pltpu.roll(col_buf[c, pl.ds(quarter - whole[c], 2 * quarter), :], rest[c], 1)
        above = pltpu.roll(col_buf[c, pl.ds(quarter - whole[c] - 1, 2 * quarter), :], rest[c], 1)
        placed = jnp.where(lane_wide >= rest[c], here, above)
        reached = placed if reached is None else jnp.maximum(reached, placed)
    col_res[...] = reached

    place = pl.ds(pl.multiple_of(part * quarter, 8), quarter)
    row_to = [
        remote(row_res, row_out.at[place, :], out_send.at[k], row_recv.at[part], tm, band)
        for k, (tm, band) in enumerate([(p, 1 - b), (partner, 0), (partner, 1)])
    ]
    slot_to = [
        remote(col_res, slots.at[part], out_send.at[3 + k], slot_recv.at[part], tm, band)
        for k, (tm, band) in enumerate([(p, 1 - b), (partner, 0), (partner, 1)])
    ]
    lower = pl.ds(0, quarter)
    lower_to = remote(
        col_res.at[lower, :],
        slots.at[part, lower, :],
        out_send.at[3],
        slot_recv.at[part],
        p,
        1 - b,
    )
    carry_to = [
        remote(
            col_res.at[pl.ds(quarter, quarter), :],
            carry_in,
            out_send.at[6 + k],
            carry_recv.at[0],
            lax.rem(p + 1, blocks),
            k,
        )
        for k in range(2)
    ]

    @pl.when(low)
    def _():
        slot_to[1].start()
        slot_to[2].start()
        row_to[0].start()
        row_out[place, :] = row_res[...]

    @pl.when(high)
    def _():
        row_to[1].start()
        row_to[2].start()

    @pl.when(jnp.logical_and(high, b == 0))
    def _():
        slot_to[0].start()
        slots[2] = col_res[...]

    @pl.when(carry_sender)
    def _():
        carry_to[0].start()
        carry_to[1].start()

    @pl.when(jnp.logical_and(high, b == 1))
    def _():
        lower_to.start()
        slots[3, lower, :] = col_res[lower, :]

    def row_from(index):
        return remote(
            row_res,
            row_out.at[pl.ds(index * quarter, quarter), :],
            out_send.at[0],
            row_recv.at[index],
            p,
            1 - b,
        )

    def slot_from(index):
        return remote(
            col_res, slots.at[index], out_send.at[0], slot_recv.at[index], p, 1 - b
        )

    @pl.when(low)
    def _():
        pl.when(b == 1)(row_from(0).wait_recv)
        pl.when(b == 0)(row_from(1).wait_recv)
        row_from(2).wait_recv()
        row_from(3).wait_recv()

    @pl.when(high)
    def _():
        slot_from(0).wait_recv()
        slot_from(1).wait_recv()

    @pl.when(jnp.logical_and(high, b == 1))
    def _():
        slot_from(2).wait_recv()

    @pl.when(jnp.logical_and(high, b == 0))
    def _():
        remote(
            col_res.at[lower, :],
            slots.at[3, lower, :],
            out_send.at[0],
            slot_recv.at[3],
            p,
            1 - b,
        ).wait_recv()

    pl.when(carry_taker)(carry_to[0].wait_recv)

    @pl.when(p == half)
    def _():
        carry_in[...] = jnp.full(carry_in.shape, -1.0, jnp.float32)

    @pl.when(high)
    def _():
        col_out[pl.ds(0, quarter), :] = jnp.maximum(slots[0, lower, :], carry_in[...])
        for k in range(1, SLOTS):
            col_out[pl.ds(k * quarter, quarter), :] = jnp.maximum(
                slots[k, lower, :], slots[k - 1, pl.ds(quarter, quarter), :]
            )

    @pl.when(high)
    def _():
        cols_copy.wait_send()
        row_to[1].wait_send()
        row_to[2].wait_send()

    @pl.when(low)
    def _():
        rows_copy.wait_send()
        slot_to[1].wait_send()
        slot_to[2].wait_send()
        row_to[0].wait_send()

    pl.when(head_sender)(head_copy.wait_send)
    pl.when(next_sender)(next_copy.wait_send)
    pl.when(jnp.logical_and(high, b == 0))(slot_to[0].wait_send)
    pl.when(jnp.logical_and(high, b == 1))(lower_to.wait_send)

    @pl.when(carry_sender)
    def _():
        carry_to[0].wait_send()
        carry_to[1].wait_send()


def spread_body(series, tail, band_starts):
    block_rows = series.shape[0] // LANES
    quarter = block_rows // SLOTS
    band_count = band_starts.shape[0]
    blocks = lax.axis_size("tm")
    span = quarter + 8
    vmem = pl.BlockSpec(memory_space=pltpu.VMEM)
    length = series.shape[0]
    outputs = jax.ShapeDtypeStruct((2 * block_rows, LANES), jnp.float32)

    operands = (band_starts, series.reshape(block_rows, LANES), tail.reshape(-1, LANES))

    def buffer(*shape, kind=jnp.float32):
        return pltpu.VMEM(shape, kind)

    both = pl.pallas_call(
        functools.partial(pair_kernel, blocks),
        out_shape=outputs,
        in_specs=[pl.BlockSpec(memory_space=pltpu.HBM)] * 3,
        out_specs=vmem,
        scratch_shapes=[
            pltpu.SMEM((band_count,), jnp.int32),
            buffer(block_rows + span, LANES),
            buffer(span, LANES),
            buffer(span, LANES),
            buffer(band_count, span, LANES),
            buffer(2 * band_count, span, LANES),
            buffer(2, LANES, quarter),
            buffer(quarter, LANES, M, kind=jnp.bfloat16),
            buffer(band_count, quarter + 1, M, LANES, kind=jnp.bfloat16),
            buffer(band_count, 3 * quarter + 8, LANES),
            buffer(quarter, LANES),
            buffer(2 * quarter, LANES),
            buffer(SLOTS, 2 * quarter, LANES),
            buffer(quarter, LANES),
            pltpu.SemaphoreType.DMA((3,)),
            pltpu.SemaphoreType.DMA((4,)),
            pltpu.SemaphoreType.DMA((4,)),
            pltpu.SemaphoreType.DMA((8,)),
            pltpu.SemaphoreType.DMA((SLOTS,)),
            pltpu.SemaphoreType.DMA((SLOTS,)),
            pltpu.SemaphoreType.DMA((1,)),
        ],
        compiler_params=pltpu.CompilerParams(
            collective_id=0, has_side_effects=True, vmem_limit_bytes=40 * 1024 * 1024
        ),
        name="banded_pairs",
    )(*[pltpu.with_memory_space_constraint(a, pltpu.HBM) for a in operands])
    flat = both.reshape(-1)
    return flat[:length], flat[length:]


def solution(mesh):
    placed = (P(("groups", "tm")), P("groups"), P("groups"))

    def chosen(series, tail, band_starts):
        halves = lax.axis_size("tm") == 2 * BAND_BLOCKS
        if halves and series.shape[0] == SLOTS * BAND_SPAN and lax.axis_size("band") == 2:
            return spread_body(series, tail, band_starts)
        return body(series, tail, band_starts)

    return jax.shard_map(
        chosen,
        mesh=mesh,
        in_specs=placed,
        out_specs=(P(("groups", "tm")), P(("groups", "tm"))),
        check_vma=False,
    )
```

```python
import functools

import jax
import jax.numpy as jnp
from jax import lax
from jax.experimental import pallas as pl
from jax.experimental.pallas import tpu as pltpu
from jax.sharding import PartitionSpec as P

M = 256
TILE = 128
OFF_DEV = 128
BAND_SPAN = 4096
BAND_BLOCKS = 4


EPS = 1e-06
tile_batch = 16


def from_behind(block, axis, distance):
    devices = range(lax.axis_size(axis))
    route = [(i - distance, i) for i in devices if i - distance in devices]
    return lax.ppermute(block, axis, route)


def hankel(samples, tile_count):
    length = tile_count * TILE + M
    shifted = jnp.stack(
        [lax.slice_in_dim(samples, offset, offset + length) for offset in range(TILE)]
    )
    blocks = shifted.reshape(TILE, length // TILE, TILE)
    joined = jnp.concatenate(
        [blocks[:, stride : stride + tile_count] for stride in range(M // TILE)], axis=2
    )
    return jnp.swapaxes(joined, 0, 1)


def moments(matrix):
    center = jnp.mean(matrix, axis=-1)
    spread = matrix - center[..., None]
    factor = lax.rsqrt(jnp.sum(spread * spread, axis=-1) + M * EPS)
    return (center, factor)


def normed(matrix, center, factor):
    return ((matrix - center[..., None]) * factor[..., None]).astype(jnp.bfloat16)


def score_group(row_z, col_z, room_left):
    tile_count = row_z.shape[0]
    near_scores = jnp.einsum("tim,tjm->tij", row_z, col_z[:-1], preferred_element_type=jnp.float32)
    far_scores = jnp.einsum(
        "tim,tjm->tij", row_z, col_z[1:, :OFF_DEV], preferred_element_type=jnp.float32
    )
    row_near = lax.broadcasted_iota(jnp.int32, (TILE, TILE), 0)
    col_near = lax.broadcasted_iota(jnp.int32, (TILE, TILE), 1)
    row_far = lax.broadcasted_iota(jnp.int32, (TILE, OFF_DEV), 0)
    col_far = lax.broadcasted_iota(jnp.int32, (TILE, OFF_DEV), 1)
    tile_index = jnp.arange(tile_count, dtype=jnp.int32)[:, None, None]
    keep_near = (
        (col_near >= row_near)[None]
        & (col_near - row_near < OFF_DEV)[None]
        & (tile_index * TILE + col_near[None] < room_left)
    )
    keep_far = (TILE + col_far - row_far < OFF_DEV)[None] & (
        (tile_index + 1) * TILE + col_far[None] < room_left
    )
    near_scores = jnp.where(keep_near, near_scores, -1.0)
    far_scores = jnp.where(keep_far, far_scores, -1.0)
    best_rows = jnp.maximum(near_scores.max(axis=2), far_scores.max(axis=2)).reshape(-1)
    floor_row = jnp.full((1, TILE), -1.0, jnp.float32)
    upper_part = jnp.concatenate([near_scores.max(axis=1), floor_row], axis=0)
    far_cols = far_scores.max(axis=1)
    lower_part = jnp.concatenate([floor_row, far_cols], axis=0)
    return (best_rows, jnp.maximum(upper_part, lower_part).reshape(-1))


def place_columns(col_groups, start, buffer_len):
    group_rows = tile_batch * TILE
    count = col_groups.shape[0]
    main_part = col_groups[:, :group_rows].reshape(-1)
    carry_part = jnp.concatenate(
        [col_groups[:, group_rows:], jnp.full((count, group_rows - TILE), -1.0, jnp.float32)],
        axis=1,
    ).reshape(-1)
    shifted = jnp.concatenate([jnp.full((group_rows,), -1.0, jnp.float32), carry_part])[
        : count * group_rows + TILE
    ]
    reached = jnp.maximum(
        jnp.concatenate([main_part, jnp.full((TILE,), -1.0, jnp.float32)]), shifted
    )
    buffer_all = jnp.full((buffer_len,), -1.0, jnp.float32)
    return lax.dynamic_update_slice(buffer_all, reached, (start,))


def body(series, tail, band_starts):
    block_len = series.shape[0]
    group_rows = tile_batch * TILE
    group_count = block_len // group_rows
    position = lax.axis_index("tm")
    devices = lax.axis_size("tm")
    distance = BAND_BLOCKS
    following = from_behind(series[:M], "tm", -1)
    following = jnp.where(position == devices - 1, tail, following)
    extended = jnp.concatenate([series, following])
    row_source = jnp.concatenate([extended, jnp.zeros((TILE,), jnp.float32)])

    def own_group(group_index):
        row_piece = lax.dynamic_slice_in_dim(
            row_source, group_index * group_rows, group_rows + M + TILE
        )
        matrix = hankel(row_piece, tile_batch)
        center, factor = moments(matrix)
        return (center.reshape(-1), factor.reshape(-1), normed(matrix, center, factor))

    centers, factors, row_z = lax.map(own_group, jnp.arange(group_count, dtype=jnp.int32))
    centers = centers.reshape(block_len)
    factors = factors.reshape(block_len)
    padding = jnp.zeros((2 * TILE,), jnp.float32)
    far_samples = from_behind(extended, "tm", -distance)
    next_samples = from_behind(series[M : M + BAND_SPAN], "tm", -distance - 1)
    pair_samples = jnp.concatenate([far_samples, next_samples, padding])
    buffer_len = block_len + BAND_SPAN + TILE
    band_count = band_starts.shape[0]
    band_here = lax.axis_index("band")
    offset_start = jnp.sum(
        jnp.where(jnp.arange(band_count, dtype=jnp.int32) == band_here, band_starts, 0)
    )
    room_all = (devices - position - distance) * block_len - offset_start

    def pair_group(inputs):
        group_index, group_z = inputs
        col_begin = offset_start + group_index * group_rows
        col_piece = lax.dynamic_slice_in_dim(pair_samples, col_begin, (tile_batch + 2) * TILE + M)
        matrix = hankel(col_piece, tile_batch + 1)
        center, factor = moments(matrix)
        col_z = normed(matrix, center, factor)
        return score_group(group_z, col_z, room_all - group_index * group_rows)

    row_best, col_groups = lax.map(pair_group, (jnp.arange(group_count, dtype=jnp.int32), row_z))
    lifted = place_columns(col_groups, offset_start, buffer_len) + 1.0
    returned = from_behind(lifted[:block_len], "tm", distance)
    returned_head = from_behind(lifted[block_len : block_len + BAND_SPAN], "tm", distance + 1)
    col_best = (
        jnp.maximum(
            returned,
            jnp.concatenate([returned_head, jnp.zeros((block_len - BAND_SPAN,), jnp.float32)]),
        )
        - 1.0
    )
    return lax.pmax((row_best.reshape(block_len), col_best), "band")


SLOTS = 4
LANES = 128


def pair_kernel(
    blocks,
    starts_in,
    x_ref,
    tail_ref,
    both_out,
    starts_ref,
    ext,
    rows_x,
    rows_back,
    shifted,
    stats,
    across,
    row_z,
    col_z,
    col_buf,
    row_res,
    col_res,
    slots,
    carry_in,
    local,
    in_send,
    in_recv,
    out_send,
    row_recv,
    slot_recv,
    carry_recv,
):
    half = BAND_BLOCKS
    block_rows = x_ref.shape[0]
    quarter = block_rows // SLOTS
    piece = 2 * quarter + 8
    band_count = starts_ref.shape[0]
    row_out = both_out.at[pl.ds(0, block_rows), :]
    col_out = both_out.at[pl.ds(block_rows, block_rows), :]
    p = lax.axis_index("tm")
    b = lax.axis_index("band")
    low = p < half
    high = p >= half
    partner = lax.rem(p + half, blocks)
    part = b + 2 * (p // half)
    first = 2 * quarter + quarter * b

    def remote(src, dst, send, recv, tm, band):
        return pltpu.make_async_remote_copy(
            src_ref=src,
            dst_ref=dst,
            send_sem=send,
            recv_sem=recv,
            device_id={"tm": tm, "band": band},
            device_id_type=pl.DeviceIdType.MESH,
        )

    head_sender = jnp.logical_and(p >= b, p < half + b)
    next_sender = p > half
    next_taker = jnp.logical_and(high, p < blocks - 1)
    carry_sender = jnp.logical_and(next_taker, b == 1)
    carry_taker = next_sender

    barrier = pltpu.get_barrier_semaphore()

    def greet(tm, band):
        pl.semaphore_signal(
            barrier, 1, device_id={"tm": tm, "band": band}, device_id_type=pl.DeviceIdType.MESH
        )

    greet(p, 1 - b)
    greet(partner, 0)
    greet(partner, 1)

    @pl.when(jnp.logical_and(high, b == 1))
    def _():
        greet(p - half + 1, 1)

    @pl.when(next_taker)
    def _():
        greet(p + 1, b)

    @pl.when(carry_taker)
    def _():
        greet(p - 1, 1)

    starts_copy = pltpu.make_async_copy(starts_in, starts_ref, local.at[0])
    own_rows = pltpu.make_async_copy(
        x_ref.at[pl.ds(pl.multiple_of(quarter * b, 8), quarter + 8), :], rows_x, local.at[1]
    )
    own_cols = pltpu.make_async_copy(
        x_ref.at[pl.ds(2 * quarter, 2 * quarter), :],
        ext.at[pl.ds(2 * quarter, 2 * quarter), :],
        local.at[1],
    )
    own_tail = pltpu.make_async_copy(
        tail_ref, ext.at[pl.ds(block_rows, M // LANES), :], local.at[2]
    )
    starts_copy.start()
    pl.when(low)(own_rows.start)
    pl.when(high)(own_cols.start)

    @pl.when(p == blocks - 1)
    def _():
        ext[pl.ds(block_rows, quarter + 8), :] = jnp.zeros((quarter + 8, LANES), jnp.float32)
        own_tail.start()

    col_buf[...] = jnp.full(col_buf.shape, -1.0, jnp.float32)

    @pl.when(low)
    def _():
        col_out[...] = jnp.full(col_out.shape, -1.0, jnp.float32)

    @pl.when(high)
    def _():
        row_out[...] = jnp.full(row_out.shape, -1.0, jnp.float32)

    head_here = jnp.where(jnp.logical_and(b == 1, jnp.logical_and(p >= 1, p <= half)), 1, 0)
    next_here = jnp.where(next_sender, 1, 0)
    carry_here = jnp.where(carry_sender, 2, 0)
    pl.semaphore_wait(barrier, 3 + head_here + next_here + carry_here)

    cols_copy = remote(
        x_ref.at[pl.ds(pl.multiple_of(quarter * b, 8), piece), :],
        ext.at[pl.ds(pl.multiple_of(first, 8), piece), :],
        in_send.at[0],
        in_recv.at[0],
        partner,
        b,
    )
    rows_copy = remote(
        x_ref.at[pl.ds(pl.multiple_of(first, 8), quarter), :],
        rows_x.at[pl.ds(0, quarter), :],
        in_send.at[1],
        in_recv.at[1],
        partner,
        b,
    )
    head_copy = remote(
        x_ref.at[pl.ds(pl.multiple_of(3 * quarter * (1 - b), 8), 8), :],
        rows_x.at[pl.ds(quarter, 8), :],
        in_send.at[2],
        in_recv.at[2],
        lax.rem(p + half - b, blocks),
        b,
    )
    next_copy = remote(
        x_ref.at[pl.ds(0, quarter + 8), :],
        ext.at[pl.ds(block_rows, quarter + 8), :],
        in_send.at[3],
        in_recv.at[3],
        lax.rem(p + blocks - 1, blocks),
        b,
    )
    pl.when(high)(cols_copy.start)
    pl.when(low)(rows_copy.start)
    pl.when(head_sender)(head_copy.start)
    pl.when(next_sender)(next_copy.start)

    starts_copy.wait()
    span = quarter + 8
    lane = lax.broadcasted_iota(jnp.int32, (span, LANES), 1)

    def moments_of(samples):
        mean, spread = samples, None
        width = 1

        def ahead(values):
            below = pltpu.roll(values, span - 1, 0)
            if width == LANES:
                return below
            turned = pltpu.roll(values, LANES - width, 1)
            return jnp.where(lane < LANES - width, turned, pltpu.roll(turned, span - 1, 0))

        while width < M:
            other = ahead(mean)
            gap = mean - other
            term = gap * gap * (0.5 * width)
            spread = term if spread is None else spread + ahead(spread) + term
            mean = 0.5 * (mean + other)
            width *= 2
        return mean, lax.rsqrt(spread + M * EPS)

    square = (LANES, LANES)
    upper = lax.broadcasted_iota(jnp.int32, square, 1) <= lax.broadcasted_iota(jnp.int32, square, 0)
    keep = lax.broadcasted_iota(jnp.int32, square, 1) >= lax.broadcasted_iota(jnp.int32, square, 0)

    def turned_row(source, index):
        line = source[pl.ds(index, 1), :]
        return pltpu.roll(jnp.broadcast_to(line, square), 1, 1, stride=1, stride_axis=0)


    def steps_of(line, begin):
        few = pltpu.roll(jnp.broadcast_to(line, (8, LANES)), begin, 1, stride=1, stride_axis=0)
        turns = [few] + [pltpu.roll(few, top, 1) for top in range(8, LANES, 8)]
        return jnp.concatenate(turns, axis=0)

    def build_rows():
        samples = rows_x[...]
        mean, factor = moments_of(samples)
        across[0] = mean[:quarter].T
        across[1] = factor[:quarter].T
        flip = jnp.where(
            lax.broadcasted_iota(jnp.int32, square, 0) + lax.broadcasted_iota(jnp.int32, square, 1)
            == LANES - 1,
            1.0,
            0.0,
        ).astype(jnp.bfloat16)
        left = samples
        back = None
        for _ in range(3):
            some = left.astype(jnp.bfloat16)
            left = left - some.astype(jnp.float32)
            moved = jnp.dot(some, flip, preferred_element_type=jnp.float32)
            back = moved if back is None else back + moved
        rows_back[...] = back

        def turned(index):
            line = rows_back[pl.ds(index, 1), :]
            return steps_of(line, 0)

        turn = turned(1)
        near = jnp.where(keep, turned(0), turn)
        for index in range(quarter):
            following = turned(index + 2)
            far = jnp.where(keep, turn, following)
            c = across[0, :, index : index + 1]
            f = across[1, :, index : index + 1]
            row_z[index, :, :LANES] = ((near - c) * f).astype(jnp.bfloat16)
            row_z[index, :, LANES:] = ((far - c) * f).astype(jnp.bfloat16)
            turn, near = following, far

    starts = [starts_ref[c] for c in range(band_count)]
    whole = [lax.shift_right_logical(s, 7) for s in starts]
    rest = [lax.bitwise_and(s, LANES - 1) for s in starts]

    def build_cols():
        for c in range(band_count):
            back = lax.rem(LANES - rest[c], LANES)
            here = pltpu.roll(ext[pl.ds(first + whole[c], span), :], back, 1)
            below = pltpu.roll(ext[pl.ds(first + whole[c] + 1, span), :], back, 1)
            samples = jnp.where(lane < LANES - rest[c], here, below)
            shifted[c] = samples
            mean, factor = moments_of(samples)
            stats[2 * c] = mean
            stats[2 * c + 1] = factor

        def turned(c, index):
            line = shifted[c, pl.ds(index, 1), :]
            return steps_of(line, 1)

        def one_band(c, _):
            turn0 = turned(c, 0)
            turn1 = turned(c, 1)

            def step(index, state):
                turn, near = state
                following = turned(c, index + 2)
                far = jnp.where(upper, turn, following)
                center = stats[2 * c, pl.ds(index, 1), :]
                factor = stats[2 * c + 1, pl.ds(index, 1), :]
                col_z[c, index, :LANES, :] = ((near - center) * factor).astype(jnp.bfloat16)
                col_z[c, index, LANES:, :] = ((far - center) * factor).astype(jnp.bfloat16)
                return following, far

            lax.fori_loop(
                0, quarter + 1, step, (turn1, jnp.where(upper, turn0, turn1)), unroll=33
            )
            return 0

        lax.fori_loop(0, band_count, one_band, 0)

    def phase(turn, _):
        rows_now = lax.rem(turn + p // half, 2) == 0

        @pl.when(rows_now)
        def _():
            pl.when(low)(own_rows.wait)

            @pl.when(high)
            def _():
                rows_copy.wait_recv()
                head_copy.wait_recv()

            build_rows()

        @pl.when(jnp.logical_not(rows_now))
        def _():
            pl.when(low)(cols_copy.wait_recv)
            pl.when(high)(own_cols.wait)
            pl.when(next_taker)(next_copy.wait_recv)
            pl.when(p == blocks - 1)(own_tail.wait)
            build_cols()

        return 0

    lax.fori_loop(0, 2, phase, 0)

    last_block = lax.rem(p, half) + half
    room_all = (blocks - last_block) * block_rows * LANES - part * quarter * LANES
    lane_row = lax.broadcasted_iota(jnp.int32, (1, LANES), 1)

    lane_square = lax.broadcasted_iota(jnp.int32, square, 1)

    def score(index, state):
        pending, rows_found = state
        best = None
        left = []
        for c in range(band_count):
            both = jnp.concatenate([col_z[c, index], col_z[c, index + 1]], axis=1)
            found = jnp.dot(row_z[index], both, preferred_element_type=jnp.float32)
            room = room_all - starts[c] - index * LANES
            near = found[:, :LANES] + jnp.where(lane_row < room, 0.0, -4.0)
            far = found[:, LANES:] + jnp.where(lane_row + LANES < room, 0.0, -4.0)
            near_cols = jnp.max(jnp.where(keep, near, -4.0), axis=0, keepdims=True)
            far_cols = jnp.max(jnp.where(keep, -4.0, far), axis=0, keepdims=True)
            col_buf[c, pl.ds(quarter + index, 1), :] = jnp.maximum(
                jnp.maximum(pending[c], near_cols), -1.0
            )
            left.append(jnp.maximum(far_cols, -1.0))
            joined = jnp.where(keep, near, far)
            best = joined if best is None else jnp.maximum(best, joined)
        rows_found = jnp.where(
            lane_square == index, jnp.max(best, axis=1, keepdims=True), rows_found
        )
        return tuple(left), rows_found

    floor = jnp.full((1, LANES), -1.0, jnp.float32)
    pending, rows_found = lax.fori_loop(
        0, quarter, score, ((floor,) * band_count, jnp.full(square, -1.0, jnp.float32)), unroll=16
    )
    lane_wide = lax.broadcasted_iota(jnp.int32, (2 * quarter, LANES), 1)
    reached = None
    for c in range(band_count):
        col_buf[c, pl.ds(2 * quarter, 1), :] = pending[c]
        here = pltpu.roll(col_buf[c, pl.ds(quarter - whole[c], 2 * quarter), :], rest[c], 1)
        above = pltpu.roll(col_buf[c, pl.ds(quarter - whole[c] - 1, 2 * quarter), :], rest[c], 1)
        placed = jnp.where(lane_wide >= rest[c], here, above)
        reached = placed if reached is None else jnp.maximum(reached, placed)
    col_res[...] = reached

    place = pl.ds(pl.multiple_of(part * quarter, 8), quarter)
    row_to = [
        remote(row_res, row_out.at[place, :], out_send.at[k], row_recv.at[part], tm, band)
        for k, (tm, band) in enumerate([(p, 1 - b), (partner, 0), (partner, 1)])
    ]
    slot_to = [
        remote(col_res, slots.at[part], out_send.at[3 + k], slot_recv.at[part], tm, band)
        for k, (tm, band) in enumerate([(p, 1 - b), (partner, 0), (partner, 1)])
    ]
    lower = pl.ds(0, quarter)
    lower_to = remote(
        col_res.at[lower, :],
        slots.at[part, lower, :],
        out_send.at[3],
        slot_recv.at[part],
        p,
        1 - b,
    )
    carry_to = [
        remote(
            col_res.at[pl.ds(quarter, quarter), :],
            carry_in,
            out_send.at[6 + k],
            carry_recv.at[0],
            lax.rem(p + 1, blocks),
            k,
        )
        for k in range(2)
    ]

    @pl.when(low)
    def _():
        slot_to[1].start()
        slot_to[2].start()

    @pl.when(carry_sender)
    def _():
        carry_to[0].start()
        carry_to[1].start()

    @pl.when(jnp.logical_and(high, b == 0))
    def _():
        slot_to[0].start()
        slots[2] = col_res[...]

    @pl.when(jnp.logical_and(high, b == 1))
    def _():
        lower_to.start()
        slots[3, lower, :] = col_res[lower, :]

    row_res[...] = jnp.maximum(rows_found.T[:quarter], -1.0)

    @pl.when(low)
    def _():
        row_to[0].start()
        row_out[place, :] = row_res[...]

    @pl.when(high)
    def _():
        row_to[1].start()
        row_to[2].start()

    def row_from(index):
        return remote(
            row_res,
            row_out.at[pl.ds(index * quarter, quarter), :],
            out_send.at[0],
            row_recv.at[index],
            p,
            1 - b,
        )

    def slot_from(index):
        return remote(
            col_res, slots.at[index], out_send.at[0], slot_recv.at[index], p, 1 - b
        )

    @pl.when(low)
    def _():
        pl.when(b == 1)(row_from(0).wait_recv)
        pl.when(b == 0)(row_from(1).wait_recv)
        row_from(2).wait_recv()
        row_from(3).wait_recv()

    @pl.when(high)
    def _():
        slot_from(0).wait_recv()
        slot_from(1).wait_recv()

    @pl.when(jnp.logical_and(high, b == 1))
    def _():
        slot_from(2).wait_recv()

    @pl.when(jnp.logical_and(high, b == 0))
    def _():
        remote(
            col_res.at[lower, :],
            slots.at[3, lower, :],
            out_send.at[0],
            slot_recv.at[3],
            p,
            1 - b,
        ).wait_recv()

    pl.when(carry_taker)(carry_to[0].wait_recv)

    @pl.when(p == half)
    def _():
        carry_in[...] = jnp.full(carry_in.shape, -1.0, jnp.float32)

    @pl.when(high)
    def _():
        col_out[pl.ds(0, quarter), :] = jnp.maximum(slots[0, lower, :], carry_in[...])
        for k in range(1, SLOTS):
            col_out[pl.ds(k * quarter, quarter), :] = jnp.maximum(
                slots[k, lower, :], slots[k - 1, pl.ds(quarter, quarter), :]
            )

    @pl.when(high)
    def _():
        cols_copy.wait_send()
        row_to[1].wait_send()
        row_to[2].wait_send()

    @pl.when(low)
    def _():
        rows_copy.wait_send()
        slot_to[1].wait_send()
        slot_to[2].wait_send()
        row_to[0].wait_send()

    pl.when(head_sender)(head_copy.wait_send)
    pl.when(next_sender)(next_copy.wait_send)
    pl.when(jnp.logical_and(high, b == 0))(slot_to[0].wait_send)
    pl.when(jnp.logical_and(high, b == 1))(lower_to.wait_send)

    @pl.when(carry_sender)
    def _():
        carry_to[0].wait_send()
        carry_to[1].wait_send()


def spread_body(series, tail, band_starts):
    block_rows = series.shape[0] // LANES
    quarter = block_rows // SLOTS
    band_count = band_starts.shape[0]
    blocks = lax.axis_size("tm")
    span = quarter + 8
    vmem = pl.BlockSpec(memory_space=pltpu.VMEM)
    length = series.shape[0]
    outputs = jax.ShapeDtypeStruct((2 * block_rows, LANES), jnp.float32)

    operands = (band_starts, series.reshape(block_rows, LANES), tail.reshape(-1, LANES))

    def buffer(*shape, kind=jnp.float32):
        return pltpu.VMEM(shape, kind)

    both = pl.pallas_call(
        functools.partial(pair_kernel, blocks),
        out_shape=outputs,
        in_specs=[pl.BlockSpec(memory_space=pltpu.HBM)] * 3,
        out_specs=vmem,
        scratch_shapes=[
            pltpu.SMEM((band_count,), jnp.int32),
            buffer(block_rows + span, LANES),
            buffer(span, LANES),
            buffer(span, LANES),
            buffer(band_count, span, LANES),
            buffer(2 * band_count, span, LANES),
            buffer(2, LANES, quarter),
            buffer(quarter, LANES, M, kind=jnp.bfloat16),
            buffer(band_count, quarter + 1, M, LANES, kind=jnp.bfloat16),
            buffer(band_count, 3 * quarter + 8, LANES),
            buffer(quarter, LANES),
            buffer(2 * quarter, LANES),
            buffer(SLOTS, 2 * quarter, LANES),
            buffer(quarter, LANES),
            pltpu.SemaphoreType.DMA((3,)),
            pltpu.SemaphoreType.DMA((4,)),
            pltpu.SemaphoreType.DMA((4,)),
            pltpu.SemaphoreType.DMA((8,)),
            pltpu.SemaphoreType.DMA((SLOTS,)),
            pltpu.SemaphoreType.DMA((SLOTS,)),
            pltpu.SemaphoreType.DMA((1,)),
        ],
        compiler_params=pltpu.CompilerParams(
            collective_id=0, has_side_effects=True, vmem_limit_bytes=40 * 1024 * 1024
        ),
        name="banded_pairs",
    )(*[pltpu.with_memory_space_constraint(a, pltpu.HBM) for a in operands])
    flat = both.reshape(-1)
    return flat[:length], flat[length:]


def solution(mesh):
    placed = (P(("groups", "tm")), P("groups"), P("groups"))

    def chosen(series, tail, band_starts):
        halves = lax.axis_size("tm") == 2 * BAND_BLOCKS
        if halves and series.shape[0] == SLOTS * BAND_SPAN and lax.axis_size("band") == 2:
            return spread_body(series, tail, band_starts)
        return body(series, tail, band_starts)

    return jax.shard_map(
        chosen,
        mesh=mesh,
        in_specs=placed,
        out_specs=(P(("groups", "tm")), P(("groups", "tm"))),
        check_vma=False,
    )
```

```python
import functools

import jax
import jax.numpy as jnp
from jax import lax
from jax.experimental import pallas as pl
from jax.experimental.pallas import tpu as pltpu
from jax.sharding import PartitionSpec as P

M = 256
TILE = 128
OFF_DEV = 128
BAND_SPAN = 4096
BAND_BLOCKS = 4


EPS = 1e-06
tile_batch = 16


def from_behind(block, axis, distance):
    devices = range(lax.axis_size(axis))
    route = [(i - distance, i) for i in devices if i - distance in devices]
    return lax.ppermute(block, axis, route)


def hankel(samples, tile_count):
    length = tile_count * TILE + M
    shifted = jnp.stack(
        [lax.slice_in_dim(samples, offset, offset + length) for offset in range(TILE)]
    )
    blocks = shifted.reshape(TILE, length // TILE, TILE)
    joined = jnp.concatenate(
        [blocks[:, stride : stride + tile_count] for stride in range(M // TILE)], axis=2
    )
    return jnp.swapaxes(joined, 0, 1)


def moments(matrix):
    center = jnp.mean(matrix, axis=-1)
    spread = matrix - center[..., None]
    factor = lax.rsqrt(jnp.sum(spread * spread, axis=-1) + M * EPS)
    return (center, factor)


def normed(matrix, center, factor):
    return ((matrix - center[..., None]) * factor[..., None]).astype(jnp.bfloat16)


def score_group(row_z, col_z, room_left):
    tile_count = row_z.shape[0]
    near_scores = jnp.einsum("tim,tjm->tij", row_z, col_z[:-1], preferred_element_type=jnp.float32)
    far_scores = jnp.einsum(
        "tim,tjm->tij", row_z, col_z[1:, :OFF_DEV], preferred_element_type=jnp.float32
    )
    row_near = lax.broadcasted_iota(jnp.int32, (TILE, TILE), 0)
    col_near = lax.broadcasted_iota(jnp.int32, (TILE, TILE), 1)
    row_far = lax.broadcasted_iota(jnp.int32, (TILE, OFF_DEV), 0)
    col_far = lax.broadcasted_iota(jnp.int32, (TILE, OFF_DEV), 1)
    tile_index = jnp.arange(tile_count, dtype=jnp.int32)[:, None, None]
    keep_near = (
        (col_near >= row_near)[None]
        & (col_near - row_near < OFF_DEV)[None]
        & (tile_index * TILE + col_near[None] < room_left)
    )
    keep_far = (TILE + col_far - row_far < OFF_DEV)[None] & (
        (tile_index + 1) * TILE + col_far[None] < room_left
    )
    near_scores = jnp.where(keep_near, near_scores, -1.0)
    far_scores = jnp.where(keep_far, far_scores, -1.0)
    best_rows = jnp.maximum(near_scores.max(axis=2), far_scores.max(axis=2)).reshape(-1)
    floor_row = jnp.full((1, TILE), -1.0, jnp.float32)
    upper_part = jnp.concatenate([near_scores.max(axis=1), floor_row], axis=0)
    far_cols = far_scores.max(axis=1)
    lower_part = jnp.concatenate([floor_row, far_cols], axis=0)
    return (best_rows, jnp.maximum(upper_part, lower_part).reshape(-1))


def place_columns(col_groups, start, buffer_len):
    group_rows = tile_batch * TILE
    count = col_groups.shape[0]
    main_part = col_groups[:, :group_rows].reshape(-1)
    carry_part = jnp.concatenate(
        [col_groups[:, group_rows:], jnp.full((count, group_rows - TILE), -1.0, jnp.float32)],
        axis=1,
    ).reshape(-1)
    shifted = jnp.concatenate([jnp.full((group_rows,), -1.0, jnp.float32), carry_part])[
        : count * group_rows + TILE
    ]
    reached = jnp.maximum(
        jnp.concatenate([main_part, jnp.full((TILE,), -1.0, jnp.float32)]), shifted
    )
    buffer_all = jnp.full((buffer_len,), -1.0, jnp.float32)
    return lax.dynamic_update_slice(buffer_all, reached, (start,))


def body(series, tail, band_starts):
    block_len = series.shape[0]
    group_rows = tile_batch * TILE
    group_count = block_len // group_rows
    position = lax.axis_index("tm")
    devices = lax.axis_size("tm")
    distance = BAND_BLOCKS
    following = from_behind(series[:M], "tm", -1)
    following = jnp.where(position == devices - 1, tail, following)
    extended = jnp.concatenate([series, following])
    row_source = jnp.concatenate([extended, jnp.zeros((TILE,), jnp.float32)])

    def own_group(group_index):
        row_piece = lax.dynamic_slice_in_dim(
            row_source, group_index * group_rows, group_rows + M + TILE
        )
        matrix = hankel(row_piece, tile_batch)
        center, factor = moments(matrix)
        return (center.reshape(-1), factor.reshape(-1), normed(matrix, center, factor))

    centers, factors, row_z = lax.map(own_group, jnp.arange(group_count, dtype=jnp.int32))
    centers = centers.reshape(block_len)
    factors = factors.reshape(block_len)
    padding = jnp.zeros((2 * TILE,), jnp.float32)
    far_samples = from_behind(extended, "tm", -distance)
    next_samples = from_behind(series[M : M + BAND_SPAN], "tm", -distance - 1)
    pair_samples = jnp.concatenate([far_samples, next_samples, padding])
    buffer_len = block_len + BAND_SPAN + TILE
    band_count = band_starts.shape[0]
    band_here = lax.axis_index("band")
    offset_start = jnp.sum(
        jnp.where(jnp.arange(band_count, dtype=jnp.int32) == band_here, band_starts, 0)
    )
    room_all = (devices - position - distance) * block_len - offset_start

    def pair_group(inputs):
        group_index, group_z = inputs
        col_begin = offset_start + group_index * group_rows
        col_piece = lax.dynamic_slice_in_dim(pair_samples, col_begin, (tile_batch + 2) * TILE + M)
        matrix = hankel(col_piece, tile_batch + 1)
        center, factor = moments(matrix)
        col_z = normed(matrix, center, factor)
        return score_group(group_z, col_z, room_all - group_index * group_rows)

    row_best, col_groups = lax.map(pair_group, (jnp.arange(group_count, dtype=jnp.int32), row_z))
    lifted = place_columns(col_groups, offset_start, buffer_len) + 1.0
    returned = from_behind(lifted[:block_len], "tm", distance)
    returned_head = from_behind(lifted[block_len : block_len + BAND_SPAN], "tm", distance + 1)
    col_best = (
        jnp.maximum(
            returned,
            jnp.concatenate([returned_head, jnp.zeros((block_len - BAND_SPAN,), jnp.float32)]),
        )
        - 1.0
    )
    return lax.pmax((row_best.reshape(block_len), col_best), "band")


SLOTS = 4
LANES = 128


def pair_kernel(
    blocks,
    starts_in,
    x_ref,
    tail_ref,
    both_out,
    starts_ref,
    ext,
    rows_x,
    rows_back,
    shifted,
    stats,
    across,
    row_z,
    col_z,
    col_buf,
    row_res,
    col_res,
    slots,
    carry_in,
    local,
    in_send,
    in_recv,
    out_send,
    row_recv,
    slot_recv,
    carry_recv,
):
    half = BAND_BLOCKS
    block_rows = x_ref.shape[0]
    quarter = block_rows // SLOTS
    piece = 2 * quarter + 8
    band_count = starts_ref.shape[0]
    row_out = both_out.at[pl.ds(0, block_rows), :]
    col_out = both_out.at[pl.ds(block_rows, block_rows), :]
    p = lax.axis_index("tm")
    b = lax.axis_index("band")
    low = p < half
    high = p >= half
    partner = lax.rem(p + half, blocks)
    part = b + 2 * (p // half)
    first = 2 * quarter + quarter * b

    def remote(src, dst, send, recv, tm, band):
        return pltpu.make_async_remote_copy(
            src_ref=src,
            dst_ref=dst,
            send_sem=send,
            recv_sem=recv,
            device_id={"tm": tm, "band": band},
            device_id_type=pl.DeviceIdType.MESH,
        )

    head_sender = jnp.logical_and(p >= b, p < half + b)
    next_sender = p > half
    next_taker = jnp.logical_and(high, p < blocks - 1)
    carry_sender = jnp.logical_and(next_taker, b == 1)
    carry_taker = next_sender

    barrier = pltpu.get_barrier_semaphore()

    def greet(tm, band):
        pl.semaphore_signal(
            barrier, 1, device_id={"tm": tm, "band": band}, device_id_type=pl.DeviceIdType.MESH
        )

    greet(p, 1 - b)
    greet(partner, 0)
    greet(partner, 1)

    @pl.when(jnp.logical_and(high, b == 1))
    def _():
        greet(p - half + 1, 1)

    @pl.when(next_taker)
    def _():
        greet(p + 1, b)

    @pl.when(carry_taker)
    def _():
        greet(p - 1, 1)

    starts_copy = pltpu.make_async_copy(starts_in, starts_ref, local.at[0])
    own_rows = pltpu.make_async_copy(
        x_ref.at[pl.ds(pl.multiple_of(quarter * b, 8), quarter + 8), :], rows_x, local.at[1]
    )
    own_cols = pltpu.make_async_copy(
        x_ref.at[pl.ds(2 * quarter, 2 * quarter), :],
        ext.at[pl.ds(2 * quarter, 2 * quarter), :],
        local.at[1],
    )
    own_tail = pltpu.make_async_copy(
        tail_ref, ext.at[pl.ds(block_rows, M // LANES), :], local.at[2]
    )
    starts_copy.start()
    pl.when(low)(own_rows.start)
    pl.when(high)(own_cols.start)

    @pl.when(p == blocks - 1)
    def _():
        ext[pl.ds(block_rows, quarter + 8), :] = jnp.zeros((quarter + 8, LANES), jnp.float32)
        own_tail.start()

    col_buf[...] = jnp.full(col_buf.shape, -1.0, jnp.float32)

    @pl.when(low)
    def _():
        col_out[...] = jnp.full(col_out.shape, -1.0, jnp.float32)

    @pl.when(high)
    def _():
        row_out[...] = jnp.full(row_out.shape, -1.0, jnp.float32)

    head_here = jnp.where(jnp.logical_and(b == 1, jnp.logical_and(p >= 1, p <= half)), 1, 0)
    next_here = jnp.where(next_sender, 1, 0)
    carry_here = jnp.where(carry_sender, 2, 0)
    pl.semaphore_wait(barrier, 3 + head_here + next_here + carry_here)

    cols_copy = remote(
        x_ref.at[pl.ds(pl.multiple_of(quarter * b, 8), piece), :],
        ext.at[pl.ds(pl.multiple_of(first, 8), piece), :],
        in_send.at[0],
        in_recv.at[0],
        partner,
        b,
    )
    rows_copy = remote(
        x_ref.at[pl.ds(pl.multiple_of(first, 8), quarter), :],
        rows_x.at[pl.ds(0, quarter), :],
        in_send.at[1],
        in_recv.at[1],
        partner,
        b,
    )
    head_copy = remote(
        x_ref.at[pl.ds(pl.multiple_of(3 * quarter * (1 - b), 8), 8), :],
        rows_x.at[pl.ds(quarter, 8), :],
        in_send.at[2],
        in_recv.at[2],
        lax.rem(p + half - b, blocks),
        b,
    )
    next_copy = remote(
        x_ref.at[pl.ds(0, quarter + 8), :],
        ext.at[pl.ds(block_rows, quarter + 8), :],
        in_send.at[3],
        in_recv.at[3],
        lax.rem(p + blocks - 1, blocks),
        b,
    )
    pl.when(high)(cols_copy.start)
    pl.when(low)(rows_copy.start)
    pl.when(head_sender)(head_copy.start)
    pl.when(next_sender)(next_copy.start)

    starts_copy.wait()
    span = quarter + 8
    lane = lax.broadcasted_iota(jnp.int32, (span, LANES), 1)

    def moments_of(samples):
        mean, spread = samples, None
        width = 1

        def ahead(values):
            below = pltpu.roll(values, span - 1, 0)
            if width == LANES:
                return below
            turned = pltpu.roll(values, LANES - width, 1)
            return jnp.where(lane < LANES - width, turned, pltpu.roll(turned, span - 1, 0))

        while width < M:
            other = ahead(mean)
            gap = mean - other
            term = gap * gap * (0.5 * width)
            spread = term if spread is None else spread + ahead(spread) + term
            mean = 0.5 * (mean + other)
            width *= 2
        return mean, lax.rsqrt(spread + M * EPS)

    square = (LANES, LANES)
    upper = lax.broadcasted_iota(jnp.int32, square, 1) <= lax.broadcasted_iota(jnp.int32, square, 0)
    keep = lax.broadcasted_iota(jnp.int32, square, 1) >= lax.broadcasted_iota(jnp.int32, square, 0)

    def turned_row(source, index):
        line = source[pl.ds(index, 1), :]
        return pltpu.roll(jnp.broadcast_to(line, square), 1, 1, stride=1, stride_axis=0)


    def build_rows():
        samples = rows_x[...]
        mean, factor = moments_of(samples)
        for side, values in enumerate((mean[:quarter], factor[:quarter])):
            left = values
            pieces = []
            for _ in range(3):
                some = left.astype(jnp.bfloat16).astype(jnp.float32)
                left = left - some
                pieces.append(some)
            pieces.append(jnp.zeros((LANES - 3 * quarter, LANES), jnp.float32))
            turned_pieces = jnp.concatenate(pieces, axis=0).T.astype(jnp.bfloat16)
            across[:, side * LANES : (side + 1) * LANES] = turned_pieces
        wide = (2 * LANES, 2 * LANES)
        ones = jnp.where(
            (lax.broadcasted_iota(jnp.int32, wide, 0) < LANES)
            == (lax.broadcasted_iota(jnp.int32, wide, 1) < LANES),
            1.0,
            0.0,
        ).astype(jnp.bfloat16)
        wide_lane = lax.rem(lax.broadcasted_iota(jnp.int32, (1, 2 * LANES), 1), quarter)
        flip = jnp.where(
            lax.broadcasted_iota(jnp.int32, square, 0) + lax.broadcasted_iota(jnp.int32, square, 1)
            == LANES - 1,
            1.0,
            0.0,
        ).astype(jnp.bfloat16)
        left = samples
        back = None
        for _ in range(3):
            some = left.astype(jnp.bfloat16)
            left = left - some.astype(jnp.float32)
            moved = jnp.dot(some, flip, preferred_element_type=jnp.float32)
            back = moved if back is None else back + moved
        rows_back[...] = back

        def turned(index):
            line = rows_back[pl.ds(index, 1), :]
            return pltpu.roll(jnp.broadcast_to(line, square), 0, 1, stride=1, stride_axis=0)

        turn = turned(1)
        near = jnp.where(keep, turned(0), turn)
        for index in range(quarter):
            following = turned(index + 2)
            far = jnp.where(keep, turn, following)
            pick = jnp.where(wide_lane == index, 1.0, 0.0).astype(jnp.bfloat16)
            spread = jnp.dot(across[...] * pick, ones, preferred_element_type=jnp.float32)
            c = spread[:, :LANES]
            f = spread[:, LANES:]
            row_z[index, :, :LANES] = ((near - c) * f).astype(jnp.bfloat16)
            row_z[index, :, LANES:] = ((far - c) * f).astype(jnp.bfloat16)
            turn, near = following, far

    starts = [starts_ref[c] for c in range(band_count)]
    whole = [lax.shift_right_logical(s, 7) for s in starts]
    rest = [lax.bitwise_and(s, LANES - 1) for s in starts]

    def build_cols():
        for c in range(band_count):
            back = lax.rem(LANES - rest[c], LANES)
            here = pltpu.roll(ext[pl.ds(first + whole[c], span), :], back, 1)
            below = pltpu.roll(ext[pl.ds(first + whole[c] + 1, span), :], back, 1)
            samples = jnp.where(lane < LANES - rest[c], here, below)
            shifted[c] = samples
            mean, factor = moments_of(samples)
            stats[2 * c] = mean
            stats[2 * c + 1] = factor

        def turned(c, index):
            line = shifted[c, pl.ds(index, 1), :]
            return pltpu.roll(jnp.broadcast_to(line, square), 1, 1, stride=1, stride_axis=0)

        def one_band(c, _):
            turn0 = turned(c, 0)
            turn1 = turned(c, 1)

            def step(index, state):
                turn, near = state
                following = turned(c, index + 2)
                far = jnp.where(upper, turn, following)
                center = stats[2 * c, pl.ds(index, 1), :]
                factor = stats[2 * c + 1, pl.ds(index, 1), :]
                col_z[c, index, :LANES, :] = ((near - center) * factor).astype(jnp.bfloat16)
                col_z[c, index, LANES:, :] = ((far - center) * factor).astype(jnp.bfloat16)
                return following, far

            lax.fori_loop(
                0, quarter + 1, step, (turn1, jnp.where(upper, turn0, turn1)), unroll=33
            )
            return 0

        lax.fori_loop(0, band_count, one_band, 0)

    def phase(turn, _):
        rows_now = lax.rem(turn + p // half, 2) == 0

        @pl.when(rows_now)
        def _():
            pl.when(low)(own_rows.wait)

            @pl.when(high)
            def _():
                rows_copy.wait_recv()
                head_copy.wait_recv()

            build_rows()

        @pl.when(jnp.logical_not(rows_now))
        def _():
            pl.when(low)(cols_copy.wait_recv)
            pl.when(high)(own_cols.wait)
            pl.when(next_taker)(next_copy.wait_recv)
            pl.when(p == blocks - 1)(own_tail.wait)
            build_cols()

        return 0

    lax.fori_loop(0, 2, phase, 0)

    last_block = lax.rem(p, half) + half
    room_all = (blocks - last_block) * block_rows * LANES - part * quarter * LANES
    lane_row = lax.broadcasted_iota(jnp.int32, (1, LANES), 1)

    lane_square = lax.broadcasted_iota(jnp.int32, square, 1)

    def score(index, state):
        pending, rows_found = state
        best = None
        left = []
        for c in range(band_count):
            both = jnp.concatenate([col_z[c, index], col_z[c, index + 1]], axis=1)
            found = jnp.dot(row_z[index], both, preferred_element_type=jnp.float32)
            room = room_all - starts[c] - index * LANES
            near = found[:, :LANES] + jnp.where(lane_row < room, 0.0, -4.0)
            far = found[:, LANES:] + jnp.where(lane_row + LANES < room, 0.0, -4.0)
            near_cols = jnp.max(jnp.where(keep, near, -4.0), axis=0, keepdims=True)
            far_cols = jnp.max(jnp.where(keep, -4.0, far), axis=0, keepdims=True)
            col_buf[c, pl.ds(quarter + index, 1), :] = jnp.maximum(
                jnp.maximum(pending[c], near_cols), -1.0
            )
            left.append(jnp.maximum(far_cols, -1.0))
            joined = jnp.where(keep, near, far)
            best = joined if best is None else jnp.maximum(best, joined)
        rows_found = jnp.where(
            lane_square == index, jnp.max(best, axis=1, keepdims=True), rows_found
        )
        return tuple(left), rows_found

    floor = jnp.full((1, LANES), -1.0, jnp.float32)
    pending, rows_found = lax.fori_loop(
        0, quarter, score, ((floor,) * band_count, jnp.full(square, -1.0, jnp.float32)), unroll=16
    )
    lane_wide = lax.broadcasted_iota(jnp.int32, (2 * quarter, LANES), 1)
    reached = None
    for c in range(band_count):
        col_buf[c, pl.ds(2 * quarter, 1), :] = pending[c]
        here = pltpu.roll(col_buf[c, pl.ds(quarter - whole[c], 2 * quarter), :], rest[c], 1)
        above = pltpu.roll(col_buf[c, pl.ds(quarter - whole[c] - 1, 2 * quarter), :], rest[c], 1)
        placed = jnp.where(lane_wide >= rest[c], here, above)
        reached = placed if reached is None else jnp.maximum(reached, placed)
    col_res[...] = reached

    place = pl.ds(pl.multiple_of(part * quarter, 8), quarter)
    row_to = [
        remote(row_res, row_out.at[place, :], out_send.at[k], row_recv.at[part], tm, band)
        for k, (tm, band) in enumerate([(p, 1 - b), (partner, 0), (partner, 1)])
    ]
    slot_to = [
        remote(col_res, slots.at[part], out_send.at[3 + k], slot_recv.at[part], tm, band)
        for k, (tm, band) in enumerate([(p, 1 - b), (partner, 0), (partner, 1)])
    ]
    lower = pl.ds(0, quarter)
    lower_to = remote(
        col_res.at[lower, :],
        slots.at[part, lower, :],
        out_send.at[3],
        slot_recv.at[part],
        p,
        1 - b,
    )
    carry_to = [
        remote(
            col_res.at[pl.ds(quarter, quarter), :],
            carry_in,
            out_send.at[6 + k],
            carry_recv.at[0],
            lax.rem(p + 1, blocks),
            k,
        )
        for k in range(2)
    ]

    @pl.when(low)
    def _():
        slot_to[1].start()
        slot_to[2].start()

    @pl.when(carry_sender)
    def _():
        carry_to[0].start()
        carry_to[1].start()

    @pl.when(jnp.logical_and(high, b == 0))
    def _():
        slot_to[0].start()
        slots[2] = col_res[...]

    @pl.when(jnp.logical_and(high, b == 1))
    def _():
        lower_to.start()
        slots[3, lower, :] = col_res[lower, :]

    row_res[...] = jnp.maximum(rows_found.T[:quarter], -1.0)

    @pl.when(low)
    def _():
        row_to[0].start()
        row_out[place, :] = row_res[...]

    @pl.when(high)
    def _():
        row_to[1].start()
        row_to[2].start()

    def row_from(index):
        return remote(
            row_res,
            row_out.at[pl.ds(index * quarter, quarter), :],
            out_send.at[0],
            row_recv.at[index],
            p,
            1 - b,
        )

    def slot_from(index):
        return remote(
            col_res, slots.at[index], out_send.at[0], slot_recv.at[index], p, 1 - b
        )

    @pl.when(low)
    def _():
        pl.when(b == 1)(row_from(0).wait_recv)
        pl.when(b == 0)(row_from(1).wait_recv)
        row_from(2).wait_recv()
        row_from(3).wait_recv()

    @pl.when(high)
    def _():
        slot_from(0).wait_recv()
        slot_from(1).wait_recv()

    @pl.when(jnp.logical_and(high, b == 1))
    def _():
        slot_from(2).wait_recv()

    @pl.when(jnp.logical_and(high, b == 0))
    def _():
        remote(
            col_res.at[lower, :],
            slots.at[3, lower, :],
            out_send.at[0],
            slot_recv.at[3],
            p,
            1 - b,
        ).wait_recv()

    pl.when(carry_taker)(carry_to[0].wait_recv)

    @pl.when(p == half)
    def _():
        carry_in[...] = jnp.full(carry_in.shape, -1.0, jnp.float32)

    @pl.when(high)
    def _():
        col_out[pl.ds(0, quarter), :] = jnp.maximum(slots[0, lower, :], carry_in[...])
        for k in range(1, SLOTS):
            col_out[pl.ds(k * quarter, quarter), :] = jnp.maximum(
                slots[k, lower, :], slots[k - 1, pl.ds(quarter, quarter), :]
            )

    @pl.when(high)
    def _():
        cols_copy.wait_send()
        row_to[1].wait_send()
        row_to[2].wait_send()

    @pl.when(low)
    def _():
        rows_copy.wait_send()
        slot_to[1].wait_send()
        slot_to[2].wait_send()
        row_to[0].wait_send()

    pl.when(head_sender)(head_copy.wait_send)
    pl.when(next_sender)(next_copy.wait_send)
    pl.when(jnp.logical_and(high, b == 0))(slot_to[0].wait_send)
    pl.when(jnp.logical_and(high, b == 1))(lower_to.wait_send)

    @pl.when(carry_sender)
    def _():
        carry_to[0].wait_send()
        carry_to[1].wait_send()


def spread_body(series, tail, band_starts):
    block_rows = series.shape[0] // LANES
    quarter = block_rows // SLOTS
    band_count = band_starts.shape[0]
    blocks = lax.axis_size("tm")
    span = quarter + 8
    vmem = pl.BlockSpec(memory_space=pltpu.VMEM)
    length = series.shape[0]
    outputs = jax.ShapeDtypeStruct((2 * block_rows, LANES), jnp.float32)

    operands = (band_starts, series.reshape(block_rows, LANES), tail.reshape(-1, LANES))

    def buffer(*shape, kind=jnp.float32):
        return pltpu.VMEM(shape, kind)

    both = pl.pallas_call(
        functools.partial(pair_kernel, blocks),
        out_shape=outputs,
        in_specs=[pl.BlockSpec(memory_space=pltpu.HBM)] * 3,
        out_specs=vmem,
        scratch_shapes=[
            pltpu.SMEM((band_count,), jnp.int32),
            buffer(block_rows + span, LANES),
            buffer(span, LANES),
            buffer(span, LANES),
            buffer(band_count, span, LANES),
            buffer(2 * band_count, span, LANES),
            buffer(LANES, 2 * LANES, kind=jnp.bfloat16),
            buffer(quarter, LANES, M, kind=jnp.bfloat16),
            buffer(band_count, quarter + 1, M, LANES, kind=jnp.bfloat16),
            buffer(band_count, 3 * quarter + 8, LANES),
            buffer(quarter, LANES),
            buffer(2 * quarter, LANES),
            buffer(SLOTS, 2 * quarter, LANES),
            buffer(quarter, LANES),
            pltpu.SemaphoreType.DMA((3,)),
            pltpu.SemaphoreType.DMA((4,)),
            pltpu.SemaphoreType.DMA((4,)),
            pltpu.SemaphoreType.DMA((8,)),
            pltpu.SemaphoreType.DMA((SLOTS,)),
            pltpu.SemaphoreType.DMA((SLOTS,)),
            pltpu.SemaphoreType.DMA((1,)),
        ],
        compiler_params=pltpu.CompilerParams(
            collective_id=0, has_side_effects=True, vmem_limit_bytes=40 * 1024 * 1024
        ),
        name="banded_pairs",
    )(*[pltpu.with_memory_space_constraint(a, pltpu.HBM) for a in operands])
    flat = both.reshape(-1)
    return flat[:length], flat[length:]


def solution(mesh):
    placed = (P(("groups", "tm")), P("groups"), P("groups"))

    def chosen(series, tail, band_starts):
        halves = lax.axis_size("tm") == 2 * BAND_BLOCKS
        if halves and series.shape[0] == SLOTS * BAND_SPAN and lax.axis_size("band") == 2:
            return spread_body(series, tail, band_starts)
        return body(series, tail, band_starts)

    return jax.shard_map(
        chosen,
        mesh=mesh,
        in_specs=placed,
        out_specs=(P(("groups", "tm")), P(("groups", "tm"))),
        check_vma=False,
    )
```

```python
import functools

import jax
import jax.numpy as jnp
from jax import lax
from jax.experimental import pallas as pl
from jax.experimental.pallas import tpu as pltpu
from jax.sharding import PartitionSpec as P

M = 256
TILE = 128
OFF_DEV = 128
BAND_SPAN = 4096
BAND_BLOCKS = 4


EPS = 1e-06
tile_batch = 16


def from_behind(block, axis, distance):
    devices = range(lax.axis_size(axis))
    route = [(i - distance, i) for i in devices if i - distance in devices]
    return lax.ppermute(block, axis, route)


def hankel(samples, tile_count):
    length = tile_count * TILE + M
    shifted = jnp.stack(
        [lax.slice_in_dim(samples, offset, offset + length) for offset in range(TILE)]
    )
    blocks = shifted.reshape(TILE, length // TILE, TILE)
    joined = jnp.concatenate(
        [blocks[:, stride : stride + tile_count] for stride in range(M // TILE)], axis=2
    )
    return jnp.swapaxes(joined, 0, 1)


def moments(matrix):
    center = jnp.mean(matrix, axis=-1)
    spread = matrix - center[..., None]
    factor = lax.rsqrt(jnp.sum(spread * spread, axis=-1) + M * EPS)
    return (center, factor)


def normed(matrix, center, factor):
    return ((matrix - center[..., None]) * factor[..., None]).astype(jnp.bfloat16)


def score_group(row_z, col_z, room_left):
    tile_count = row_z.shape[0]
    near_scores = jnp.einsum("tim,tjm->tij", row_z, col_z[:-1], preferred_element_type=jnp.float32)
    far_scores = jnp.einsum(
        "tim,tjm->tij", row_z, col_z[1:, :OFF_DEV], preferred_element_type=jnp.float32
    )
    row_near = lax.broadcasted_iota(jnp.int32, (TILE, TILE), 0)
    col_near = lax.broadcasted_iota(jnp.int32, (TILE, TILE), 1)
    row_far = lax.broadcasted_iota(jnp.int32, (TILE, OFF_DEV), 0)
    col_far = lax.broadcasted_iota(jnp.int32, (TILE, OFF_DEV), 1)
    tile_index = jnp.arange(tile_count, dtype=jnp.int32)[:, None, None]
    keep_near = (
        (col_near >= row_near)[None]
        & (col_near - row_near < OFF_DEV)[None]
        & (tile_index * TILE + col_near[None] < room_left)
    )
    keep_far = (TILE + col_far - row_far < OFF_DEV)[None] & (
        (tile_index + 1) * TILE + col_far[None] < room_left
    )
    near_scores = jnp.where(keep_near, near_scores, -1.0)
    far_scores = jnp.where(keep_far, far_scores, -1.0)
    best_rows = jnp.maximum(near_scores.max(axis=2), far_scores.max(axis=2)).reshape(-1)
    floor_row = jnp.full((1, TILE), -1.0, jnp.float32)
    upper_part = jnp.concatenate([near_scores.max(axis=1), floor_row], axis=0)
    far_cols = far_scores.max(axis=1)
    lower_part = jnp.concatenate([floor_row, far_cols], axis=0)
    return (best_rows, jnp.maximum(upper_part, lower_part).reshape(-1))


def place_columns(col_groups, start, buffer_len):
    group_rows = tile_batch * TILE
    count = col_groups.shape[0]
    main_part = col_groups[:, :group_rows].reshape(-1)
    carry_part = jnp.concatenate(
        [col_groups[:, group_rows:], jnp.full((count, group_rows - TILE), -1.0, jnp.float32)],
        axis=1,
    ).reshape(-1)
    shifted = jnp.concatenate([jnp.full((group_rows,), -1.0, jnp.float32), carry_part])[
        : count * group_rows + TILE
    ]
    reached = jnp.maximum(
        jnp.concatenate([main_part, jnp.full((TILE,), -1.0, jnp.float32)]), shifted
    )
    buffer_all = jnp.full((buffer_len,), -1.0, jnp.float32)
    return lax.dynamic_update_slice(buffer_all, reached, (start,))


def body(series, tail, band_starts):
    block_len = series.shape[0]
    group_rows = tile_batch * TILE
    group_count = block_len // group_rows
    position = lax.axis_index("tm")
    devices = lax.axis_size("tm")
    distance = BAND_BLOCKS
    following = from_behind(series[:M], "tm", -1)
    following = jnp.where(position == devices - 1, tail, following)
    extended = jnp.concatenate([series, following])
    row_source = jnp.concatenate([extended, jnp.zeros((TILE,), jnp.float32)])

    def own_group(group_index):
        row_piece = lax.dynamic_slice_in_dim(
            row_source, group_index * group_rows, group_rows + M + TILE
        )
        matrix = hankel(row_piece, tile_batch)
        center, factor = moments(matrix)
        return (center.reshape(-1), factor.reshape(-1), normed(matrix, center, factor))

    centers, factors, row_z = lax.map(own_group, jnp.arange(group_count, dtype=jnp.int32))
    centers = centers.reshape(block_len)
    factors = factors.reshape(block_len)
    padding = jnp.zeros((2 * TILE,), jnp.float32)
    far_samples = from_behind(extended, "tm", -distance)
    next_samples = from_behind(series[M : M + BAND_SPAN], "tm", -distance - 1)
    pair_samples = jnp.concatenate([far_samples, next_samples, padding])
    buffer_len = block_len + BAND_SPAN + TILE
    band_count = band_starts.shape[0]
    band_here = lax.axis_index("band")
    offset_start = jnp.sum(
        jnp.where(jnp.arange(band_count, dtype=jnp.int32) == band_here, band_starts, 0)
    )
    room_all = (devices - position - distance) * block_len - offset_start

    def pair_group(inputs):
        group_index, group_z = inputs
        col_begin = offset_start + group_index * group_rows
        col_piece = lax.dynamic_slice_in_dim(pair_samples, col_begin, (tile_batch + 2) * TILE + M)
        matrix = hankel(col_piece, tile_batch + 1)
        center, factor = moments(matrix)
        col_z = normed(matrix, center, factor)
        return score_group(group_z, col_z, room_all - group_index * group_rows)

    row_best, col_groups = lax.map(pair_group, (jnp.arange(group_count, dtype=jnp.int32), row_z))
    lifted = place_columns(col_groups, offset_start, buffer_len) + 1.0
    returned = from_behind(lifted[:block_len], "tm", distance)
    returned_head = from_behind(lifted[block_len : block_len + BAND_SPAN], "tm", distance + 1)
    col_best = (
        jnp.maximum(
            returned,
            jnp.concatenate([returned_head, jnp.zeros((block_len - BAND_SPAN,), jnp.float32)]),
        )
        - 1.0
    )
    return lax.pmax((row_best.reshape(block_len), col_best), "band")


SLOTS = 4
LANES = 128


def pair_kernel(
    blocks,
    starts_in,
    x_ref,
    tail_ref,
    both_out,
    starts_ref,
    ext,
    rows_x,
    rows_back,
    shifted,
    stats,
    across,
    row_z,
    col_z,
    col_buf,
    row_res,
    col_res,
    slots,
    carry_in,
    local,
    in_send,
    in_recv,
    out_send,
    row_recv,
    slot_recv,
    carry_recv,
):
    half = BAND_BLOCKS
    block_rows = x_ref.shape[0]
    quarter = block_rows // SLOTS
    piece = 2 * quarter + 8
    band_count = starts_ref.shape[0]
    row_out = both_out.at[pl.ds(0, block_rows), :]
    col_out = both_out.at[pl.ds(block_rows, block_rows), :]
    p = lax.axis_index("tm")
    b = lax.axis_index("band")
    low = p < half
    high = p >= half
    partner = lax.rem(p + half, blocks)
    part = b + 2 * (p // half)
    first = 2 * quarter + quarter * b

    def remote(src, dst, send, recv, tm, band):
        return pltpu.make_async_remote_copy(
            src_ref=src,
            dst_ref=dst,
            send_sem=send,
            recv_sem=recv,
            device_id={"tm": tm, "band": band},
            device_id_type=pl.DeviceIdType.MESH,
        )

    head_sender = jnp.logical_and(p >= b, p < half + b)
    next_sender = p > half
    next_taker = jnp.logical_and(high, p < blocks - 1)
    carry_sender = jnp.logical_and(next_taker, b == 1)
    carry_taker = next_sender

    barrier = pltpu.get_barrier_semaphore()

    def greet(tm, band):
        pl.semaphore_signal(
            barrier, 1, device_id={"tm": tm, "band": band}, device_id_type=pl.DeviceIdType.MESH
        )

    greet(p, 1 - b)
    greet(partner, 0)
    greet(partner, 1)

    @pl.when(jnp.logical_and(high, b == 1))
    def _():
        greet(p - half + 1, 1)

    @pl.when(next_taker)
    def _():
        greet(p + 1, b)

    @pl.when(carry_taker)
    def _():
        greet(p - 1, 1)

    starts_copy = pltpu.make_async_copy(starts_in, starts_ref, local.at[0])
    own_rows = pltpu.make_async_copy(
        x_ref.at[pl.ds(pl.multiple_of(quarter * b, 8), quarter + 8), :], rows_x, local.at[1]
    )
    own_cols = pltpu.make_async_copy(
        x_ref.at[pl.ds(2 * quarter, 2 * quarter), :],
        ext.at[pl.ds(2 * quarter, 2 * quarter), :],
        local.at[1],
    )
    own_tail = pltpu.make_async_copy(
        tail_ref, ext.at[pl.ds(block_rows, M // LANES), :], local.at[2]
    )
    starts_copy.start()
    pl.when(low)(own_rows.start)
    pl.when(high)(own_cols.start)

    @pl.when(p == blocks - 1)
    def _():
        ext[pl.ds(block_rows, quarter + 8), :] = jnp.zeros((quarter + 8, LANES), jnp.float32)
        own_tail.start()

    col_buf[...] = jnp.full(col_buf.shape, -1.0, jnp.float32)

    @pl.when(low)
    def _():
        col_out[...] = jnp.full(col_out.shape, -1.0, jnp.float32)

    @pl.when(high)
    def _():
        row_out[...] = jnp.full(row_out.shape, -1.0, jnp.float32)

    head_here = jnp.where(jnp.logical_and(b == 1, jnp.logical_and(p >= 1, p <= half)), 1, 0)
    next_here = jnp.where(next_sender, 1, 0)
    carry_here = jnp.where(carry_sender, 2, 0)
    pl.semaphore_wait(barrier, 3 + head_here + next_here + carry_here)

    cols_copy = remote(
        x_ref.at[pl.ds(pl.multiple_of(quarter * b, 8), piece), :],
        ext.at[pl.ds(pl.multiple_of(first, 8), piece), :],
        in_send.at[0],
        in_recv.at[0],
        partner,
        b,
    )
    rows_copy = remote(
        x_ref.at[pl.ds(pl.multiple_of(first, 8), quarter), :],
        rows_x.at[pl.ds(0, quarter), :],
        in_send.at[1],
        in_recv.at[1],
        partner,
        b,
    )
    head_copy = remote(
        x_ref.at[pl.ds(pl.multiple_of(3 * quarter * (1 - b), 8), 8), :],
        rows_x.at[pl.ds(quarter, 8), :],
        in_send.at[2],
        in_recv.at[2],
        lax.rem(p + half - b, blocks),
        b,
    )
    next_copy = remote(
        x_ref.at[pl.ds(0, quarter + 8), :],
        ext.at[pl.ds(block_rows, quarter + 8), :],
        in_send.at[3],
        in_recv.at[3],
        lax.rem(p + blocks - 1, blocks),
        b,
    )
    pl.when(high)(cols_copy.start)
    pl.when(low)(rows_copy.start)
    pl.when(head_sender)(head_copy.start)
    pl.when(next_sender)(next_copy.start)

    starts_copy.wait()
    span = quarter + 8
    lane = lax.broadcasted_iota(jnp.int32, (span, LANES), 1)

    def moments_of(samples):
        mean, spread = samples, None
        width = 1

        def ahead(values):
            below = pltpu.roll(values, span - 1, 0)
            if width == LANES:
                return below
            turned = pltpu.roll(values, LANES - width, 1)
            return jnp.where(lane < LANES - width, turned, pltpu.roll(turned, span - 1, 0))

        while width < M:
            other = ahead(mean)
            gap = mean - other
            term = gap * gap * (0.5 * width)
            spread = term if spread is None else spread + ahead(spread) + term
            mean = 0.5 * (mean + other)
            width *= 2
        return mean, lax.rsqrt(spread + M * EPS)

    square = (LANES, LANES)
    upper = lax.broadcasted_iota(jnp.int32, square, 1) <= lax.broadcasted_iota(jnp.int32, square, 0)
    keep = lax.broadcasted_iota(jnp.int32, square, 1) >= lax.broadcasted_iota(jnp.int32, square, 0)

    def turned_row(source, index):
        line = source[pl.ds(index, 1), :]
        return pltpu.roll(jnp.broadcast_to(line, square), 1, 1, stride=1, stride_axis=0)


    def build_rows():
        samples = rows_x[...]
        mean, factor = moments_of(samples)
        for side, values in enumerate((mean[:quarter], factor[:quarter])):
            left = values
            pieces = []
            for _ in range(3):
                some = left.astype(jnp.bfloat16).astype(jnp.float32)
                left = left - some
                pieces.append(some)
            pieces.append(jnp.zeros((LANES - 3 * quarter, LANES), jnp.float32))
            turned_pieces = jnp.concatenate(pieces, axis=0).T.astype(jnp.bfloat16)
            across[:, side * LANES : (side + 1) * LANES] = turned_pieces
        wide = (2 * LANES, 2 * LANES)
        ones = jnp.where(
            (lax.broadcasted_iota(jnp.int32, wide, 0) < LANES)
            == (lax.broadcasted_iota(jnp.int32, wide, 1) < LANES),
            1.0,
            0.0,
        ).astype(jnp.bfloat16)
        wide_lane = lax.rem(lax.broadcasted_iota(jnp.int32, (1, 2 * LANES), 1), quarter)
        flip = jnp.where(
            lax.broadcasted_iota(jnp.int32, square, 0) + lax.broadcasted_iota(jnp.int32, square, 1)
            == LANES - 1,
            1.0,
            0.0,
        ).astype(jnp.bfloat16)
        left = samples
        back = None
        for _ in range(3):
            some = left.astype(jnp.bfloat16)
            left = left - some.astype(jnp.float32)
            moved = jnp.dot(some, flip, preferred_element_type=jnp.float32)
            back = moved if back is None else back + moved
        rows_back[...] = back

        def turned(index):
            line = rows_back[pl.ds(index, 1), :]
            return pltpu.roll(jnp.broadcast_to(line, square), 0, 1, stride=1, stride_axis=0)

        turn = turned(1)
        near = jnp.where(keep, turned(0), turn)
        for index in range(quarter):
            following = turned(index + 2)
            far = jnp.where(keep, turn, following)
            pick = jnp.where(wide_lane == index, 1.0, 0.0).astype(jnp.bfloat16)
            spread = jnp.dot(across[...] * pick, ones, preferred_element_type=jnp.float32)
            c = spread[:, :LANES]
            f = spread[:, LANES:]
            row_z[index, :, :LANES] = ((near - c) * f).astype(jnp.bfloat16)
            row_z[index, :, LANES:] = ((far - c) * f).astype(jnp.bfloat16)
            turn, near = following, far

    starts = [starts_ref[c] for c in range(band_count)]
    whole = [lax.shift_right_logical(s, 7) for s in starts]
    rest = [lax.bitwise_and(s, LANES - 1) for s in starts]

    def build_cols():
        for c in range(band_count):
            back = lax.rem(LANES - rest[c], LANES)
            here = pltpu.roll(ext[pl.ds(first + whole[c], span), :], back, 1)
            below = pltpu.roll(ext[pl.ds(first + whole[c] + 1, span), :], back, 1)
            samples = jnp.where(lane < LANES - rest[c], here, below)
            shifted[c] = samples
            mean, factor = moments_of(samples)
            stats[2 * c] = mean
            stats[2 * c + 1] = factor

        def turned(c, index):
            line = shifted[c, pl.ds(index, 1), :]
            return pltpu.roll(jnp.broadcast_to(line, square), 1, 1, stride=1, stride_axis=0)

        def one_band(c, _):
            turn0 = turned(c, 0)
            turn1 = turned(c, 1)

            def step(index, state):
                turn, near = state
                following = turned(c, index + 2)
                far = jnp.where(upper, turn, following)
                center = stats[2 * c, pl.ds(index, 1), :]
                factor = stats[2 * c + 1, pl.ds(index, 1), :]
                col_z[c, index, :LANES, :] = ((near - center) * factor).astype(jnp.bfloat16)
                col_z[c, index, LANES:, :] = ((far - center) * factor).astype(jnp.bfloat16)
                return following, far

            lax.fori_loop(
                0, quarter + 1, step, (turn1, jnp.where(upper, turn0, turn1)), unroll=33
            )
            return 0

        lax.fori_loop(0, band_count, one_band, 0)

    def phase(turn, _):
        rows_now = lax.rem(turn + p // half, 2) == 0

        @pl.when(rows_now)
        def _():
            pl.when(low)(own_rows.wait)

            @pl.when(high)
            def _():
                rows_copy.wait_recv()
                head_copy.wait_recv()

            build_rows()

        @pl.when(jnp.logical_not(rows_now))
        def _():
            pl.when(low)(cols_copy.wait_recv)
            pl.when(high)(own_cols.wait)
            pl.when(next_taker)(next_copy.wait_recv)
            pl.when(p == blocks - 1)(own_tail.wait)
            build_cols()

        return 0

    lax.fori_loop(0, 2, phase, 0)

    last_block = lax.rem(p, half) + half
    room_all = (blocks - last_block) * block_rows * LANES - part * quarter * LANES
    lane_row = lax.broadcasted_iota(jnp.int32, (1, LANES), 1)

    lane_square = lax.broadcasted_iota(jnp.int32, square, 1)

    def score(index, state):
        pending, rows_found = state
        best = None
        left = []
        for c in range(band_count):
            both = jnp.concatenate([col_z[c, index], col_z[c, index + 1]], axis=1)
            found = jnp.dot(row_z[index], both, preferred_element_type=jnp.float32)
            room = room_all - starts[c] - index * LANES
            near = found[:, :LANES] + jnp.where(lane_row < room, 0.0, -4.0)
            far = found[:, LANES:] + jnp.where(lane_row + LANES < room, 0.0, -4.0)
            near_cols = jnp.max(jnp.where(keep, near, -4.0), axis=0, keepdims=True)
            far_cols = jnp.max(jnp.where(keep, -4.0, far), axis=0, keepdims=True)
            col_buf[c, pl.ds(quarter + index, 1), :] = jnp.maximum(
                jnp.maximum(pending[c], near_cols), -1.0
            )
            left.append(jnp.maximum(far_cols, -1.0))
            joined = jnp.where(keep, near, far)
            best = joined if best is None else jnp.maximum(best, joined)
        rows_found = jnp.where(
            lane_square == index, jnp.max(best, axis=1, keepdims=True), rows_found
        )
        return tuple(left), rows_found

    floor = jnp.full((1, LANES), -1.0, jnp.float32)
    pending, rows_found = lax.fori_loop(
        0, quarter, score, ((floor,) * band_count, jnp.full(square, -1.0, jnp.float32)), unroll=32
    )
    lane_wide = lax.broadcasted_iota(jnp.int32, (2 * quarter, LANES), 1)
    reached = None
    for c in range(band_count):
        col_buf[c, pl.ds(2 * quarter, 1), :] = pending[c]
        here = pltpu.roll(col_buf[c, pl.ds(quarter - whole[c], 2 * quarter), :], rest[c], 1)
        above = pltpu.roll(col_buf[c, pl.ds(quarter - whole[c] - 1, 2 * quarter), :], rest[c], 1)
        placed = jnp.where(lane_wide >= rest[c], here, above)
        reached = placed if reached is None else jnp.maximum(reached, placed)
    col_res[...] = reached

    place = pl.ds(pl.multiple_of(part * quarter, 8), quarter)
    row_to = [
        remote(row_res, row_out.at[place, :], out_send.at[k], row_recv.at[part], tm, band)
        for k, (tm, band) in enumerate([(p, 1 - b), (partner, 0), (partner, 1)])
    ]
    slot_to = [
        remote(col_res, slots.at[part], out_send.at[3 + k], slot_recv.at[part], tm, band)
        for k, (tm, band) in enumerate([(p, 1 - b), (partner, 0), (partner, 1)])
    ]
    lower = pl.ds(0, quarter)
    lower_to = remote(
        col_res.at[lower, :],
        slots.at[part, lower, :],
        out_send.at[3],
        slot_recv.at[part],
        p,
        1 - b,
    )
    carry_to = [
        remote(
            col_res.at[pl.ds(quarter, quarter), :],
            carry_in,
            out_send.at[6 + k],
            carry_recv.at[0],
            lax.rem(p + 1, blocks),
            k,
        )
        for k in range(2)
    ]

    @pl.when(low)
    def _():
        slot_to[1].start()
        slot_to[2].start()

    @pl.when(carry_sender)
    def _():
        carry_to[0].start()
        carry_to[1].start()

    @pl.when(jnp.logical_and(high, b == 0))
    def _():
        slot_to[0].start()
        slots[2] = col_res[...]

    @pl.when(jnp.logical_and(high, b == 1))
    def _():
        lower_to.start()
        slots[3, lower, :] = col_res[lower, :]

    row_res[...] = jnp.maximum(rows_found.T[:quarter], -1.0)

    @pl.when(low)
    def _():
        row_to[0].start()
        row_out[place, :] = row_res[...]

    @pl.when(high)
    def _():
        row_to[1].start()
        row_to[2].start()

    def row_from(index):
        return remote(
            row_res,
            row_out.at[pl.ds(index * quarter, quarter), :],
            out_send.at[0],
            row_recv.at[index],
            p,
            1 - b,
        )

    def slot_from(index):
        return remote(
            col_res, slots.at[index], out_send.at[0], slot_recv.at[index], p, 1 - b
        )

    @pl.when(low)
    def _():
        pl.when(b == 1)(row_from(0).wait_recv)
        pl.when(b == 0)(row_from(1).wait_recv)
        row_from(2).wait_recv()
        row_from(3).wait_recv()

    @pl.when(high)
    def _():
        slot_from(0).wait_recv()
        slot_from(1).wait_recv()

    @pl.when(jnp.logical_and(high, b == 1))
    def _():
        slot_from(2).wait_recv()

    @pl.when(jnp.logical_and(high, b == 0))
    def _():
        remote(
            col_res.at[lower, :],
            slots.at[3, lower, :],
            out_send.at[0],
            slot_recv.at[3],
            p,
            1 - b,
        ).wait_recv()

    pl.when(carry_taker)(carry_to[0].wait_recv)

    @pl.when(p == half)
    def _():
        carry_in[...] = jnp.full(carry_in.shape, -1.0, jnp.float32)

    @pl.when(high)
    def _():
        col_out[pl.ds(0, quarter), :] = jnp.maximum(slots[0, lower, :], carry_in[...])
        for k in range(1, SLOTS):
            col_out[pl.ds(k * quarter, quarter), :] = jnp.maximum(
                slots[k, lower, :], slots[k - 1, pl.ds(quarter, quarter), :]
            )

    @pl.when(high)
    def _():
        cols_copy.wait_send()
        row_to[1].wait_send()
        row_to[2].wait_send()

    @pl.when(low)
    def _():
        rows_copy.wait_send()
        slot_to[1].wait_send()
        slot_to[2].wait_send()
        row_to[0].wait_send()

    pl.when(head_sender)(head_copy.wait_send)
    pl.when(next_sender)(next_copy.wait_send)
    pl.when(jnp.logical_and(high, b == 0))(slot_to[0].wait_send)
    pl.when(jnp.logical_and(high, b == 1))(lower_to.wait_send)

    @pl.when(carry_sender)
    def _():
        carry_to[0].wait_send()
        carry_to[1].wait_send()


def spread_body(series, tail, band_starts):
    block_rows = series.shape[0] // LANES
    quarter = block_rows // SLOTS
    band_count = band_starts.shape[0]
    blocks = lax.axis_size("tm")
    span = quarter + 8
    vmem = pl.BlockSpec(memory_space=pltpu.VMEM)
    length = series.shape[0]
    outputs = jax.ShapeDtypeStruct((2 * block_rows, LANES), jnp.float32)

    operands = (band_starts, series.reshape(block_rows, LANES), tail.reshape(-1, LANES))

    def buffer(*shape, kind=jnp.float32):
        return pltpu.VMEM(shape, kind)

    both = pl.pallas_call(
        functools.partial(pair_kernel, blocks),
        out_shape=outputs,
        in_specs=[pl.BlockSpec(memory_space=pltpu.HBM)] * 3,
        out_specs=vmem,
        scratch_shapes=[
            pltpu.SMEM((band_count,), jnp.int32),
            buffer(block_rows + span, LANES),
            buffer(span, LANES),
            buffer(span, LANES),
            buffer(band_count, span, LANES),
            buffer(2 * band_count, span, LANES),
            buffer(LANES, 2 * LANES, kind=jnp.bfloat16),
            buffer(quarter, LANES, M, kind=jnp.bfloat16),
            buffer(band_count, quarter + 1, M, LANES, kind=jnp.bfloat16),
            buffer(band_count, 3 * quarter + 8, LANES),
            buffer(quarter, LANES),
            buffer(2 * quarter, LANES),
            buffer(SLOTS, 2 * quarter, LANES),
            buffer(quarter, LANES),
            pltpu.SemaphoreType.DMA((3,)),
            pltpu.SemaphoreType.DMA((4,)),
            pltpu.SemaphoreType.DMA((4,)),
            pltpu.SemaphoreType.DMA((8,)),
            pltpu.SemaphoreType.DMA((SLOTS,)),
            pltpu.SemaphoreType.DMA((SLOTS,)),
            pltpu.SemaphoreType.DMA((1,)),
        ],
        compiler_params=pltpu.CompilerParams(
            collective_id=0, has_side_effects=True, vmem_limit_bytes=40 * 1024 * 1024
        ),
        name="banded_pairs",
    )(*[pltpu.with_memory_space_constraint(a, pltpu.HBM) for a in operands])
    flat = both.reshape(-1)
    return flat[:length], flat[length:]


def solution(mesh):
    placed = (P(("groups", "tm")), P("groups"), P("groups"))

    def chosen(series, tail, band_starts):
        halves = lax.axis_size("tm") == 2 * BAND_BLOCKS
        if halves and series.shape[0] == SLOTS * BAND_SPAN and lax.axis_size("band") == 2:
            return spread_body(series, tail, band_starts)
        return body(series, tail, band_starts)

    return jax.shard_map(
        chosen,
        mesh=mesh,
        in_specs=placed,
        out_specs=(P(("groups", "tm")), P(("groups", "tm"))),
        check_vma=False,
    )
```
